32 devices in a mesh: seq: 4 (over z), dp: 8 (over y, x, core).
Axes of the slice: x: 2, y: 2, z: 4, core: 2. Of those that a mesh axis runs over, the one named last changes fastest.
Arguments:
- layer_in: bfloat16 [2, 8, 1024, 768], P(None, 'dp', 'seq'), may hold values from -6 to 6
- cotangent: bfloat16 [2, 8, 1024, 768], P(None, 'dp', 'seq'), may hold values from -6 to 6
- valid_len: int32 [2, 8], P(None, 'dp'), may hold values from 512 to 1024, as said below
- sep_pos: int32 [2, 8], P(None, 'dp'), may hold values from 128 to 768, as said below
- w_query: bfloat16 [768, 384], P(('seq', 'dp')), may hold values from -0.21875 to 0.21875
- w_key: bfloat16 [768, 384], P(('seq', 'dp')), may hold values from -0.21875 to 0.21875
- w_value: bfloat16 [768, 384], P(('seq', 'dp')), may hold values from -0.21875 to 0.21875
- w_depth: bfloat16 [9, 768], P(None, ('seq', 'dp')), may hold values from -2 to 2
- w_point: bfloat16 [768, 384], P(('seq', 'dp')), may hold values from -0.21875 to 0.21875
- w_kernel: bfloat16 [20736], P(('seq', 'dp')), may hold values from -0.3125 to 0.3125
- w_convout: bfloat16 [768, 384], P(('seq', 'dp')), may hold values from -0.21875 to 0.21875
- w_output: bfloat16 [768, 768], P(('seq', 'dp')), may hold values from -0.875 to 0.875
- gain_attn: bfloat16 [768], P(('seq', 'dp')), may hold values from 0.3984375 to 1.59375
- shift_attn: bfloat16 [768], P(('seq', 'dp')), may hold values from -0.3984375 to 0.3984375
- w_up: bfloat16 [2, 384, 1536], P(None, None, ('seq', 'dp')), may hold values from -0.3125 to 0.3125
- w_down: bfloat16 [2, 1536, 384], P(None, ('seq', 'dp')), may hold values from -0.15625 to 0.15625
- gain_out: bfloat16 [768], P(('seq', 'dp')), may hold values from 0.3984375 to 1.59375
- shift_out: bfloat16 [768], P(('seq', 'dp')), may hold values from -0.3984375 to 0.3984375
Outputs:
- layer_out: bfloat16 [2, 8, 1024, 768], P(None, 'dp', 'seq')
- x_grad: float32 [2, 8, 1024, 768], P(None, 'dp', 'seq')
- grad_query: float32 [768, 384], P(('seq', 'dp'))
- grad_key: float32 [768, 384], P(('seq', 'dp'))
- grad_value: float32 [768, 384], P(('seq', 'dp'))
- grad_depth: float32 [9, 768], P(None, ('seq', 'dp'))
- grad_point: float32 [768, 384], P(('seq', 'dp'))
- grad_kernel: float32 [20736], P(('seq', 'dp'))
- grad_convout: float32 [768, 384], P(('seq', 'dp'))
- grad_output: float32 [768, 768], P(('seq', 'dp'))
- grad_gain_attn: float32 [768], P(('seq', 'dp'))
- grad_shift_attn: float32 [768], P(('seq', 'dp'))
- grad_up: float32 [2, 384, 1536], P(None, None, ('seq', 'dp'))
- grad_down: float32 [2, 1536, 384], P(None, ('seq', 'dp'))
- grad_gain_out: float32 [768], P(('seq', 'dp'))
- grad_shift_out: float32 [768], P(('seq', 'dp'))
The draws below stay inside these ranges and needn't reach their ends.
Inputs may be any that keep to these rules, and one draw needn't show every extreme that they name: `valid_len`: for every index of dp, one of its rows over the 2 micro-batches, which one drawn from the seed, has all 1024 tokens. `sep_pos`: below the row's valid_len and at least valid_len // 4 (a quarter, rounded down).
All inputs are finite; a program needn't handle non-finite values.
Results may differ from the reference program's by a relative error of at most 0.015.
Values may be sent and summed in bfloat16 or wider, within the bound.
No kernel may reach another device: no remote copies, remote signals or barrier semaphores. Data moves between devices by JAX's collectives and lax.ppermute only.
A program may use at most 192 MiB of HBM per device.

```python
import math
import jax
import jax.numpy as jnp
from jax import lax

D = 768
HEADS = 6
HEAD_DIM = 64
KERNEL = 9
FF = 3072
GROUPS = 2
LEN = 1024
MICRO = 2
ROW_DEV = 1
AH = 384
ROWS = 8


def row_layout(key):
    dp_count = ROWS // ROW_DEV
    first_key, second_key, third_key = jax.random.split(key, 3)
    lengths = jax.random.randint(first_key, (MICRO, dp_count, ROW_DEV), LEN // 2, LEN + 1)
    chosen = jax.random.randint(second_key, (dp_count,), 0, MICRO * ROW_DEV)
    slot_index = jnp.arange(MICRO)[:, None, None] * ROW_DEV + jnp.arange(ROW_DEV)[None, None, :]
    lengths = jnp.where(slot_index == chosen[None, :, None], LEN, lengths).reshape(MICRO, ROWS)
    fraction = jax.random.randint(third_key, (MICRO, ROWS), 0, 1048576)
    separators = lengths // 4 + fraction * (lengths // 2) // 1048576
    return (lengths.astype(jnp.int32), separators.astype(jnp.int32))


def draw_valid_len(key, part):
    shared = row_layout(key)
    return shared[0]


def draw_sep_pos(key, part):
    shared = row_layout(key)
    return shared[1]


def block_levels(own_key, shape, shards, low, high):
    def one(position, shards_of):
        draws = jax.random.uniform(jax.random.fold_in(jax.random.fold_in(own_key, 6), position), (shards_of,), jnp.float32, low / len(shards), high / len(shards))
        return jnp.repeat(jnp.exp(draws), shape[position] // shards_of).reshape((-1,) + (1,) * (len(shape) - position - 1))

    gain = one(*shards[0])
    for cut in shards[1:]:
        gain = gain * one(*cut)
    return gain


def gaussian(own_key, dims, deviation, bound, cuts=(), dtype=jnp.bfloat16):
    values = jax.random.normal(own_key, dims, jnp.float32) * deviation
    if len(cuts) > 0:
        values = block_levels(own_key, dims, cuts, -0.22, 0.18) * values
    return jnp.clip(values, min=-bound, max=bound).astype(dtype)


def setup_inputs(seed: int = 0) -> dict:
    key_of = jax.random.split(jax.random.key(seed), 19)
    layer_in = gaussian(key_of[0], (MICRO, ROWS, LEN, D), 1.0, 6.0, ((1, 8), (2, 4)))
    cotangent = gaussian(key_of[1], (MICRO, ROWS, LEN, D), 1.0, 6.0, ((1, 8), (2, 4)))
    valid_len = draw_valid_len(jax.random.fold_in(key_of[18], 71), 0)
    sep_pos = draw_sep_pos(jax.random.fold_in(key_of[18], 71), 0)
    w_query = gaussian(key_of[4], (D, AH), D ** -0.5, 0.21875, ((0, 32),))
    w_key = gaussian(key_of[5], (D, AH), D ** -0.5, 0.21875, ((0, 32),))
    w_value = gaussian(key_of[6], (D, AH), D ** -0.5, 0.21875, ((0, 32),))
    w_depth = gaussian(key_of[7], (KERNEL, D), KERNEL ** -0.5, 2.0, ((1, 32),))
    w_point = gaussian(key_of[8], (D, AH), D ** -0.5, 0.21875, ((0, 32),))
    w_kernel = gaussian(key_of[9], (AH * HEADS * KERNEL,), AH ** -0.5, 0.3125, ((0, 32),))
    w_convout = gaussian(key_of[10], (D, AH), D ** -0.5, 0.21875, ((0, 32),))
    w_output = gaussian(key_of[11], (2 * AH, D), (AH // 8) ** -0.5, 0.875, ((0, 32),))
    gain_attn = jnp.clip(1.0 + 0.12 * jax.random.normal(key_of[12], (D,), jnp.float32), 0.3984375, 1.59375).astype(jnp.bfloat16)
    shift_attn = jnp.clip(jax.random.uniform(key_of[13], (D,), jnp.float32, -0.3984375, 0.3984375) * block_levels(key_of[13], (D,), ((0, 32),), -0.4, 0.0), -0.3984375, 0.3984375).astype(jnp.bfloat16)
    w_up = gaussian(key_of[14], (GROUPS, D // GROUPS, FF // GROUPS), (D // GROUPS) ** -0.5, 0.3125, ((2, 32),))
    w_down = gaussian(key_of[15], (GROUPS, FF // GROUPS, D // GROUPS), (FF // GROUPS) ** -0.5, 0.15625, ((1, 32),))
    gain_out = jnp.clip(1.0 + 0.12 * jax.random.normal(key_of[16], (D,), jnp.float32), 0.3984375, 1.59375).astype(jnp.bfloat16)
    shift_out = jnp.clip(jax.random.uniform(key_of[17], (D,), jnp.float32, -0.3984375, 0.3984375) * block_levels(key_of[17], (D,), ((0, 32),), -0.4, 0.0), -0.3984375, 0.3984375).astype(jnp.bfloat16)
    return {"layer_in": layer_in, "cotangent": cotangent, "valid_len": valid_len, "sep_pos": sep_pos, "w_query": w_query, "w_key": w_key, "w_value": w_value, "w_depth": w_depth, "w_point": w_point, "w_kernel": w_kernel, "w_convout": w_convout, "w_output": w_output, "gain_attn": gain_attn, "shift_attn": shift_attn, "w_up": w_up, "w_down": w_down, "gain_out": gain_out, "shift_out": shift_out}


@jax.custom_vjp
def low(v):
    return lax.optimization_barrier(v.astype(jnp.bfloat16)).astype(jnp.float32)

@jax.custom_vjp
def low_back(v):
    return v

def low_keep(v):
    return (low(v), None)

def low_pass(kept, grad):
    return (grad,)

def back_keep(v):
    return (v, None)

def back_low(kept, grad):
    return (low(grad),)
low.defvjp(low_keep, low_pass)
low_back.defvjp(back_keep, back_low)
inv_root_two = 0.7071067811865476

def product(form, first_op, second_op):
    return jnp.einsum(form, first_op, second_op, precision=lax.Precision.HIGHEST, preferred_element_type=jnp.float32)

def both_low(tensor):
    return low(low_back(tensor))

def softmax_last(scores):
    row_peak = lax.optimization_barrier(jnp.max(scores, -1, keepdims=True))
    exponent = jnp.exp(scores - row_peak)
    return exponent / lax.optimization_barrier(jnp.sum(exponent, -1, keepdims=True))

def layer_norm(signal, gain_vec, shift_vec):
    centred = signal - lax.optimization_barrier(jnp.mean(signal, -1, keepdims=True))
    return centred * lax.rsqrt(lax.optimization_barrier(jnp.mean(centred * centred, -1, keepdims=True)) + 1e-06) * gain_vec + shift_vec

def erf_gelu(pre_act):
    return 0.5 * pre_act * (1.0 + lax.erf(pre_act * inv_root_two))

def layer_forward(params, tokens, valid_rows, sep_rows):
    query_weight, key_weight, value_weight, depth_kernel, point_weight, kernel_flat, conv_weight, out_weight, attn_gain, attn_shift, up_weight, down_weight, out_gain, out_shift = params
    group_rows = tokens.shape[0]
    half_span = (KERNEL - 1) // 2
    heads_width = HEADS * HEAD_DIM
    group_width = D // GROUPS
    query_full = both_low(product('rtd,da->rta', tokens, query_weight))
    keys_full = both_low(product('rtd,da->rta', tokens, key_weight))
    values_full = both_low(product('rtd,da->rta', tokens, value_weight))
    query_heads = query_full.reshape(group_rows, LEN, HEADS, HEAD_DIM)
    keys_heads = keys_full.reshape(group_rows, LEN, HEADS, HEAD_DIM)
    values_heads = values_full.reshape(group_rows, LEN, HEADS, HEAD_DIM)
    scores = low_back(product('rqhe,rkhe->rhqk', query_heads, keys_heads) * HEAD_DIM ** (-0.5))
    positions = jnp.arange(LEN)
    key_live = positions[None, :] < valid_rows[:, None]
    scores = jnp.where(key_live[:, None, None, :], scores, -1e+30)
    probs = softmax_last(scores)
    attended = product('rhqk,rkhe->rqhe', low(probs), values_heads).reshape(group_rows, LEN, heads_width)
    padded = jnp.pad(tokens, ((0, 0), (half_span, half_span), (0, 0)))
    depth_out = jnp.zeros_like(tokens)
    for tap_index in range(KERNEL):
        depth_out = depth_out + depth_kernel[tap_index] * padded[:, tap_index:tap_index + LEN]
    depth_low = low(depth_out)
    key_conv = low_back(product('rtd,da->rta', depth_low, point_weight))
    conv_attn = low(key_conv * query_full)
    kernel_weight = kernel_flat.reshape(heads_width, HEADS * KERNEL)
    kernel_logits = low_back(product('rta,ak->rtk', conv_attn, kernel_weight))
    kernel_probs = softmax_last(kernel_logits.reshape(group_rows, LEN, HEADS, KERNEL))
    conv_values = low_back(product('rtd,da->rta', tokens, conv_weight))
    padded_values = jnp.pad(conv_values, ((0, 0), (half_span, half_span), (0, 0)))
    segment = jnp.where(positions[None, :] < sep_rows[:, None], 0, jnp.where(key_live, 1, 2)).astype(jnp.int32)
    padded_segment = jnp.pad(segment, ((0, 0), (half_span, half_span)), constant_values=-1)
    conv_heads = jnp.zeros_like(query_heads)
    for tap_index in range(KERNEL):
        same_seg = (padded_segment[:, tap_index:tap_index + LEN] == segment).astype(jnp.float32)
        tap_weight = kernel_probs[..., tap_index] * same_seg[:, :, None]
        window = padded_values[:, tap_index:tap_index + LEN].reshape(group_rows, LEN, HEADS, HEAD_DIM)
        conv_heads = conv_heads + tap_weight[..., None] * window
    context = both_low(jnp.concatenate([attended, conv_heads.reshape(group_rows, LEN, heads_width)], -1))
    first_sum = low_back(product('rta,ad->rtd', context, out_weight)) + tokens
    attn_out = layer_norm(first_sum, attn_gain, attn_shift)
    grouped = low(attn_out).reshape(group_rows, LEN, GROUPS, group_width)
    pre_act = low_back(product('rtgd,gdf->rtgf', grouped, up_weight))
    act_low = low(erf_gelu(pre_act))
    down_out = low_back(product('rtgf,gfd->rtgd', act_low, down_weight)).reshape(group_rows, LEN, D)
    return layer_norm(down_out + attn_out, out_gain, out_shift)

def reference(layer_in, cotangent, valid_len, sep_pos, w_query, w_key, w_value, w_depth, w_point, w_kernel, w_convout, w_output, gain_attn, shift_attn, w_up, w_down, gain_out, shift_out):
    params = tuple((weight.astype(jnp.float32) for weight in (w_query, w_key, w_value, w_depth, w_point, w_kernel, w_convout, w_output, gain_attn, shift_attn, w_up, w_down, gain_out, shift_out)))
    total_rows = MICRO * ROWS
    group_rows = math.gcd(4, total_rows)
    group_count = total_rows // group_rows
    token_groups = layer_in.astype(jnp.float32).reshape(group_count, group_rows, LEN, D)
    cot_groups = cotangent.astype(jnp.float32).reshape(group_count, group_rows, LEN, D)
    valid_groups = valid_len.reshape(group_count, group_rows).astype(jnp.int32)
    sep_groups = sep_pos.reshape(group_count, group_rows).astype(jnp.int32)

    def visit(running, batch_item):
        token_rows, cot_rows, valid_rows, sep_rows = batch_item

        def apply_layer(weights, inputs):
            return layer_forward(weights, inputs, valid_rows, sep_rows)
        result, pullback = jax.vjp(apply_layer, params, token_rows)
        d_params, d_tokens = pullback(cot_rows)
        return (jax.tree.map(jnp.add, running, d_params), (result.astype(jnp.bfloat16), d_tokens))
    zero_grads = jax.tree.map(jnp.zeros_like, params)
    totals, (outputs, input_grads) = lax.scan(visit, zero_grads, (token_groups, cot_groups, valid_groups, sep_groups))
    grad_query, grad_key, grad_value, grad_depth, grad_point, grad_kernel, grad_convout, grad_output, grad_gain_attn, grad_shift_attn, grad_up, grad_down, grad_gain_out, grad_shift_out = totals
    return (outputs.reshape(MICRO, ROWS, LEN, D), input_grads.reshape(MICRO, ROWS, LEN, D), grad_query, grad_key, grad_value, grad_depth, grad_point, grad_kernel, grad_convout, grad_output, grad_gain_attn, grad_shift_attn, grad_up, grad_down, grad_gain_out, grad_shift_out)
```

```python
import functools

import jax
import jax.numpy as jnp
import numpy as np
from jax import lax
from jax.experimental import pallas as pl
from jax.experimental.pallas import tpu as pltpu
from jax.sharding import PartitionSpec as P

HEADS = 6
HEAD_DIM = 64
KERNEL = 9
GROUPS = 2
LEN = 1024


inv_root_two = 0.7071067811865476
inv_root_tau = 0.3989422804014327


def erf_gelu(pre_act):
    return 0.5 * pre_act * (1.0 + lax.erf(pre_act * inv_root_two))


def gelu_slope(pre_act):
    return (
        0.5 * (1.0 + lax.erf(pre_act * inv_root_two))
        + pre_act * jnp.exp(-0.5 * pre_act * pre_act) * inv_root_tau
    )


def softmax_last(scores):
    row_peak = jnp.max(scores, -1, keepdims=True)
    exponent = jnp.exp(scores - row_peak)
    return exponent / jnp.sum(exponent, -1, keepdims=True)


def norm_forward(signal, gain_vec, shift_vec):
    centred = signal - jnp.mean(signal, -1, keepdims=True)
    inv_scale = lax.rsqrt(jnp.mean(centred * centred, -1, keepdims=True) + 1e-06)
    normed = centred * inv_scale
    return (normed * gain_vec + shift_vec, normed, inv_scale)


def norm_backward(grad_out, normed, inv_scale, gain_vec):
    d_gain = jnp.sum(grad_out * normed, axis=(0, 1))
    d_shift = jnp.sum(grad_out, axis=(0, 1))
    d_normed = grad_out * gain_vec
    d_signal = inv_scale * (
        d_normed
        - jnp.mean(d_normed, -1, keepdims=True)
        - normed * jnp.mean(d_normed * normed, -1, keepdims=True)
    )
    return (d_signal, d_gain, d_shift)


def run_batch(gathered, tokens, row_tokens, grad_rows, valid_row, sep_row, core):
    (
        query_weight,
        key_weight,
        value_weight,
        depth_kernel,
        point_weight,
        kernel_flat,
        conv_weight,
        out_weight,
        attn_gain,
        attn_shift,
        up_weight,
        down_weight,
        out_gain,
        out_shift,
    ) = gathered
    tokens = tokens[None]
    row_tokens = row_tokens[None]
    grad_rows = grad_rows[None]
    valid_rows = valid_row[None]
    sep_rows = sep_row[None]
    row_count, local_len, width = tokens.shape
    first_pos = core * local_len
    half_span = (KERNEL - 1) // 2
    heads_width = HEADS * HEAD_DIM
    group_width = width // GROUPS
    score_scale = HEAD_DIM ** (-0.5)
    kernel_weight = kernel_flat.reshape(heads_width, HEADS * KERNEL)
    tokens_wide = tokens.astype(jnp.float32)
    query_low = jnp.dot(tokens, query_weight, preferred_element_type=jnp.float32).astype(
        jnp.bfloat16
    )
    keys_all = jnp.dot(row_tokens, key_weight, preferred_element_type=jnp.float32).astype(
        jnp.bfloat16
    )
    values_all = jnp.dot(row_tokens, value_weight, preferred_element_type=jnp.float32).astype(
        jnp.bfloat16
    )
    full_len = keys_all.shape[1]
    query_heads = query_low.reshape(row_count, local_len, HEADS, HEAD_DIM)
    keys_heads = keys_all.reshape(row_count, full_len, HEADS, HEAD_DIM)
    values_heads = values_all.reshape(row_count, full_len, HEADS, HEAD_DIM)
    scores = (
        jnp.einsum("rqhe,rkhe->rhqk", query_heads, keys_heads, preferred_element_type=jnp.float32)
        * score_scale
    )
    key_live = jnp.arange(full_len)[None, :] < valid_rows[:, None]
    scores = jnp.where(key_live[:, None, None, :], scores, -1e30)
    probs = softmax_last(scores)
    probs_low = probs.astype(jnp.bfloat16)
    attended = jnp.einsum(
        "rhqk,rkhe->rqhe", probs_low, values_heads, preferred_element_type=jnp.float32
    ).reshape(row_count, local_len, heads_width)
    padded = lax.dynamic_slice_in_dim(
        jnp.pad(row_tokens, ((0, 0), (half_span, half_span), (0, 0))),
        first_pos,
        local_len + 2 * half_span,
        1,
    )
    padded_wide = padded.astype(jnp.float32)
    depth_wide = depth_kernel.astype(jnp.float32)
    depth_out = jnp.zeros((row_count, local_len, width), jnp.float32)
    for tap_index in range(KERNEL):
        depth_out = (
            depth_out + depth_wide[tap_index] * padded_wide[:, tap_index : tap_index + local_len]
        )
    depth_low = depth_out.astype(jnp.bfloat16)
    key_conv = jnp.dot(depth_low, point_weight, preferred_element_type=jnp.float32)
    query_wide = query_low.astype(jnp.float32)
    conv_attn_low = (key_conv * query_wide).astype(jnp.bfloat16)
    kernel_logits = jnp.dot(conv_attn_low, kernel_weight, preferred_element_type=jnp.float32)
    kernel_probs = softmax_last(kernel_logits.reshape(row_count, local_len, HEADS, KERNEL))
    conv_values = jnp.dot(padded, conv_weight, preferred_element_type=jnp.float32)
    positions = first_pos - half_span + jnp.arange(local_len + 2 * half_span)
    inside = (positions >= 0) & (positions < LEN)
    segment = jnp.where(
        positions[None, :] < sep_rows[:, None],
        0,
        jnp.where(positions[None, :] < valid_rows[:, None], 1, 2),
    )
    segment = jnp.where(inside[None, :], segment, -1)
    own_segment = segment[:, half_span : half_span + local_len]
    tap_weights = []
    same_masks = []
    conv_heads = jnp.zeros((row_count, local_len, HEADS, HEAD_DIM), jnp.float32)
    for tap_index in range(KERNEL):
        same_seg = (segment[:, tap_index : tap_index + local_len] == own_segment).astype(
            jnp.float32
        )
        tap_weight = kernel_probs[..., tap_index] * same_seg[:, :, None]
        window = conv_values[:, tap_index : tap_index + local_len].reshape(
            row_count, local_len, HEADS, HEAD_DIM
        )
        conv_heads = conv_heads + tap_weight[..., None] * window
        tap_weights.append(tap_weight)
        same_masks.append(same_seg)
    context_low = jnp.concatenate(
        [attended, conv_heads.reshape(row_count, local_len, heads_width)], -1
    ).astype(jnp.bfloat16)
    branch = jnp.dot(context_low, out_weight, preferred_element_type=jnp.float32)
    attn_gain_wide = attn_gain.astype(jnp.float32)
    out_gain_wide = out_gain.astype(jnp.float32)
    attn_out, normed_one, inv_one = norm_forward(
        branch + tokens_wide, attn_gain_wide, attn_shift.astype(jnp.float32)
    )
    grouped = attn_out.astype(jnp.bfloat16).reshape(row_count, local_len, GROUPS, group_width)
    pre_act = jnp.einsum("rsgd,gfd->rsgf", grouped, up_weight, preferred_element_type=jnp.float32)
    act_low = erf_gelu(pre_act).astype(jnp.bfloat16)
    down_out = jnp.einsum(
        "rsgf,gfd->rsgd", act_low, down_weight, preferred_element_type=jnp.float32
    ).reshape(row_count, local_len, width)
    final_out, normed_two, inv_two = norm_forward(
        down_out + attn_out, out_gain_wide, out_shift.astype(jnp.float32)
    )
    grad_wide = grad_rows.astype(jnp.float32)
    d_second, d_out_gain, d_out_shift = norm_backward(grad_wide, normed_two, inv_two, out_gain_wide)
    d_down_low = d_second.astype(jnp.bfloat16).reshape(row_count, local_len, GROUPS, group_width)
    d_down_w = jnp.einsum("rsgf,rsgd->gfd", act_low, d_down_low, preferred_element_type=jnp.float32)
    d_act = jnp.einsum(
        "rsgd,gfd->rsgf", d_down_low, down_weight, preferred_element_type=jnp.float32
    )
    d_pre_low = (d_act * gelu_slope(pre_act)).astype(jnp.bfloat16)
    d_up_w = jnp.einsum("rsgd,rsgf->gfd", grouped, d_pre_low, preferred_element_type=jnp.float32)
    d_attn_out = d_second + jnp.einsum(
        "rsgf,gfd->rsgd", d_pre_low, up_weight, preferred_element_type=jnp.float32
    ).reshape(row_count, local_len, width)
    d_first, d_attn_gain, d_attn_shift = norm_backward(
        d_attn_out, normed_one, inv_one, attn_gain_wide
    )
    d_branch_low = d_first.astype(jnp.bfloat16)
    d_out_w = jnp.einsum(
        "rsa,rsd->ad", context_low, d_branch_low, preferred_element_type=jnp.float32
    )
    d_context_low = jnp.einsum(
        "rsd,ad->rsa", d_branch_low, out_weight, preferred_element_type=jnp.float32
    ).astype(jnp.bfloat16)
    d_attended = d_context_low[..., :heads_width].reshape(row_count, local_len, HEADS, HEAD_DIM)
    d_conv_heads = (
        d_context_low[..., heads_width:]
        .astype(jnp.float32)
        .reshape(row_count, local_len, HEADS, HEAD_DIM)
    )
    d_probs = jnp.einsum(
        "rqhe,rkhe->rhqk", d_attended, values_heads, preferred_element_type=jnp.float32
    )
    d_values_part = jnp.einsum(
        "rhqk,rqhe->rkhe", probs_low, d_attended, preferred_element_type=jnp.float32
    )
    row_dot = jnp.sum(probs * d_probs, -1, keepdims=True)
    d_scores_low = (probs * (d_probs - row_dot)).astype(jnp.bfloat16)
    d_query_attn = (
        jnp.einsum("rhqk,rkhe->rqhe", d_scores_low, keys_heads, preferred_element_type=jnp.float32)
        * score_scale
    )
    d_keys_part = (
        jnp.einsum("rhqk,rqhe->rkhe", d_scores_low, query_heads, preferred_element_type=jnp.float32)
        * score_scale
    )
    parts = jnp.concatenate(
        [
            d_keys_part.reshape(full_len, heads_width),
            d_values_part.reshape(full_len, heads_width),
        ],
        -1,
    ).astype(jnp.bfloat16)
    other_half = lax.dynamic_slice_in_dim(parts, (1 - core) * local_len, local_len, 0)
    own_half = lax.dynamic_slice_in_dim(parts, core * local_len, local_len, 0)
    whole = (add_up([own_half, swap(other_half, "dp", 1)]).astype(jnp.bfloat16))[None]
    d_keys_low = whole[..., :heads_width]
    d_values_low = whole[..., heads_width:]
    d_values_pad = jnp.zeros((row_count, local_len + 2 * half_span, heads_width), jnp.float32)
    d_tap_list = []
    for tap_index in range(KERNEL):
        window = conv_values[:, tap_index : tap_index + local_len].reshape(
            row_count, local_len, HEADS, HEAD_DIM
        )
        d_tap_list.append(jnp.sum(d_conv_heads * window, -1) * same_masks[tap_index][:, :, None])
        spread_back = (tap_weights[tap_index][..., None] * d_conv_heads).reshape(
            row_count, local_len, heads_width
        )
        d_values_pad = d_values_pad.at[:, tap_index : tap_index + local_len].add(spread_back)
    d_kernel_probs = jnp.stack(d_tap_list, -1)
    d_logits_low = kernel_probs * (
        d_kernel_probs - jnp.sum(kernel_probs * d_kernel_probs, -1, keepdims=True)
    )
    d_logits_low = d_logits_low.astype(jnp.bfloat16).reshape(row_count, local_len, HEADS * KERNEL)
    d_kernel_w = jnp.einsum(
        "rsa,rsk->ak", conv_attn_low, d_logits_low, preferred_element_type=jnp.float32
    ).reshape(-1)
    d_conv_attn = jnp.einsum(
        "rsk,ak->rsa", d_logits_low, kernel_weight, preferred_element_type=jnp.float32
    )
    d_key_conv_low = (d_conv_attn * query_wide).astype(jnp.bfloat16)
    d_point_w = jnp.einsum(
        "rsd,rsa->da", depth_low, d_key_conv_low, preferred_element_type=jnp.float32
    )
    d_depth = jnp.einsum(
        "rsa,da->rsd", d_key_conv_low, point_weight, preferred_element_type=jnp.float32
    )
    d_input_pad = jnp.zeros((row_count, local_len + 2 * half_span, width), jnp.float32)
    d_depth_rows = []
    for tap_index in range(KERNEL):
        d_depth_rows.append(
            jnp.sum(d_depth * padded_wide[:, tap_index : tap_index + local_len], axis=(0, 1))
        )
        d_input_pad = d_input_pad.at[:, tap_index : tap_index + local_len].add(
            depth_wide[tap_index] * d_depth
        )
    d_depth_w = jnp.stack(d_depth_rows, 0)
    left_rim = jnp.concatenate([d_values_pad[:, :half_span], d_input_pad[:, :half_span]], -1)
    right_rim = jnp.concatenate(
        [d_values_pad[:, local_len + half_span :], d_input_pad[:, local_len + half_span :]], -1
    )
    rim = jnp.where(core == 0, right_rim, left_rim).astype(jnp.bfloat16)
    arrived = swap(rim, "dp", 1).astype(jnp.float32)
    gap = ((0, 0), (local_len - half_span, 0), (0, 0))
    incoming = jnp.where(
        core == 0,
        jnp.pad(arrived, gap),
        jnp.pad(arrived, ((0, 0), (0, local_len - half_span), (0, 0))),
    )
    d_conv_values_low = (
        d_values_pad[:, half_span : half_span + local_len] + incoming[..., :heads_width]
    ).astype(jnp.bfloat16)
    d_query_low = (
        d_query_attn.reshape(row_count, local_len, heads_width) + d_conv_attn * key_conv
    ).astype(jnp.bfloat16)
    d_query_w = jnp.einsum("rsd,rsa->da", tokens, d_query_low, preferred_element_type=jnp.float32)
    d_key_w = jnp.einsum("rsd,rsa->da", tokens, d_keys_low, preferred_element_type=jnp.float32)
    d_value_w = jnp.einsum("rsd,rsa->da", tokens, d_values_low, preferred_element_type=jnp.float32)
    d_conv_w = jnp.einsum(
        "rsd,rsa->da", tokens, d_conv_values_low, preferred_element_type=jnp.float32
    )
    input_grad = (
        d_first
        + d_input_pad[:, half_span : half_span + local_len]
        + incoming[..., heads_width:]
        + jnp.einsum("rsa,da->rsd", d_query_low, query_weight, preferred_element_type=jnp.float32)
        + jnp.einsum("rsa,da->rsd", d_keys_low, key_weight, preferred_element_type=jnp.float32)
        + jnp.einsum("rsa,da->rsd", d_values_low, value_weight, preferred_element_type=jnp.float32)
        + jnp.einsum(
            "rsa,da->rsd", d_conv_values_low, conv_weight, preferred_element_type=jnp.float32
        )
    )
    grads = (
        d_query_w,
        d_key_w,
        d_value_w,
        d_depth_w,
        d_point_w,
        d_kernel_w,
        d_conv_w,
        d_out_w,
        d_attn_gain,
        d_attn_shift,
        d_up_w,
        d_down_w,
        d_out_gain,
        d_out_shift,
    )
    return (final_out.astype(jnp.bfloat16)[0], input_grad[0], grads)


def dp_groups(count):
    masks = []
    bit = 2
    while bit < count:
        if bit * 2 < count:
            masks.append((bit, 2 * bit, 3 * bit))
            bit *= 4
        else:
            masks.append((bit,))
            bit *= 2
    return masks


def swap(x, axis, mask):
    count = lax.axis_size(axis)
    return lax.ppermute(x, axis, [(i, i ^ mask) for i in range(count)])


def relative_codes():
    seq, dp = lax.axis_size("seq"), lax.axis_size("dp")
    codes = [j * dp for j in range(seq)]
    for masks in dp_groups(dp):
        codes = [c ^ m for m in (0,) + masks for c in codes]
    return codes + [c ^ 1 for c in codes]


def gather_relative(x):
    seq, dp = lax.axis_size("seq"), lax.axis_size("dp")
    held = jnp.stack([x] + [swap(x, "seq", j) for j in range(1, seq)])
    for masks in dp_groups(dp):
        held = jnp.concatenate([held] + [swap(held, "dp", m) for m in masks])
    return held, swap(held, "dp", 1)


def add_up(parts):
    total = parts[0].astype(jnp.float32)
    for part in parts[1:]:
        total = total + part.astype(jnp.float32)
    return total


def scatter_relative(kept, sent):
    seq, dp = lax.axis_size("seq"), lax.axis_size("dp")
    held = add_up([kept, swap(sent, "dp", 1)]).astype(jnp.bfloat16)
    for masks in reversed(dp_groups(dp)):
        held = held.reshape((len(masks) + 1, -1) + held.shape[1:])
        parts = [held[0]] + [swap(held[i + 1], "dp", m) for i, m in enumerate(masks)]
        held = add_up(parts).astype(jnp.bfloat16)
    return add_up([held[0]] + [swap(held[j], "seq", j) for j in range(1, seq)])


def reorder_kernel(count, index, *refs):
    sources, target, sems = refs[:-2], refs[-2], refs[-1]
    per = count // len(sources)
    copies = []
    for i in range(count):
        copies.append(
            pltpu.make_async_copy(
                sources[i // per].at[i % per], target.at[index[i]], sems.at[i]
            )
        )
    for copy in copies:
        copy.start()
    for copy in copies:
        copy.wait()


def reorder(parts, index):
    count = sum(p.shape[0] for p in parts)
    return pl.pallas_call(
        functools.partial(reorder_kernel, count),
        out_shape=jax.ShapeDtypeStruct((count,) + parts[0].shape[1:], parts[0].dtype),
        in_specs=[pl.BlockSpec(memory_space=pltpu.SMEM)]
        + [pl.BlockSpec(memory_space=pltpu.VMEM)] * len(parts),
        out_specs=pl.BlockSpec(memory_space=pl.ANY),
        scratch_shapes=[pltpu.SemaphoreType.DMA((count,))],
        compiler_params=pltpu.CompilerParams(vmem_limit_bytes=40 * 1024 * 1024),
    )(index, *parts)


def token_perms():
    seq, dp = lax.axis_size("seq"), lax.axis_size("dp")
    first, second = [], []
    for z in range(seq):
        for d in range(dp):
            core, rest = d & 1, d & ~1
            odd = z & 1
            first.append((z * dp + d, (2 * odd + core) * dp + rest + (z >> 1)))
            second.append((z * dp + d, (2 * (1 - odd) + core) * dp + rest + (z >> 1)))
    return first, second


def to_rows(x):
    first, second = token_perms()
    z = lax.axis_index("seq")
    odd, high = z & 1, z >> 1
    a = lax.ppermute(lax.dynamic_index_in_dim(x, odd, 0, False), ("seq", "dp"), first)
    b = lax.ppermute(lax.dynamic_index_in_dim(x, 1 - odd, 0, False), ("seq", "dp"), second)
    return jnp.where(high == 0, jnp.concatenate([a, b]), jnp.concatenate([b, a]))


def from_rows(x):
    first, second = token_perms()
    z = lax.axis_index("seq")
    odd, high = z & 1, z >> 1
    half = x.reshape(2, x.shape[0] // 2, x.shape[1])
    a = lax.ppermute(
        lax.dynamic_index_in_dim(half, high, 0, False), ("seq", "dp"), [(t, s) for s, t in first]
    )
    b = lax.ppermute(
        lax.dynamic_index_in_dim(half, 1 - high, 0, False),
        ("seq", "dp"),
        [(t, s) for s, t in second],
    )
    return jnp.where(odd == 0, jnp.stack([a, b]), jnp.stack([b, a]))


def pad_rows(x, multiple):
    return jnp.pad(x, ((0, -x.shape[0] % multiple), (0, 0)))


def local(
    layer_in,
    cotangent,
    valid_len,
    sep_pos,
    w_query,
    w_key,
    w_value,
    w_depth,
    w_point,
    w_kernel,
    w_convout,
    w_output,
    gain_attn,
    shift_attn,
    w_up,
    w_down,
    gain_out,
    shift_out,
):
    seq, dp = lax.axis_size("seq"), lax.axis_size("dp")
    count = seq * dp
    z, d = lax.axis_index("seq"), lax.axis_index("dp")
    core = d & 1
    me = z * dp + d
    codes = relative_codes()
    absolute = jnp.asarray(np.array(codes, np.int32)) ^ me
    inverse = np.zeros(count, np.int32)
    inverse[np.array(codes)] = np.arange(count)
    relative = jnp.asarray(inverse)[jnp.arange(count, dtype=jnp.int32) ^ me]
    width = layer_in.shape[-1]
    wide = w_query.shape[1]
    rows = w_query.shape[0]
    hidden = w_up.shape[2]

    small = jnp.concatenate(
        [w_kernel, w_depth.reshape(-1), gain_attn, shift_attn, gain_out, shift_out]
    )
    small_size = small.shape[0]
    small = pad_rows(jnp.pad(small, (0, -small_size % wide)).reshape(-1, wide), 8)
    early = pad_rows(
        jnp.concatenate([w_query, w_key, w_value, w_point, w_convout, small]), 16
    )
    late = pad_rows(
        jnp.concatenate(
            [
                w_output[:, :wide],
                w_output[:, wide:],
                jnp.swapaxes(w_up, 1, 2).reshape(2 * hidden, wide),
                w_down.reshape(2 * hidden, wide),
            ]
        ),
        16,
    )
    late_rows = late.shape[0]
    tokens_own = to_rows(layer_in[:, 0])
    tokens_other = swap(tokens_own, "dp", 1)
    row_tokens = jnp.where(
        core == 0,
        jnp.concatenate([tokens_own, tokens_other]),
        jnp.concatenate([tokens_other, tokens_own]),
    )
    late_all = lax.all_gather(late, ("seq", "dp"), axis=0, tiled=False)
    early_all = reorder(gather_relative(early), absolute)
    cot_own = to_rows(cotangent[:, 0])

    def take(index):
        return early_all[:, index * rows : (index + 1) * rows].reshape(count * rows, wide)

    small_all = early_all[:, 5 * rows : 5 * rows + small.shape[0]].reshape(count, -1)
    sizes = [w_kernel.shape[0], w_depth.size, rows, rows, rows, rows]
    offsets = np.cumsum([0] + sizes)
    pieces = [small_all[:, offsets[i] : offsets[i + 1]] for i in range(6)]
    kernel_flat = pieces[0].reshape(-1)
    depth_kernel = (
        pieces[1].reshape(count, KERNEL, rows).transpose(1, 0, 2).reshape(KERNEL, width)
    )
    gains = [p.reshape(-1) for p in pieces[2:]]
    out_weight = jnp.concatenate(
        [late_all[:, :rows].reshape(-1, wide), late_all[:, rows : 2 * rows].reshape(-1, wide)], 1
    )
    up_t = (
        late_all[:, 2 * rows : 2 * rows + 2 * hidden]
        .reshape(count, 2, hidden, wide)
        .transpose(1, 0, 2, 3)
        .reshape(2, count * hidden, wide)
    )
    down = (
        late_all[:, 2 * rows + 2 * hidden : 2 * rows + 4 * hidden]
        .reshape(count, 2, hidden, wide)
        .transpose(1, 0, 2, 3)
        .reshape(2, count * hidden, wide)
    )
    slot_valid = valid_len[:, 0]
    slot_sep = sep_pos[:, 0]
    pair_valid = jnp.stack([slot_valid, slot_sep]).astype(jnp.float32)
    pair_other = swap(pair_valid, "dp", 1)
    row_info = jnp.where((z & 1) == core, pair_valid, pair_other)[:, z >> 1].astype(jnp.int32)
    gathered = (
        take(0),
        take(1),
        take(2),
        depth_kernel,
        take(3),
        kernel_flat,
        take(4),
        out_weight,
        gains[0],
        gains[1],
        up_t,
        down,
        gains[2],
        gains[3],
    )
    layer_rows, grad_input, grads = run_batch(
        gathered, tokens_own, row_tokens, cot_own, row_info[0], row_info[1], core
    )
    (
        d_query_w,
        d_key_w,
        d_value_w,
        d_depth_w,
        d_point_w,
        d_kernel_w,
        d_conv_w,
        d_out_w,
        d_attn_gain,
        d_attn_shift,
        d_up_w,
        d_down_w,
        d_out_gain,
        d_out_shift,
    ) = grads

    def blocks(x):
        return x.reshape(count, rows, wide)

    first_pack = jnp.concatenate(
        [
            blocks(d_out_w[:, :wide]),
            blocks(d_out_w[:, wide:]),
            d_up_w.reshape(2, count, hidden, wide)
            .transpose(1, 0, 2, 3)
            .reshape(count, 2 * hidden, wide),
            d_down_w.reshape(2, count, hidden, wide)
            .transpose(1, 0, 2, 3)
            .reshape(count, 2 * hidden, wide),
        ],
        1,
    ).astype(jnp.bfloat16)
    first_pack = jnp.pad(first_pack, ((0, 0), (0, late_rows - first_pack.shape[1]), (0, 0)))
    small_pack = jnp.concatenate(
        [
            d_kernel_w.reshape(count, -1),
            d_depth_w.reshape(KERNEL, count, rows).transpose(1, 0, 2).reshape(count, -1),
        ]
        + [g.reshape(count, rows) for g in (d_attn_gain, d_attn_shift, d_out_gain, d_out_shift)],
        1,
    )
    small_pack = jnp.pad(small_pack, ((0, 0), (0, small.size - small_size))).reshape(
        count, small.shape[0], wide
    )
    second_pack = jnp.concatenate(
        [blocks(g) for g in (d_query_w, d_key_w, d_value_w, d_point_w, d_conv_w)] + [small_pack], 1
    ).astype(jnp.bfloat16)
    second_pack = jnp.pad(
        second_pack, ((0, 0), (0, early.shape[0] - second_pack.shape[1]), (0, 0))
    )
    half = count // 2
    first_rel = reorder([first_pack], relative)
    second_rel = reorder([second_pack], relative)
    first = scatter_relative(first_rel[:half], first_rel[half:])
    second = scatter_relative(second_rel[:half], second_rel[half:])

    def part(index):
        return second[index * rows : (index + 1) * rows]

    flat = second[5 * rows : 5 * rows + small.shape[0]].reshape(-1)
    outs = [flat[offsets[i] : offsets[i + 1]] for i in range(6)]
    x_grad = from_rows(grad_input.astype(jnp.bfloat16)).astype(jnp.float32)
    return (
        from_rows(layer_rows)[:, None],
        x_grad[:, None],
        part(0),
        part(1),
        part(2),
        outs[1].reshape(KERNEL, rows),
        part(3),
        outs[0],
        part(4),
        jnp.concatenate([first[:rows], first[rows : 2 * rows]], 1),
        outs[2],
        outs[3],
        jnp.swapaxes(first[2 * rows : 2 * rows + 2 * hidden].reshape(2, hidden, wide), 1, 2),
        first[2 * rows + 2 * hidden : 2 * rows + 4 * hidden].reshape(2, hidden, wide),
        outs[4],
        outs[5],
    )


def solution(mesh):
    in_specs = (
        P(None, "dp", "seq", None),
        P(None, "dp", "seq", None),
        P(None, "dp"),
        P(None, "dp"),
        P(("seq", "dp"), None),
        P(("seq", "dp"), None),
        P(("seq", "dp"), None),
        P(None, ("seq", "dp")),
        P(("seq", "dp"), None),
        P(("seq", "dp")),
        P(("seq", "dp"), None),
        P(("seq", "dp"), None),
        P(("seq", "dp")),
        P(("seq", "dp")),
        P(None, None, ("seq", "dp")),
        P(None, ("seq", "dp"), None),
        P(("seq", "dp")),
        P(("seq", "dp")),
    )
    out_specs = (
        P(None, "dp", "seq", None),
        P(None, "dp", "seq", None),
        P(("seq", "dp"), None),
        P(("seq", "dp"), None),
        P(("seq", "dp"), None),
        P(None, ("seq", "dp")),
        P(("seq", "dp"), None),
        P(("seq", "dp")),
        P(("seq", "dp"), None),
        P(("seq", "dp"), None),
        P(("seq", "dp")),
        P(("seq", "dp")),
        P(None, None, ("seq", "dp")),
        P(None, ("seq", "dp"), None),
        P(("seq", "dp")),
        P(("seq", "dp")),
    )
    return jax.shard_map(local, mesh=mesh, in_specs=in_specs, out_specs=out_specs, check_vma=False)
```

```python
import functools

import jax
import jax.numpy as jnp
import numpy as np
from jax import lax
from jax.experimental import pallas as pl
from jax.experimental.pallas import tpu as pltpu
from jax.sharding import PartitionSpec as P

HEADS = 6
HEAD_DIM = 64
KERNEL = 9
GROUPS = 2
LEN = 1024
HALF = LEN // 2
WIDTH = 768
WIDE = HEADS * HEAD_DIM
CHUNK = 128
EDGE = 16
WINDOW = HALF + 2 * EDGE
BLOCKS = 32
HIDDEN = 48
PACK = 240

F32 = jnp.float32
BF16 = jnp.bfloat16

inv_root_two = 0.7071067811865476
inv_root_tau = 0.3989422804014327


def nn(a, b):
    return jnp.dot(a, b, preferred_element_type=F32)


def nt(a, b):
    return lax.dot_general(a, b, (((1,), (1,)), ((), ())), preferred_element_type=F32)


def tn(a, b):
    return lax.dot_general(a, b, (((0,), (0,)), ((), ())), preferred_element_type=F32)


def call(kernel, out_shape, args, scalars=1, scratch=(), flops=0):
    vmem = pl.BlockSpec(memory_space=pltpu.VMEM)
    return pl.pallas_call(
        kernel,
        out_shape=out_shape,
        in_specs=[pl.BlockSpec(memory_space=pltpu.SMEM)] * scalars
        + [vmem] * (len(args) - scalars),
        out_specs=jax.tree.map(lambda _: vmem, out_shape),
        scratch_shapes=list(scratch),
        compiler_params=pltpu.CompilerParams(vmem_limit_bytes=56 * 1024 * 1024),
        cost_estimate=pl.CostEstimate(flops=flops, bytes_accessed=0, transcendentals=0),
    )(*args)


def shape(dims, dtype):
    return jax.ShapeDtypeStruct(dims, dtype)


def lane(rows):
    return lax.broadcasted_iota(jnp.int32, (rows, CHUNK), 1)


def load_window(core, source, target, chunks):
    value = source(pl.ds(pl.multiple_of(core * (HALF - EDGE), EDGE), HALF + EDGE))
    start = pl.multiple_of(EDGE - core * EDGE, EDGE)
    edge = pl.multiple_of(core * (HALF + EDGE), EDGE)
    for c in range(chunks):
        target[c, pl.ds(edge, EDGE), :] = jnp.zeros((EDGE, CHUNK), F32)
        target[c, pl.ds(start, HALF + EDGE), :] = value[:, c * CHUNK : (c + 1) * CHUNK].astype(F32)


def weight(own, other, index):
    rows = slice(index * WIDE, (index + 1) * WIDE)
    return own[rows, :], other[rows, :]


def project(tokens, own, other, index):
    first, second = weight(own, other, index)
    return nn(tokens[:, :WIDE], first) + nn(tokens[:, WIDE:], second)


def fill_masks(info, masks):
    sep, valid, core = info[1], info[0], info[2]

    def segment(position):
        return jnp.where(position < sep, 0, jnp.where(position < valid, 1, 2))

    row = core * HALF + lax.broadcasted_iota(jnp.int32, (HALF, CHUNK), 0)
    own = segment(row)
    for j in range(KERNEL):
        masks[j] = (segment(row + (j - 4)) == own).astype(F32)


def permute_kernel(tokens, matrix, out):
    out[...] = nn(tokens[...], matrix[...]).astype(BF16)


def attend_kernel(info, tokens, own, other, q_out, k_out, v_out, att_out, stat_out):
    core, valid = info[2], info[0]
    mine = tokens[pl.ds(pl.multiple_of(core * HALF, HALF), HALF), :]
    q_out[...] = project(mine, own, other, 0).astype(BF16)
    k_out[...] = project(tokens[...], own, other, 1).astype(BF16)
    v_out[...] = project(tokens[...], own, other, 2).astype(BF16)
    rows = 256
    bias = jnp.where(
        lax.broadcasted_iota(jnp.int32, (1, LEN), 1) < valid, 0.0, -1e30
    ).astype(F32)
    for block in range(HALF // rows):
        at = slice(block * rows, (block + 1) * rows)
        stats = jnp.zeros((rows, CHUNK), F32)
        for pair in range(HEADS // 2):
            cols = slice(pair * CHUNK, (pair + 1) * CHUNK)
            q = q_out[at, cols] * BF16(0.125)
            k, v = k_out[:, cols], v_out[:, cols]
            results = []
            for head in range(2):
                keep = (lane(rows) < HEAD_DIM) == (head == 0)
                scores = nt(jnp.where(keep, q, BF16(0)), k) + bias
                peak = jnp.max(scores, -1, keepdims=True)
                exponent = jnp.exp(scores - peak)
                total = jnp.sum(exponent, -1, keepdims=True)
                results.append(nn(exponent.astype(BF16), v) / total)
                stats = jnp.where(
                    lane(rows) == 2 * pair + head, peak + jnp.log(total), stats
                )
            att_out[at, cols] = jnp.where(lane(rows) < HEAD_DIM, *results).astype(BF16)
        stat_out[at, :] = stats


def spread(j):
    row = lax.broadcasted_iota(jnp.int32, (CHUNK, WIDE), 0)
    col = lax.broadcasted_iota(jnp.int32, (CHUNK, WIDE), 1)
    return (row == (col >> 6) * KERNEL + j).astype(F32).astype(BF16)


def conv_kernel(
    info,
    tokens,
    own,
    other,
    q,
    att,
    taps_weight,
    depth_weight,
    context,
    key_out,
    attn_out,
    depth_out,
    values_out,
    spread_out,
    window,
    logits,
    masks,
):
    core = info[2]
    load_window(core, lambda rows: tokens[rows, :], window, WIDTH // CHUNK)
    fill_masks(info, masks)
    rows = 64
    for c in range(WIDTH // CHUNK):
        cols = slice(c * CHUNK, (c + 1) * CHUNK)
        for b in range(HALF // rows):
            total = jnp.zeros((rows, CHUNK), F32)
            for j in range(KERNEL):
                first = EDGE - 4 + b * rows + j
                total = total + depth_weight[j : j + 1, cols] * window[c, first : first + rows, :]
            depth_out[b * rows : (b + 1) * rows, cols] = total.astype(BF16)
    key_conv = project(depth_out[...], own, other, 3)
    key_out[...] = key_conv
    attn_out[...] = (key_conv * q[...].astype(F32)).astype(BF16)
    load_window(
        core, lambda rows: project(tokens[rows, :], own, other, 4), values_out, WIDE // CHUNK
    )
    for j in range(KERNEL):
        spread_out[j] = nn(taps_weight[...], spread(j)).astype(BF16)
        logits[j] = nn(attn_out[...], spread_out[j])
    context[:, :WIDE] = att[...]
    for b in range(HALF // rows):
        at = slice(b * rows, (b + 1) * rows)
        for c in range(WIDE // CHUNK):
            cols = slice(c * CHUNK, (c + 1) * CHUNK)
            peak = logits[0, at, cols]
            for j in range(1, KERNEL):
                peak = jnp.maximum(peak, logits[j, at, cols])
            total = jnp.zeros((rows, CHUNK), F32)
            result = jnp.zeros((rows, CHUNK), F32)
            for j in range(KERNEL):
                first = EDGE - 4 + b * rows + j
                exponent = jnp.exp(logits[j, at, cols] - peak)
                total = total + exponent
                result = result + exponent * masks[j, at, :] * values_out[
                    c, first : first + rows, :
                ]
            context[at, WIDE + c * CHUNK : WIDE + (c + 1) * CHUNK] = (result / total).astype(BF16)


def normalize(value):
    centred = value - jnp.mean(value, -1, keepdims=True)
    inv = lax.rsqrt(jnp.mean(centred * centred, -1, keepdims=True) + 1e-06)
    return centred * inv, inv


def normalize_back(grad, normed, inv, gain):
    e = grad * gain
    return inv * (
        e - jnp.mean(e, -1, keepdims=True) - normed * jnp.mean(e * normed, -1, keepdims=True)
    )


def feed_kernel(
    order,
    context,
    tokens,
    late,
    cotangent,
    gains,
    matrix,
    layer_out,
    first_out,
    context_grad,
    kept,
    sent,
    small_out,
    out_weight,
    up,
    down,
    act,
    slope,
    normed,
    attn,
    attn_low,
    grad_low,
    branch_low,
    second,
    scale,
):
    rows = 128
    steps = [slice(i * rows, (i + 1) * rows) for i in range(HALF // rows)]
    gain_attn, shift_attn = gains[0:1, :], gains[1:2, :]
    gain_out, shift_out = gains[2:3, :], gains[3:4, :]
    for i in range(BLOCKS // 2):
        sides = [late[2 * i + k, 0:HIDDEN, :].astype(F32) for k in range(2)]
        out_weight[i * HIDDEN : (i + 1) * HIDDEN, :] = jnp.concatenate(
            [jnp.concatenate([s[: HIDDEN // 2], s[HIDDEN // 2 :]], 1) for s in sides], 0
        ).astype(BF16)
    for h in range(2):
        for i in range(BLOCKS // 2):
            source = order[h * (BLOCKS // 2) + i]
            for g in range(GROUPS):
                at = slice(i * HIDDEN, (i + 1) * HIDDEN)
                up[g, h, at, :] = late[source, (1 + g) * HIDDEN : (2 + g) * HIDDEN, :]
                down[g, h, at, :] = late[source, (3 + g) * HIDDEN : (4 + g) * HIDDEN, :]
    for at in steps:
        branch = nn(context[at, :], out_weight[...]) + tokens[at, :].astype(F32)
        n, inv = normalize(branch)
        normed[at, :] = n
        scale[at, :] = inv
        value = n * gain_attn + shift_attn
        attn[at, :] = value
        attn_low[at, :] = value.astype(BF16)
    for g in range(GROUPS):
        part = slice(g * WIDE, (g + 1) * WIDE)
        for h in range(2):
            for at in steps:
                pre = nt(attn_low[at, part], up[g, h])
                cdf = 0.5 * (1.0 + lax.erf(pre * inv_root_two))
                act[g, h, at, :] = (pre * cdf).astype(BF16)
                slope[g, h, at, :] = cdf + pre * jnp.exp(-0.5 * pre * pre) * inv_root_tau
    gain_grad = jnp.zeros((1, WIDTH), F32)
    shift_grad = jnp.zeros((1, WIDTH), F32)
    for at in steps:
        value = attn[at, :] + jnp.concatenate(
            [
                nn(act[g, 0, at, :], down[g, 0]) + nn(act[g, 1, at, :], down[g, 1])
                for g in range(GROUPS)
            ],
            1,
        )
        n, inv = normalize(value)
        layer_out[at, :] = (n * gain_out + shift_out).astype(BF16)
        grad = cotangent[at, :].astype(F32)
        gain_grad = gain_grad + jnp.sum(grad * n, 0, keepdims=True)
        shift_grad = shift_grad + jnp.sum(grad, 0, keepdims=True)
        value = normalize_back(grad, n, inv, gain_out)
        second[at, :] = value
        grad_low[at, :] = value.astype(BF16)
    small_out[2:3, :] = gain_grad
    small_out[3:4, :] = shift_grad
    for g in range(GROUPS):
        part = slice(g * WIDE, (g + 1) * WIDE)
        for h in range(2):
            target = (kept, sent)[h]
            result = tn(act[g, h], grad_low[:, part]).astype(BF16)
            for i in range(BLOCKS // 2):
                target[i, (3 + g) * HIDDEN : (4 + g) * HIDDEN, :] = result[
                    i * HIDDEN : (i + 1) * HIDDEN
                ]
            for at in steps:
                act[g, h, at, :] = (
                    nt(grad_low[at, part], down[g, h]) * slope[g, h, at, :]
                ).astype(BF16)
            result = tn(act[g, h], attn_low[:, part]).astype(BF16)
            for i in range(BLOCKS // 2):
                target[i, (1 + g) * HIDDEN : (2 + g) * HIDDEN, :] = result[
                    i * HIDDEN : (i + 1) * HIDDEN
                ]
    gain_grad = jnp.zeros((1, WIDTH), F32)
    shift_grad = jnp.zeros((1, WIDTH), F32)
    for at in steps:
        grad = second[at, :] + jnp.concatenate(
            [nn(act[g, 0, at, :], up[g, 0]) + nn(act[g, 1, at, :], up[g, 1]) for g in range(GROUPS)],
            1,
        )
        n = normed[at, :]
        gain_grad = gain_grad + jnp.sum(grad * n, 0, keepdims=True)
        shift_grad = shift_grad + jnp.sum(grad, 0, keepdims=True)
        value = normalize_back(grad, n, scale[at, :], gain_attn)
        first_out[at, :] = value
        branch_low[at, :] = value.astype(BF16)
        context_grad[at, :] = nt(branch_low[at, :], out_weight[...]).astype(BF16)
        grad_low[at, :] = nn(context[at, :], matrix[...]).astype(BF16)
    small_out[0:1, :] = gain_grad
    small_out[1:2, :] = shift_grad
    small_out[4:8, :] = jnp.zeros((4, WIDTH), F32)
    for h in range(2):
        result = tn(grad_low[:, h * WIDE : (h + 1) * WIDE], branch_low[...])
        for i in range(BLOCKS // 2):
            piece = result[i * (HIDDEN // 2) : (i + 1) * (HIDDEN // 2)]
            (kept, sent)[h][i, 0:HIDDEN, :] = jnp.concatenate(
                [piece[:, :WIDE], piece[:, WIDE:]], 0
            ).astype(BF16)


def conv_back_kernel(
    info,
    tokens,
    own,
    other,
    q,
    context_grad,
    key_conv,
    conv_attn,
    depth_low,
    values,
    spreads,
    taps_weight,
    depth_weight,
    query_out,
    point_out,
    kernel_out,
    depth_grad,
    values_grad,
    input_grad,
    rim_out,
    window,
    logits,
    masks,
    sums,
    pads,
    depth_back,
    compact,
):
    core = info[2]
    load_window(core, lambda rows: tokens[rows, :], window, WIDTH // CHUNK)
    fill_masks(info, masks)
    rows = 64
    steps = [slice(i * rows, (i + 1) * rows) for i in range(HALF // rows)]
    block = (lax.broadcasted_iota(jnp.int32, (CHUNK, CHUNK), 0) >> 6) == (
        lax.broadcasted_iota(jnp.int32, (CHUNK, CHUNK), 1) >> 6
    )
    ones = block.astype(F32).astype(BF16)
    pick_row = lax.broadcasted_iota(jnp.int32, (CHUNK, CHUNK), 0)
    pick_col = lax.broadcasted_iota(jnp.int32, (CHUNK, CHUNK), 1)
    for j in range(KERNEL):
        logits[j] = nn(conv_attn[...], spreads[j])
        pads[j, 0:EDGE, :] = jnp.zeros((EDGE, CHUNK), F32)
        pads[j, HALF + EDGE : WINDOW, :] = jnp.zeros((EDGE, CHUNK), F32)
    total_compact = jnp.zeros((HALF, CHUNK), F32)
    for c in range(WIDE // CHUNK):
        cols = slice(c * CHUNK, (c + 1) * CHUNK)
        grad_cols = slice(WIDE + c * CHUNK, WIDE + (c + 1) * CHUNK)
        for j in range(KERNEL):
            product = (
                context_grad[:, grad_cols].astype(F32)
                * values[c, EDGE - 4 + j : EDGE - 4 + j + HALF, :]
            )
            sums[j] = nn(product.astype(BF16), ones)
        for b, at in enumerate(steps):
            grad = context_grad[at, grad_cols].astype(F32)
            peak = logits[0, at, cols]
            for j in range(1, KERNEL):
                peak = jnp.maximum(peak, logits[j, at, cols])
            total = jnp.zeros((rows, CHUNK), F32)
            dot = jnp.zeros((rows, CHUNK), F32)
            for j in range(KERNEL):
                exponent = jnp.exp(logits[j, at, cols] - peak)
                mask = masks[j, at, :]
                logits[j, at, cols] = exponent
                change = sums[j, at, :] * mask
                sums[j, at, :] = change
                total = total + exponent
                dot = dot + exponent * change
            inv = 1.0 / total
            dot = dot * inv
            inside = slice(EDGE + b * rows, EDGE + (b + 1) * rows)
            for j in range(KERNEL):
                tap = logits[j, at, cols] * inv
                pads[j, inside, :] = tap * masks[j, at, :] * grad
                compact[j, at, :] = (tap * (sums[j, at, :] - dot)).astype(BF16)
        for j in range(KERNEL):
            pick = (pick_row & 63 == 0) & (pick_col == (2 * c + (pick_row >> 6)) * KERNEL + j)
            total_compact = total_compact + nn(compact[j], pick.astype(F32).astype(BF16))
        for b in range(WINDOW // 32):
            total = jnp.zeros((32, CHUNK), F32)
            for j in range(KERNEL):
                first = b * 32 + 4 - j
                low, high = max(first, 0), min(first + 32, WINDOW)
                piece = pads[j, low:high, :]
                if high - low < 32:
                    zero = jnp.zeros((32 - (high - low), CHUNK), F32)
                    piece = jnp.concatenate([zero, piece] if low > first else [piece, zero], 0)
                total = total + piece
            values_grad[c, b * 32 : (b + 1) * 32, :] = total
    compact_low = total_compact.astype(BF16)
    kernel_out[...] = tn(conv_attn[...], compact_low)
    attn_grad = nt(compact_low, taps_weight[...])
    query_out[...] = attn_grad * key_conv[...]
    key_low = (attn_grad * q[...].astype(F32)).astype(BF16)
    point_out[...] = tn(depth_low[...], key_low)
    depth_grad[...] = jnp.zeros((16, WIDTH), F32)
    for side, rows_weight in enumerate(weight(own, other, 3)):
        back = nt(key_low, rows_weight)
        for k in range(WIDE // CHUNK):
            c = side * (WIDE // CHUNK) + k
            depth_back[0:EDGE, :] = jnp.zeros((EDGE, CHUNK), F32)
            depth_back[HALF + EDGE : WINDOW, :] = jnp.zeros((EDGE, CHUNK), F32)
            depth_back[EDGE : HALF + EDGE, :] = back[:, k * CHUNK : (k + 1) * CHUNK]
            cols = slice(c * CHUNK, (c + 1) * CHUNK)
            totals = [jnp.zeros((8, CHUNK), F32) for _ in range(KERNEL)]
            for b in range(HALF // 32):
                grad = depth_back[EDGE + b * 32 : EDGE + (b + 1) * 32, :]
                for j in range(KERNEL):
                    first = EDGE - 4 + b * 32 + j
                    product = grad * window[c, first : first + 32, :]
                    totals[j] = totals[j] + (
                        (product[0:8] + product[8:16]) + (product[16:24] + product[24:32])
                    )
            for j in range(KERNEL):
                depth_grad[j : j + 1, cols] = jnp.sum(totals[j], 0, keepdims=True)
            for b in range(WINDOW // 32):
                total = jnp.zeros((32, CHUNK), F32)
                for j in range(KERNEL):
                    first = b * 32 + 4 - j
                    low, high = max(first, 0), min(first + 32, WINDOW)
                    piece = depth_back[low:high, :]
                    if high - low < 32:
                        zero = jnp.zeros((32 - (high - low), CHUNK), F32)
                        piece = jnp.concatenate([zero, piece] if low > first else [piece, zero], 0)
                    total = total + depth_weight[j : j + 1, cols] * piece
                input_grad[c, b * 32 : (b + 1) * 32, :] = total
    rim = pl.multiple_of((1 - core) * (HALF + EDGE), EDGE)
    rim_out[...] = jnp.zeros((2 * EDGE, WIDTH), BF16)
    for c in range(WIDTH // CHUNK):
        turned = (c + WIDE // CHUNK) % (WIDTH // CHUNK)
        rim_out[0:EDGE, turned * CHUNK : (turned + 1) * CHUNK] = input_grad[
            c, pl.ds(rim, EDGE), :
        ].astype(BF16)
    for c in range(WIDE // CHUNK):
        rim_out[EDGE : 2 * EDGE, c * CHUNK : (c + 1) * CHUNK] = values_grad[
            c, pl.ds(rim, EDGE), :
        ].astype(BF16)


def attend_back_kernel(
    info, q, k, v, context, context_grad, stats, rim, query_out, own_out, message, key_sum, value_sum
):
    core, valid = info[2], info[0]
    rows = 256
    live = lax.broadcasted_iota(jnp.int32, (LEN, CHUNK), 0) < valid
    for pair in range(HEADS // 2):
        cols = slice(pair * CHUNK, (pair + 1) * CHUNK)
        keys, vals = k[:, cols], v[:, cols]
        for head in range(2):
            even = head == 0
            base = HEAD_DIM if even else 0
            key_lane = lane(LEN)
            keep_key = (key_lane < HEAD_DIM) == even
            keys_more = jnp.where(
                keep_key,
                keys.astype(F32),
                jnp.where(
                    key_lane == base,
                    jnp.where(live, 0.0, -1e30),
                    jnp.where(key_lane < base + 4, 1.0, 0.0),
                ),
            ).astype(BF16)
            vals_more = jnp.where(
                keep_key, vals.astype(F32), jnp.where(key_lane < base + 3, 1.0, 0.0)
            ).astype(BF16)
            keys_turned = keys_more.T
            for block in range(HALF // rows):
                at = slice(block * rows, (block + 1) * rows)
                here = lane(rows)
                keep = (here < HEAD_DIM) == even

                def three(value):
                    high = value.astype(BF16).astype(F32)
                    middle = (value - high).astype(BF16).astype(F32)
                    return high, middle, value - high - middle

                grad = context_grad[at, cols].astype(F32)
                product = jnp.where(keep, grad * context[at, cols].astype(F32), 0.0)
                dots = three(-jnp.sum(product, -1, keepdims=True))
                stat = three(-stats[at, 2 * pair + head : 2 * pair + head + 1])
                grad_more = jnp.where(
                    keep,
                    grad,
                    jnp.where(
                        here == base,
                        dots[0],
                        jnp.where(
                            here == base + 1, dots[1], jnp.where(here == base + 2, dots[2], 0.0)
                        ),
                    ),
                ).astype(BF16)
                query_more = jnp.where(
                    keep,
                    q[at, cols].astype(F32) * 0.125,
                    jnp.where(
                        here == base,
                        1.0,
                        jnp.where(
                            here == base + 1,
                            stat[0],
                            jnp.where(
                                here == base + 2, stat[1], jnp.where(here == base + 3, stat[2], 0.0)
                            ),
                        ),
                    ),
                ).astype(BF16)
                probs = jnp.exp(nt(keys_more, query_more))
                change = (probs * nt(vals_more, grad_more)).astype(BF16)
                value_part = nn(probs.astype(BF16), grad_more)
                key_part = nn(change, query_more)
                query_part = nn(keys_turned, change).T * 0.125
                if block == 0:
                    value_total, key_total = value_part, key_part
                else:
                    value_total, key_total = value_total + value_part, key_total + key_part
                if even:
                    query_out[at, cols] = query_part
                else:
                    query_out[at, cols] = jnp.where(keep, query_part, query_out[at, cols])
            if even:
                key_sum[:, cols] = key_total
                value_sum[:, cols] = value_total
            else:
                key_sum[:, cols] = jnp.where(keep_key, key_total, key_sum[:, cols])
                value_sum[:, cols] = jnp.where(keep_key, value_total, value_sum[:, cols])
    mine = pl.ds(pl.multiple_of(core * HALF, HALF), HALF)
    theirs = pl.ds(pl.multiple_of((1 - core) * HALF, HALF), HALF)
    own_out[:, :WIDE] = key_sum[mine, :]
    own_out[:, WIDE:] = value_sum[mine, :]
    message[0:HALF, :WIDE] = key_sum[theirs, :].astype(BF16)
    message[0:HALF, WIDE:] = value_sum[theirs, :].astype(BF16)
    message[HALF:WINDOW, :] = rim[...]


def finish_kernel(
    info,
    tokens,
    own,
    other,
    matrix,
    query_attn,
    query_conv,
    own_part,
    arrived,
    values_grad,
    input_grad,
    point_grad,
    small,
    first_grad,
    kept,
    sent,
    x_grad,
    values_sum,
    inputs,
):
    core = info[2]
    query_low = (query_attn[...] + query_conv[...]).astype(BF16)
    both = own_part[...] + arrived[0:HALF, :].astype(F32)
    key_low = both[:, :WIDE].astype(BF16)
    value_low = both[:, WIDE:].astype(BF16)
    rim = pl.ds(pl.multiple_of((1 - core) * (HALF - EDGE), EDGE), EDGE)
    inside = slice(EDGE, EDGE + HALF)
    for c in range(WIDE // CHUNK):
        cols = slice(c * CHUNK, (c + 1) * CHUNK)
        values_sum[:, cols] = values_grad[c, inside, :]
    for c in range(WIDTH // CHUNK):
        cols = slice(c * CHUNK, (c + 1) * CHUNK)
        inputs[:, cols] = input_grad[c, inside, :]
    inputs[rim, :] = inputs[rim, :] + arrived[HALF : HALF + EDGE, :].astype(F32)
    values_sum[rim, :] = values_sum[rim, :] + arrived[HALF + EDGE : WINDOW, :WIDE].astype(F32)
    values_low = values_sum[...].astype(BF16)
    mine = tokens[pl.ds(pl.multiple_of(core * HALF, HALF), HALF), :]
    grads = [query_low, key_low, value_low, None, values_low]
    unit = HIDDEN // 2
    for h in range(2):
        part = mine[:, h * WIDE : (h + 1) * WIDE]
        results = [
            point_grad[h * WIDE : (h + 1) * WIDE, :] if g is None else tn(part, g) for g in grads
        ]
        target = (kept, sent)[h]
        for i in range(BLOCKS // 2):
            at = slice(i * unit, (i + 1) * unit)
            target[i, 0:48, :] = jnp.concatenate([results[0][at], results[1][at]], 0).astype(BF16)
            target[i, 48:96, :] = jnp.concatenate([results[2][at], results[3][at]], 0).astype(BF16)
            target[i, 96:128, :] = jnp.concatenate(
                [results[4][at], small[h * (BLOCKS // 2) + i]], 0
            ).astype(BF16)
        rows = (own, other)[h]
        total = inputs[:, h * WIDE : (h + 1) * WIDE]
        for index, g in enumerate(grads):
            if g is not None:
                total = total + nt(g, rows[index * WIDE : (index + 1) * WIDE, :])
        inputs[:, h * WIDE : (h + 1) * WIDE] = total
    x_grad[...] = (nt(inputs[...].astype(BF16), matrix[...]) + first_grad[...]).astype(BF16)


def dp_groups(count):
    masks = []
    bit = 2
    while bit < count:
        if bit * 2 < count:
            masks.append((bit, 2 * bit, 3 * bit))
            bit *= 4
        else:
            masks.append((bit,))
            bit *= 2
    return masks


def swap(x, axis, mask):
    count = lax.axis_size(axis)
    return lax.ppermute(x, axis, [(i, i ^ mask) for i in range(count)])


def relative_codes():
    seq, dp = lax.axis_size("seq"), lax.axis_size("dp")
    codes = [j * dp for j in range(seq)]
    for masks in dp_groups(dp):
        codes = [c ^ m for m in (0,) + masks for c in codes]
    return codes + [c ^ 1 for c in codes]


def add_up(parts):
    total = parts[0].astype(jnp.float32)
    for part in parts[1:]:
        total = total + part.astype(jnp.float32)
    return total


def scatter_relative(kept, sent):
    seq, dp = lax.axis_size("seq"), lax.axis_size("dp")
    held = add_up([kept, swap(sent, "dp", 1)]).astype(jnp.bfloat16)
    for masks in reversed(dp_groups(dp)):
        held = held.reshape((len(masks) + 1, -1) + held.shape[1:])
        parts = [held[0]] + [swap(held[i + 1], "dp", m) for i, m in enumerate(masks)]
        held = add_up(parts).astype(jnp.bfloat16)
    return add_up([held[0]] + [swap(held[j], "seq", j) for j in range(1, seq)])


def token_perms():
    seq, dp = lax.axis_size("seq"), lax.axis_size("dp")
    first, second = [], []
    for z in range(seq):
        for d in range(dp):
            core, rest = d & 1, d & ~1
            odd = z & 1
            first.append((z * dp + d, (2 * odd + core) * dp + rest + (z >> 1)))
            second.append((z * dp + d, (2 * (1 - odd) + core) * dp + rest + (z >> 1)))
    return first, second


def to_rows(x):
    first, second = token_perms()
    z = lax.axis_index("seq")
    odd, high = z & 1, z >> 1
    a = lax.ppermute(lax.dynamic_index_in_dim(x, odd, 0, False), ("seq", "dp"), first)
    b = lax.ppermute(lax.dynamic_index_in_dim(x, 1 - odd, 0, False), ("seq", "dp"), second)
    return jnp.where(high == 0, jnp.concatenate([a, b]), jnp.concatenate([b, a]))


def from_rows(x):
    first, second = token_perms()
    z = lax.axis_index("seq")
    odd, high = z & 1, z >> 1
    half = x.reshape(2, x.shape[0] // 2, x.shape[1])
    a = lax.ppermute(
        lax.dynamic_index_in_dim(half, high, 0, False), ("seq", "dp"), [(t, s) for s, t in first]
    )
    b = lax.ppermute(
        lax.dynamic_index_in_dim(half, 1 - high, 0, False),
        ("seq", "dp"),
        [(t, s) for s, t in second],
    )
    return jnp.where(odd == 0, jnp.stack([a, b]), jnp.stack([b, a]))


def pad_rows(x, multiple):
    return jnp.pad(x, ((0, -x.shape[0] % multiple), (0, 0)))


def merge(packs, rows):
    cut = packs[0].shape[0] // (5 * rows + 8) * (5 * rows)
    weights = jnp.concatenate([p[:cut].reshape(5, -1, WIDE) for p in packs], 1)
    return jnp.concatenate([weights.reshape(-1, WIDE)] + [p[cut:] for p in packs])


def gather_weights(pack, rows):
    held = merge([pack] + [swap(pack, "seq", j) for j in range(1, lax.axis_size("seq"))], rows)
    for masks in dp_groups(lax.axis_size("dp")):
        held = merge([held] + [swap(held, "dp", m) for m in masks], rows)
    return held, swap(held, "dp", 1)


def to_lines(x):
    return jnp.pad(x, (0, -x.shape[0] % WIDE)).reshape(-1, WIDE)


def to_block(x):
    return jnp.pad(x, ((0, 0), (0, -x.shape[1] % WIDE)))


def regroup(late_all, order, rows, hidden):
    count = late_all.shape[0]
    relative = jnp.take(late_all, order, axis=0)

    def out_rows(first):
        return late_all[:, first : first + rows].reshape(BLOCKS, HIDDEN // 2, WIDE)

    def units(first):
        return relative[:, first : first + hidden].reshape(BLOCKS, HIDDEN, WIDE)

    parts = [out_rows(0), out_rows(rows)]
    parts += [units(2 * rows + i * hidden) for i in range(2 * GROUPS)]
    return jnp.concatenate(parts, 1), jnp.arange(BLOCKS, dtype=jnp.int32)


def split_late(packs, rows, hidden):
    cuts = [0, HIDDEN // 2] + [HIDDEN * i for i in range(1, 2 * GROUPS + 2)]
    sizes = [rows, rows] + [hidden] * (2 * GROUPS)
    parts = [
        packs[:, cuts[i] : cuts[i + 1]].reshape(-1, sizes[i], WIDE) for i in range(len(sizes))
    ]
    whole = jnp.concatenate(parts, 1)
    return jnp.pad(whole, ((0, 0), (0, -whole.shape[1] % 16), (0, 0)))


def split_early(packs, small, rows):
    parts = [packs[:, 24 * i : 24 * (i + 1)].reshape(-1, rows, WIDE) for i in range(5)]
    return jnp.concatenate(parts + [small.astype(BF16)], 1)


def local(
    layer_in,
    cotangent,
    valid_len,
    sep_pos,
    w_query,
    w_key,
    w_value,
    w_depth,
    w_point,
    w_kernel,
    w_convout,
    w_output,
    gain_attn,
    shift_attn,
    w_up,
    w_down,
    gain_out,
    shift_out,
):
    seq, dp = lax.axis_size("seq"), lax.axis_size("dp")
    count = seq * dp
    z, d = lax.axis_index("seq"), lax.axis_index("dp")
    core = d & 1
    me = z * dp + d
    codes = np.array(relative_codes(), np.int32)
    order = jnp.asarray(codes) ^ me
    to_absolute = (jnp.arange(count)[:, None] == order[None, :]).astype(BF16)
    rows = w_query.shape[0]
    hidden = w_up.shape[2]
    half = count // 2
    features = (order[:, None] * rows + jnp.arange(rows)[None, :]).reshape(1, WIDTH)
    matrix = (jnp.arange(WIDTH)[:, None] == features).astype(BF16)

    tokens_own = to_rows(layer_in[:, 0])
    lines = [
        to_lines(w_kernel),
        to_lines(w_depth.reshape(-1)),
        to_lines(jnp.concatenate([gain_attn, shift_attn, gain_out, shift_out])),
    ]
    starts = np.cumsum([0] + [line.shape[0] for line in lines])
    early = jnp.concatenate(
        [w_query, w_key, w_value, w_point, w_convout, pad_rows(jnp.concatenate(lines), 8)]
    )
    late = pad_rows(
        jnp.concatenate(
            [
                w_output[:, :WIDE],
                w_output[:, WIDE:],
                jnp.swapaxes(w_up, 1, 2).reshape(GROUPS * hidden, WIDE),
                w_down.reshape(GROUPS * hidden, WIDE),
            ]
        ),
        16,
    )
    late_all = lax.all_gather(late, ("seq", "dp"), axis=0, tiled=False)
    own, other = gather_weights(early, rows)
    tokens_other = swap(tokens_own, "dp", 1)
    row_tokens = jnp.where(
        core == 0,
        jnp.concatenate([tokens_own, tokens_other]),
        jnp.concatenate([tokens_other, tokens_own]),
    )
    cot_own = to_rows(cotangent[:, 0])
    pair_info = jnp.stack([valid_len[:, 0], sep_pos[:, 0]]).astype(F32)
    row_info = jnp.where((z & 1) == core, pair_info, swap(pair_info, "dp", 1))[:, z >> 1]
    info = jnp.concatenate([row_info.astype(jnp.int32), core[None]])

    turned = call(
        permute_kernel,
        shape((LEN, WIDTH), BF16),
        (row_tokens, matrix),
        0,
        flops=2 * LEN * WIDTH * WIDTH,
    )
    q, k, v, att, stats = call(
        attend_kernel,
        (
            shape((HALF, WIDE), BF16),
            shape((LEN, WIDE), BF16),
            shape((LEN, WIDE), BF16),
            shape((HALF, WIDE), BF16),
            shape((HALF, CHUNK), F32),
        ),
        (info, turned, own, other),
        flops=10**10,
    )
    small_rel = jnp.concatenate([own[5 * WIDE :], other[5 * WIDE :]]).reshape(count, -1, WIDE)
    kernel_rel = small_rel[:, starts[0] : starts[1]].reshape(count, -1)[:, : w_kernel.shape[0]]
    depth_rel = small_rel[:, starts[1] : starts[2]].reshape(count, -1)[:, : w_depth.size]
    gains_rel = small_rel[:, starts[2] : starts[3]].reshape(count, -1)[:, : 4 * rows]
    kernel_abs = jnp.dot(to_absolute, kernel_rel, preferred_element_type=F32).astype(BF16)
    taps_weight = jnp.pad(
        kernel_abs.reshape(WIDE, HEADS * KERNEL), ((0, 0), (0, CHUNK - HEADS * KERNEL))
    )
    depth_weight = jnp.pad(
        depth_rel.astype(F32).reshape(count, KERNEL, rows).transpose(1, 0, 2).reshape(KERNEL, WIDTH),
        ((0, 16 - KERNEL), (0, 0)),
    )
    gains = jnp.pad(
        jnp.dot(to_absolute, gains_rel, preferred_element_type=F32)
        .reshape(count, 4, rows)
        .transpose(1, 0, 2)
        .reshape(4, WIDTH),
        ((0, 4), (0, 0)),
    )
    context, key_conv, conv_attn, depth_low, values, spreads = call(
        conv_kernel,
        (
            shape((HALF, WIDTH), BF16),
            shape((HALF, WIDE), F32),
            shape((HALF, WIDE), BF16),
            shape((HALF, WIDTH), BF16),
            shape((WIDE // CHUNK, WINDOW, CHUNK), F32),
            shape((KERNEL, WIDE, WIDE), BF16),
        ),
        (info, turned, own, other, q, att, taps_weight, depth_weight),
        scratch=(
            pltpu.VMEM((WIDTH // CHUNK, WINDOW, CHUNK), F32),
            pltpu.VMEM((KERNEL, HALF, WIDE), F32),
            pltpu.VMEM((KERNEL, HALF, CHUNK), F32),
        ),
        flops=10**10,
    )
    if count == BLOCKS:
        late_blocks, late_order = late_all, order
    else:
        late_blocks, late_order = regroup(late_all, order, rows, hidden)
    halves = (GROUPS, 2, BLOCKS // 2 * HIDDEN, WIDE)
    layer_rows, first_grad, context_grad, kept, sent, gain_grads = call(
        feed_kernel,
        (
            shape((HALF, WIDTH), BF16),
            shape((HALF, WIDTH), F32),
            shape((HALF, WIDTH), BF16),
            shape((BLOCKS // 2, PACK, WIDE), BF16),
            shape((BLOCKS // 2, PACK, WIDE), BF16),
            shape((8, WIDTH), F32),
        ),
        (late_order, context, tokens_own, late_blocks, cot_own, gains, matrix),
        scratch=(
            pltpu.VMEM((WIDTH, WIDTH), BF16),
            pltpu.VMEM(halves, BF16),
            pltpu.VMEM(halves, BF16),
            pltpu.VMEM((GROUPS, 2, HALF, WIDTH), BF16),
            pltpu.VMEM((GROUPS, 2, HALF, WIDTH), F32),
            pltpu.VMEM((HALF, WIDTH), F32),
            pltpu.VMEM((HALF, WIDTH), F32),
            pltpu.VMEM((HALF, WIDTH), BF16),
            pltpu.VMEM((HALF, WIDTH), BF16),
            pltpu.VMEM((HALF, WIDTH), BF16),
            pltpu.VMEM((HALF, WIDTH), F32),
            pltpu.VMEM((HALF, 1), F32),
        ),
        flops=2 * 10**10,
    )
    if count == BLOCKS:
        first = scatter_relative(kept, sent)
    else:
        first = scatter_relative(split_late(kept, rows, hidden), split_late(sent, rows, hidden))
    query_conv, point_grad, kernel_grad, depth_grad, values_grad, input_grad, rim = call(
        conv_back_kernel,
        (
            shape((HALF, WIDE), F32),
            shape((WIDTH, WIDE), F32),
            shape((WIDE, CHUNK), F32),
            shape((16, WIDTH), F32),
            shape((WIDE // CHUNK, WINDOW, CHUNK), F32),
            shape((WIDTH // CHUNK, WINDOW, CHUNK), F32),
            shape((2 * EDGE, WIDTH), BF16),
        ),
        (
            info,
            turned,
            own,
            other,
            q,
            context_grad,
            key_conv,
            conv_attn,
            depth_low,
            values,
            spreads,
            taps_weight,
            depth_weight,
        ),
        scratch=(
            pltpu.VMEM((WIDTH // CHUNK, WINDOW, CHUNK), F32),
            pltpu.VMEM((KERNEL, HALF, WIDE), F32),
            pltpu.VMEM((KERNEL, HALF, CHUNK), F32),
            pltpu.VMEM((KERNEL, HALF, CHUNK), F32),
            pltpu.VMEM((KERNEL, WINDOW, CHUNK), F32),
            pltpu.VMEM((WINDOW, CHUNK), F32),
            pltpu.VMEM((KERNEL, HALF, CHUNK), BF16),
        ),
        flops=10**10,
    )
    query_attn, own_part, message = call(
        attend_back_kernel,
        (shape((HALF, WIDE), F32), shape((HALF, WIDTH), F32), shape((WINDOW, WIDTH), BF16)),
        (info, q, k, v, context, context_grad, stats, rim),
        scratch=(pltpu.VMEM((LEN, WIDE), F32), pltpu.VMEM((LEN, WIDE), F32)),
        flops=2 * 10**10,
    )
    arrived = swap(message, "dp", 1)

    kernel_lines = kernel_grad[:, : HEADS * KERNEL].reshape(count, -1)
    gain_lines = gain_grads[:4].reshape(4, count, rows).transpose(1, 0, 2).reshape(count, -1)
    turned_lines = lax.dot_general(
        to_absolute,
        jnp.concatenate([to_block(kernel_lines), to_block(gain_lines)], 1).astype(BF16),
        (((0,), (0,)), ((), ())),
        preferred_element_type=F32,
    )
    cut = starts[1] * WIDE
    depth_lines = to_block(
        depth_grad[:KERNEL].reshape(KERNEL, count, rows).transpose(1, 0, 2).reshape(count, -1)
    )
    small = jnp.concatenate([turned_lines[:, :cut], depth_lines, turned_lines[:, cut:]], 1)
    small = jnp.pad(small, ((0, 0), (0, 8 * WIDE - small.shape[1]))).reshape(count, 8, WIDE)
    kept, sent, x_low = call(
        finish_kernel,
        (
            shape((BLOCKS // 2, 128, WIDE), BF16),
            shape((BLOCKS // 2, 128, WIDE), BF16),
            shape((HALF, WIDTH), BF16),
        ),
        (
            info,
            turned,
            own,
            other,
            matrix,
            query_attn,
            query_conv,
            own_part,
            arrived,
            values_grad,
            input_grad,
            point_grad,
            small[:BLOCKS],
            first_grad,
        ),
        scratch=(pltpu.VMEM((HALF, WIDE), F32), pltpu.VMEM((HALF, WIDTH), F32)),
        flops=10**10,
    )
    if count != BLOCKS:
        kept, sent = split_early(kept, small[:half], rows), split_early(sent, small[half:], rows)
    second = scatter_relative(kept, sent)
    x_grad = from_rows(x_low).astype(F32)

    def part(index):
        return second[index * rows : (index + 1) * rows]

    lines = second[5 * rows : 5 * rows + 8].reshape(-1)
    kernel_at, depth_at, gain_at = (start * WIDE for start in starts[:3])
    depth_line = lines[depth_at : depth_at + w_depth.size].reshape(KERNEL, rows)
    gain_line = lines[gain_at : gain_at + 4 * rows].reshape(4, rows)
    return (
        from_rows(layer_rows)[:, None],
        x_grad[:, None],
        part(0),
        part(1),
        part(2),
        depth_line,
        part(3),
        lines[kernel_at : kernel_at + w_kernel.shape[0]],
        part(4),
        jnp.concatenate([first[:rows], first[rows : 2 * rows]], 1),
        gain_line[0],
        gain_line[1],
        jnp.swapaxes(
            first[2 * rows : 2 * rows + GROUPS * hidden].reshape(GROUPS, hidden, WIDE), 1, 2
        ),
        first[2 * rows + GROUPS * hidden : 2 * rows + 2 * GROUPS * hidden].reshape(
            GROUPS, hidden, WIDE
        ),
        gain_line[2],
        gain_line[3],
    )


def solution(mesh):
    in_specs = (
        P(None, "dp", "seq", None),
        P(None, "dp", "seq", None),
        P(None, "dp"),
        P(None, "dp"),
        P(("seq", "dp"), None),
        P(("seq", "dp"), None),
        P(("seq", "dp"), None),
        P(None, ("seq", "dp")),
        P(("seq", "dp"), None),
        P(("seq", "dp")),
        P(("seq", "dp"), None),
        P(("seq", "dp"), None),
        P(("seq", "dp")),
        P(("seq", "dp")),
        P(None, None, ("seq", "dp")),
        P(None, ("seq", "dp"), None),
        P(("seq", "dp")),
        P(("seq", "dp")),
    )
    out_specs = (
        P(None, "dp", "seq", None),
        P(None, "dp", "seq", None),
        P(("seq", "dp"), None),
        P(("seq", "dp"), None),
        P(("seq", "dp"), None),
        P(None, ("seq", "dp")),
        P(("seq", "dp"), None),
        P(("seq", "dp")),
        P(("seq", "dp"), None),
        P(("seq", "dp"), None),
        P(("seq", "dp")),
        P(("seq", "dp")),
        P(None, None, ("seq", "dp")),
        P(None, ("seq", "dp"), None),
        P(("seq", "dp")),
        P(("seq", "dp")),
    )
    return jax.shard_map(local, mesh=mesh, in_specs=in_specs, out_specs=out_specs, check_vma=False)
```

```python
import functools

import jax
import jax.numpy as jnp
import numpy as np
from jax import lax
from jax.experimental import pallas as pl
from jax.experimental.pallas import tpu as pltpu
from jax.sharding import PartitionSpec as P

HEADS = 6
HEAD_DIM = 64
KERNEL = 9
GROUPS = 2
LEN = 1024
HALF = LEN // 2
WIDTH = 768
WIDE = HEADS * HEAD_DIM
CHUNK = 128
EDGE = 16
WINDOW = HALF + 2 * EDGE
BLOCKS = 32
HIDDEN = 48
PACK = 240
COST = 10**8

F32 = jnp.float32
BF16 = jnp.bfloat16

inv_root_two = 0.7071067811865476
inv_root_tau = 0.3989422804014327


def nn(a, b):
    return jnp.dot(a, b, preferred_element_type=F32)


def nt(a, b):
    return lax.dot_general(a, b, (((1,), (1,)), ((), ())), preferred_element_type=F32)


def tn(a, b):
    return lax.dot_general(a, b, (((0,), (0,)), ((), ())), preferred_element_type=F32)


def call(kernel, out_shape, args, scalars=1, scratch=(), micros=0):
    vmem = pl.BlockSpec(memory_space=pltpu.VMEM)
    smem = pl.BlockSpec(memory_space=pltpu.SMEM)
    return pl.pallas_call(
        kernel,
        out_shape=out_shape,
        in_specs=[smem] * scalars
        + [vmem] * (len(args) - scalars),
        out_specs=jax.tree.map(
            lambda s: smem if s.dtype == jnp.int32 else vmem, out_shape
        ),
        scratch_shapes=list(scratch),
        compiler_params=pltpu.CompilerParams(vmem_limit_bytes=56 * 1024 * 1024),
        cost_estimate=pl.CostEstimate(flops=micros * COST, bytes_accessed=0, transcendentals=0),
    )(*args)


def shape(dims, dtype):
    return jax.ShapeDtypeStruct(dims, dtype)


def lane(rows):
    return lax.broadcasted_iota(jnp.int32, (rows, CHUNK), 1)


def load_window(core, source, target, chunks):
    value = source(pl.ds(pl.multiple_of(core * (HALF - EDGE), EDGE), HALF + EDGE))
    start = pl.multiple_of(EDGE - core * EDGE, EDGE)
    edge = pl.multiple_of(core * (HALF + EDGE), EDGE)
    for c in range(chunks):
        target[c, pl.ds(edge, EDGE), :] = jnp.zeros((EDGE, CHUNK), F32)
        target[c, pl.ds(start, HALF + EDGE), :] = value[:, c * CHUNK : (c + 1) * CHUNK].astype(F32)


def weight(own, other, index):
    rows = slice(index * WIDE, (index + 1) * WIDE)
    return own[rows, :], other[rows, :]


def project(tokens, own, other, index):
    first, second = weight(own, other, index)
    return nn(tokens[:, :WIDE], first) + nn(tokens[:, WIDE:], second)


def fill_masks(info, masks):
    sep, valid, core = info[1], info[0], info[2]

    def segment(position):
        return jnp.where(position < sep, 0, jnp.where(position < valid, 1, 2))

    row = core * HALF + lax.broadcasted_iota(jnp.int32, (HALF, CHUNK), 0)
    own = segment(row)
    for j in range(KERNEL):
        masks[j] = (segment(row + (j - 4)) == own).astype(F32)


def prepare_kernel(info, tokens, *refs):
    weights, small, early, token_a, token_b = refs[:5], refs[5], refs[6], refs[7], refs[8]
    rows = weights[0].shape[0]
    odd = info[0]
    token_a[...] = tokens[pl.ds(odd, 1), 0][0]
    token_b[...] = tokens[pl.ds(1 - odd, 1), 0][0]
    pieces = [ref[...].astype(F32) for ref in weights] + [small[...].astype(F32)]
    for i in range(3):
        pair = jnp.concatenate(pieces[2 * i : 2 * i + 2], 0)
        early[2 * i * rows : 2 * i * rows + pair.shape[0], :] = pair.astype(BF16)


def permute_kernel(
    place, mine, theirs, own_a, own_b, other_a, other_b, codes, info, out, own_out, matrix
):
    z, core, me, rows = place[0], place[1], place[2], place[3]
    high = z >> 1
    for i in range(2):
        own_value = jnp.where(high == 0, mine[i, 0], mine[i, 1])
        other_value = jnp.where(high == 0, theirs[i, 0], theirs[i, 1])
        info[i] = jnp.where((z & 1) == core, own_value, other_value).astype(jnp.int32)
    info[2] = core
    info[3] = high
    features = (codes[0:1, :] ^ me) * rows + codes[1:2, :]
    matrix[...] = (
        (lax.broadcasted_iota(jnp.int32, (WIDTH, WIDTH), 0) == features)
        .astype(F32)
        .astype(BF16)
    )
    quarter = HALF // 2
    for side, pieces in ((core, (own_a, own_b)), (1 - core, (other_a, other_b))):
        for place, piece in zip((high, 1 - high), pieces):
            at = pl.multiple_of(side * HALF + place * quarter, quarter)
            out[pl.ds(at, quarter), :] = nn(piece[...], matrix[...]).astype(BF16)
    own_out[pl.ds(pl.multiple_of(high * quarter, quarter), quarter), :] = own_a[...]
    own_out[pl.ds(pl.multiple_of((1 - high) * quarter, quarter), quarter), :] = own_b[...]


def attend_kernel(info, tokens, *refs):
    parts, refs = refs[:-8], refs[-8:]
    own, other, small_out, q_out, k_out, v_out, att_out, stat_out = refs
    core, valid = info[2], info[0]
    count = len(parts) // 2
    unit = WIDE // count
    rest = parts[0].shape[0] - 5 * unit
    for h, target in enumerate((own, other)):
        for i in range(count):
            part = parts[h * count + i]
            for w in range(5):
                target[w * WIDE + i * unit : w * WIDE + (i + 1) * unit, :] = part[
                    w * unit : (w + 1) * unit, :
                ]
            first = (h * count + i) * rest
            small_out[first : first + rest, :] = part[5 * unit :, :]
    mine = tokens[pl.ds(pl.multiple_of(core * HALF, HALF), HALF), :]
    q_out[...] = project(mine, own, other, 0).astype(BF16)
    k_out[...] = project(tokens[...], own, other, 1).astype(BF16)
    v_out[...] = project(tokens[...], own, other, 2).astype(BF16)
    rows = 256
    bias = jnp.where(
        lax.broadcasted_iota(jnp.int32, (1, LEN), 1) < valid, 0.0, -1e30
    ).astype(F32)
    for block in range(HALF // rows):
        at = slice(block * rows, (block + 1) * rows)
        stats = jnp.zeros((rows, CHUNK), F32)
        for pair in range(HEADS // 2):
            cols = slice(pair * CHUNK, (pair + 1) * CHUNK)
            q = q_out[at, cols] * BF16(0.125)
            k, v = k_out[:, cols], v_out[:, cols]
            results = []
            for head in range(2):
                keep = (lane(rows) < HEAD_DIM) == (head == 0)
                scores = nt(jnp.where(keep, q, BF16(0)), k) + bias
                peak = jnp.max(scores, -1, keepdims=True)
                exponent = jnp.exp(scores - peak)
                total = jnp.sum(exponent, -1, keepdims=True)
                results.append(nn(exponent.astype(BF16), v) / total)
                stats = jnp.where(
                    lane(rows) == 2 * pair + head, peak + jnp.log(total), stats
                )
            att_out[at, cols] = jnp.where(lane(rows) < HEAD_DIM, *results).astype(BF16)
        stat_out[at, :] = stats


def spread(j):
    row = lax.broadcasted_iota(jnp.int32, (CHUNK, WIDE), 0)
    col = lax.broadcasted_iota(jnp.int32, (CHUNK, WIDE), 1)
    return (row == (col >> 6) * KERNEL + j).astype(F32).astype(BF16)


def conv_kernel(
    info,
    tokens,
    own,
    other,
    q,
    att,
    taps_weight,
    depth_weight,
    context,
    key_out,
    attn_out,
    depth_out,
    values_out,
    spread_out,
    window,
    logits,
    masks,
):
    core = info[2]
    load_window(core, lambda rows: tokens[rows, :], window, WIDTH // CHUNK)
    fill_masks(info, masks)
    rows = 64
    for c in range(WIDTH // CHUNK):
        cols = slice(c * CHUNK, (c + 1) * CHUNK)
        for b in range(HALF // rows):
            total = jnp.zeros((rows, CHUNK), F32)
            for j in range(KERNEL):
                first = EDGE - 4 + b * rows + j
                total = total + depth_weight[j : j + 1, cols] * window[c, first : first + rows, :]
            depth_out[b * rows : (b + 1) * rows, cols] = total.astype(BF16)
    key_conv = project(depth_out[...], own, other, 3)
    key_out[...] = key_conv
    attn_out[...] = (key_conv * q[...].astype(F32)).astype(BF16)
    load_window(
        core, lambda rows: project(tokens[rows, :], own, other, 4), values_out, WIDE // CHUNK
    )
    for j in range(KERNEL):
        spread_out[j] = nn(taps_weight[...], spread(j)).astype(BF16)
        logits[j] = nn(attn_out[...], spread_out[j])
    context[:, :WIDE] = att[...]
    for b in range(HALF // rows):
        at = slice(b * rows, (b + 1) * rows)
        for c in range(WIDE // CHUNK):
            cols = slice(c * CHUNK, (c + 1) * CHUNK)
            peak = logits[0, at, cols]
            for j in range(1, KERNEL):
                peak = jnp.maximum(peak, logits[j, at, cols])
            total = jnp.zeros((rows, CHUNK), F32)
            result = jnp.zeros((rows, CHUNK), F32)
            for j in range(KERNEL):
                first = EDGE - 4 + b * rows + j
                exponent = jnp.exp(logits[j, at, cols] - peak)
                total = total + exponent
                result = result + exponent * masks[j, at, :] * values_out[
                    c, first : first + rows, :
                ]
            context[at, WIDE + c * CHUNK : WIDE + (c + 1) * CHUNK] = (result / total).astype(BF16)


def normalize(value):
    centred = value - jnp.mean(value, -1, keepdims=True)
    inv = lax.rsqrt(jnp.mean(centred * centred, -1, keepdims=True) + 1e-06)
    return centred * inv, inv


def normalize_back(grad, normed, inv, gain):
    e = grad * gain
    return inv * (
        e - jnp.mean(e, -1, keepdims=True) - normed * jnp.mean(e * normed, -1, keepdims=True)
    )


def store_piece(info, target_a, target_b, step, rows, value):
    inner = slice(step % 2 * rows, (step % 2 + 1) * rows)

    @pl.when(info[3] == step // 2)
    def _():
        target_a[inner, :] = value

    @pl.when(info[3] != step // 2)
    def _():
        target_b[inner, :] = value


def place_kernel(info, first, second, out):
    odd = info[0]
    out[pl.ds(odd, 1), 0] = first[...].astype(out.dtype)[None]
    out[pl.ds(1 - odd, 1), 0] = second[...].astype(out.dtype)[None]


def feed_kernel(
    info,
    order,
    context,
    tokens,
    late,
    cot_a,
    cot_b,
    gains,
    matrix,
    layer_a,
    layer_b,
    first_out,
    context_grad,
    kept,
    sent,
    small_out,
    out_weight,
    up,
    down,
    act,
    slope,
    normed,
    attn,
    attn_low,
    grad_low,
    branch_low,
    second,
    scale,
):
    rows = 128
    steps = [slice(i * rows, (i + 1) * rows) for i in range(HALF // rows)]
    gain_attn, shift_attn = gains[0:1, :], gains[1:2, :]
    gain_out, shift_out = gains[2:3, :], gains[3:4, :]
    for i in range(BLOCKS // 2):
        sides = [late[2 * i + k, 0:HIDDEN, :].astype(F32) for k in range(2)]
        out_weight[i * HIDDEN : (i + 1) * HIDDEN, :] = jnp.concatenate(
            [jnp.concatenate([s[: HIDDEN // 2], s[HIDDEN // 2 :]], 1) for s in sides], 0
        ).astype(BF16)
    for h in range(2):
        for i in range(BLOCKS // 2):
            source = order[h * (BLOCKS // 2) + i]
            for g in range(GROUPS):
                at = slice(i * HIDDEN, (i + 1) * HIDDEN)
                up[g, h, at, :] = late[source, (1 + g) * HIDDEN : (2 + g) * HIDDEN, :]
                down[g, h, at, :] = late[source, (3 + g) * HIDDEN : (4 + g) * HIDDEN, :]
    for at in steps:
        branch = nn(context[at, :], out_weight[...]) + tokens[at, :].astype(F32)
        n, inv = normalize(branch)
        normed[at, :] = n
        scale[at, :] = inv
        value = n * gain_attn + shift_attn
        attn[at, :] = value
        attn_low[at, :] = value.astype(BF16)
    for g in range(GROUPS):
        part = slice(g * WIDE, (g + 1) * WIDE)
        for h in range(2):
            for at in steps:
                pre = nt(attn_low[at, part], up[g, h])
                cdf = 0.5 * (1.0 + lax.erf(pre * inv_root_two))
                act[g, h, at, :] = (pre * cdf).astype(BF16)
                slope[g, h, at, :] = cdf + pre * jnp.exp(-0.5 * pre * pre) * inv_root_tau
    gain_grad = jnp.zeros((1, WIDTH), F32)
    shift_grad = jnp.zeros((1, WIDTH), F32)
    for step, at in enumerate(steps):
        value = attn[at, :] + jnp.concatenate(
            [
                nn(act[g, 0, at, :], down[g, 0]) + nn(act[g, 1, at, :], down[g, 1])
                for g in range(GROUPS)
            ],
            1,
        )
        n, inv = normalize(value)
        value = (n * gain_out + shift_out).astype(BF16)
        store_piece(info, layer_a, layer_b, step, rows, value)
        inner = slice(step % 2 * rows, (step % 2 + 1) * rows)
        grad = jnp.where(
            info[3] == step // 2, cot_a[inner, :].astype(F32), cot_b[inner, :].astype(F32)
        )
        gain_grad = gain_grad + jnp.sum(grad * n, 0, keepdims=True)
        shift_grad = shift_grad + jnp.sum(grad, 0, keepdims=True)
        value = normalize_back(grad, n, inv, gain_out)
        second[at, :] = value
        grad_low[at, :] = value.astype(BF16)
    small_out[2:3, :] = gain_grad
    small_out[3:4, :] = shift_grad
    for g in range(GROUPS):
        part = slice(g * WIDE, (g + 1) * WIDE)
        for h in range(2):
            target = (kept, sent)[h]
            result = tn(act[g, h], grad_low[:, part]).astype(BF16)
            for i in range(BLOCKS // 2):
                target[i, (3 + g) * HIDDEN : (4 + g) * HIDDEN, :] = result[
                    i * HIDDEN : (i + 1) * HIDDEN
                ]
            for at in steps:
                act[g, h, at, :] = (
                    nt(grad_low[at, part], down[g, h]) * slope[g, h, at, :]
                ).astype(BF16)
            result = tn(act[g, h], attn_low[:, part]).astype(BF16)
            for i in range(BLOCKS // 2):
                target[i, (1 + g) * HIDDEN : (2 + g) * HIDDEN, :] = result[
                    i * HIDDEN : (i + 1) * HIDDEN
                ]
    gain_grad = jnp.zeros((1, WIDTH), F32)
    shift_grad = jnp.zeros((1, WIDTH), F32)
    for at in steps:
        grad = second[at, :] + jnp.concatenate(
            [nn(act[g, 0, at, :], up[g, 0]) + nn(act[g, 1, at, :], up[g, 1]) for g in range(GROUPS)],
            1,
        )
        n = normed[at, :]
        gain_grad = gain_grad + jnp.sum(grad * n, 0, keepdims=True)
        shift_grad = shift_grad + jnp.sum(grad, 0, keepdims=True)
        value = normalize_back(grad, n, scale[at, :], gain_attn)
        first_out[at, :] = value
        branch_low[at, :] = value.astype(BF16)
        context_grad[at, :] = nt(branch_low[at, :], out_weight[...]).astype(BF16)
        grad_low[at, :] = nn(context[at, :], matrix[...]).astype(BF16)
    small_out[0:1, :] = gain_grad
    small_out[1:2, :] = shift_grad
    small_out[4:8, :] = jnp.zeros((4, WIDTH), F32)
    for h in range(2):
        result = tn(grad_low[:, h * WIDE : (h + 1) * WIDE], branch_low[...])
        for i in range(BLOCKS // 2):
            piece = result[i * (HIDDEN // 2) : (i + 1) * (HIDDEN // 2)]
            (kept, sent)[h][i, 0:HIDDEN, :] = jnp.concatenate(
                [piece[:, :WIDE], piece[:, WIDE:]], 0
            ).astype(BF16)


def shifted_sum(source, step, scale=None):
    total = jnp.zeros((32, CHUNK), F32)
    for j in range(KERNEL):
        first = step + 4 - j
        low, high = max(first, 0), min(first + 32, WINDOW)
        piece = source(j)[low:high, :]
        if high - low < 32:
            zero = jnp.zeros((32 - (high - low), CHUNK), F32)
            piece = jnp.concatenate([zero, piece] if low > first else [piece, zero], 0)
        total = total + (piece if scale is None else scale(j) * piece)
    return total


def taps_back_kernel(
    info,
    q,
    context_grad,
    key_conv,
    conv_attn,
    values,
    spreads,
    taps_weight,
    query_out,
    key_low,
    kernel_out,
    values_grad,
    rim_out,
    logits,
    masks,
    sums,
    pads,
    compact,
):
    core = info[2]
    fill_masks(info, masks)
    rows = 64
    steps = [slice(i * rows, (i + 1) * rows) for i in range(HALF // rows)]
    block = (lax.broadcasted_iota(jnp.int32, (CHUNK, CHUNK), 0) >> 6) == (
        lax.broadcasted_iota(jnp.int32, (CHUNK, CHUNK), 1) >> 6
    )
    ones = block.astype(F32).astype(BF16)
    pick_row = lax.broadcasted_iota(jnp.int32, (CHUNK, CHUNK), 0)
    pick_col = lax.broadcasted_iota(jnp.int32, (CHUNK, CHUNK), 1)
    for j in range(KERNEL):
        logits[j] = nn(conv_attn[...], spreads[j])
        pads[j, 0:EDGE, :] = jnp.zeros((EDGE, CHUNK), F32)
        pads[j, HALF + EDGE : WINDOW, :] = jnp.zeros((EDGE, CHUNK), F32)
    total_compact = jnp.zeros((HALF, CHUNK), F32)
    for c in range(WIDE // CHUNK):
        cols = slice(c * CHUNK, (c + 1) * CHUNK)
        grad_cols = slice(WIDE + c * CHUNK, WIDE + (c + 1) * CHUNK)
        for j in range(KERNEL):
            product = (
                context_grad[:, grad_cols].astype(F32)
                * values[c, EDGE - 4 + j : EDGE - 4 + j + HALF, :]
            )
            sums[j] = nn(product.astype(BF16), ones)
        for b, at in enumerate(steps):
            grad = context_grad[at, grad_cols].astype(F32)
            peak = logits[0, at, cols]
            for j in range(1, KERNEL):
                peak = jnp.maximum(peak, logits[j, at, cols])
            total = jnp.zeros((rows, CHUNK), F32)
            dot = jnp.zeros((rows, CHUNK), F32)
            for j in range(KERNEL):
                exponent = jnp.exp(logits[j, at, cols] - peak)
                mask = masks[j, at, :]
                logits[j, at, cols] = exponent
                change = sums[j, at, :] * mask
                sums[j, at, :] = change
                total = total + exponent
                dot = dot + exponent * change
            inv = 1.0 / total
            dot = dot * inv
            inside = slice(EDGE + b * rows, EDGE + (b + 1) * rows)
            for j in range(KERNEL):
                tap = logits[j, at, cols] * inv
                pads[j, inside, :] = tap * masks[j, at, :] * grad
                compact[j, at, :] = (tap * (sums[j, at, :] - dot)).astype(BF16)
        for j in range(KERNEL):
            pick = (pick_row & 63 == 0) & (pick_col == (2 * c + (pick_row >> 6)) * KERNEL + j)
            total_compact = total_compact + nn(compact[j], pick.astype(F32).astype(BF16))
        for b in range(WINDOW // 32):
            values_grad[c, b * 32 : (b + 1) * 32, :] = shifted_sum(lambda j: pads.at[j], b * 32)
    compact_low = total_compact.astype(BF16)
    kernel_out[...] = tn(conv_attn[...], compact_low)
    attn_grad = nt(compact_low, taps_weight[...])
    query_out[...] = attn_grad * key_conv[...]
    key_low[...] = (attn_grad * q[...].astype(F32)).astype(BF16)
    rim = pl.multiple_of((1 - core) * (HALF + EDGE), EDGE)
    for c in range(WIDE // CHUNK):
        rim_out[:, c * CHUNK : (c + 1) * CHUNK] = values_grad[c, pl.ds(rim, EDGE), :].astype(BF16)


def depth_back_kernel(
    info,
    tokens,
    own,
    other,
    key_low,
    depth_low,
    depth_weight,
    point_out,
    depth_grad,
    back_out,
    rim_out,
    window,
):
    core = info[2]
    load_window(core, lambda rows: tokens[rows, :], window, WIDTH // CHUNK)
    point_out[...] = tn(depth_low[...], key_low[...])
    depth_grad[...] = jnp.zeros((16, WIDTH), F32)
    for side, rows_weight in enumerate(weight(own, other, 3)):
        back = nt(key_low[...], rows_weight)
        for k in range(WIDE // CHUNK):
            c = side * (WIDE // CHUNK) + k
            back_out[c, 0:EDGE, :] = jnp.zeros((EDGE, CHUNK), F32)
            back_out[c, HALF + EDGE : WINDOW, :] = jnp.zeros((EDGE, CHUNK), F32)
            back_out[c, EDGE : HALF + EDGE, :] = back[:, k * CHUNK : (k + 1) * CHUNK]
    for c in range(WIDTH // CHUNK):
        cols = slice(c * CHUNK, (c + 1) * CHUNK)
        totals = [jnp.zeros((8, CHUNK), F32) for _ in range(KERNEL)]
        for b in range(HALF // 32):
            grad = back_out[c, EDGE + b * 32 : EDGE + (b + 1) * 32, :]
            for j in range(KERNEL):
                first = EDGE - 4 + b * 32 + j
                product = grad * window[c, first : first + 32, :]
                totals[j] = totals[j] + (
                    (product[0:8] + product[8:16]) + (product[16:24] + product[24:32])
                )
        for j in range(KERNEL):
            depth_grad[j : j + 1, cols] = jnp.sum(totals[j], 0, keepdims=True)
        low, high = (
            shifted_sum(lambda j: back_out.at[c], step, lambda j: depth_weight[j : j + 1, cols])
            for step in (0, WINDOW - 32)
        )
        turned = (c + WIDE // CHUNK) % (WIDTH // CHUNK)
        rim_out[:, turned * CHUNK : (turned + 1) * CHUNK] = jnp.where(
            core == 0, high[32 - EDGE :], low[:EDGE]
        ).astype(BF16)


def attend_back_kernel(
    info, q, k, v, context, context_grad, stats, query_out, own_out, message, key_sum, value_sum
):
    core, valid = info[2], info[0]
    rows = 256
    live = lax.broadcasted_iota(jnp.int32, (LEN, CHUNK), 0) < valid
    for pair in range(HEADS // 2):
        cols = slice(pair * CHUNK, (pair + 1) * CHUNK)
        keys, vals = k[:, cols], v[:, cols]
        for head in range(2):
            even = head == 0
            base = HEAD_DIM if even else 0
            key_lane = lane(LEN)
            keep_key = (key_lane < HEAD_DIM) == even
            keys_more = jnp.where(
                keep_key,
                keys.astype(F32),
                jnp.where(
                    key_lane == base,
                    jnp.where(live, 0.0, -1e30),
                    jnp.where(key_lane < base + 4, 1.0, 0.0),
                ),
            ).astype(BF16)
            vals_more = jnp.where(
                keep_key, vals.astype(F32), jnp.where(key_lane < base + 3, 1.0, 0.0)
            ).astype(BF16)
            keys_turned = keys_more.T
            for block in range(HALF // rows):
                at = slice(block * rows, (block + 1) * rows)
                here = lane(rows)
                keep = (here < HEAD_DIM) == even

                def three(value):
                    high = value.astype(BF16).astype(F32)
                    middle = (value - high).astype(BF16).astype(F32)
                    return high, middle, value - high - middle

                grad = context_grad[at, cols].astype(F32)
                product = jnp.where(keep, grad * context[at, cols].astype(F32), 0.0)
                dots = three(-jnp.sum(product, -1, keepdims=True))
                stat = three(-stats[at, 2 * pair + head : 2 * pair + head + 1])
                grad_more = jnp.where(
                    keep,
                    grad,
                    jnp.where(
                        here == base,
                        dots[0],
                        jnp.where(
                            here == base + 1, dots[1], jnp.where(here == base + 2, dots[2], 0.0)
                        ),
                    ),
                ).astype(BF16)
                query_more = jnp.where(
                    keep,
                    q[at, cols].astype(F32) * 0.125,
                    jnp.where(
                        here == base,
                        1.0,
                        jnp.where(
                            here == base + 1,
                            stat[0],
                            jnp.where(
                                here == base + 2, stat[1], jnp.where(here == base + 3, stat[2], 0.0)
                            ),
                        ),
                    ),
                ).astype(BF16)
                probs = jnp.exp(nt(keys_more, query_more))
                change = (probs * nt(vals_more, grad_more)).astype(BF16)
                value_part = nn(probs.astype(BF16), grad_more)
                key_part = nn(change, query_more)
                query_part = nn(keys_turned, change).T * 0.125
                if block == 0:
                    value_total, key_total = value_part, key_part
                else:
                    value_total, key_total = value_total + value_part, key_total + key_part
                if even:
                    query_out[at, cols] = query_part
                else:
                    query_out[at, cols] = jnp.where(keep, query_part, query_out[at, cols])
            if even:
                key_sum[:, cols] = key_total
                value_sum[:, cols] = value_total
            else:
                key_sum[:, cols] = jnp.where(keep_key, key_total, key_sum[:, cols])
                value_sum[:, cols] = jnp.where(keep_key, value_total, value_sum[:, cols])
    mine = pl.ds(pl.multiple_of(core * HALF, HALF), HALF)
    theirs = pl.ds(pl.multiple_of((1 - core) * HALF, HALF), HALF)
    own_out[:, :WIDE] = key_sum[mine, :]
    own_out[:, WIDE:] = value_sum[mine, :]
    message[:, :WIDE] = key_sum[theirs, :].astype(BF16)
    message[:, WIDE:] = value_sum[theirs, :].astype(BF16)


def grads_kernel(
    info,
    tokens,
    query_attn,
    query_conv,
    own_part,
    arrived,
    rim_values,
    values_grad,
    point_grad,
    small,
    kept,
    sent,
    low_out,
    values_sum,
):
    core = info[2]
    rim = pl.ds(pl.multiple_of((1 - core) * (HALF - EDGE), EDGE), EDGE)
    for c in range(WIDE // CHUNK):
        cols = slice(c * CHUNK, (c + 1) * CHUNK)
        values_sum[:, cols] = values_grad[c, EDGE : EDGE + HALF, :]
    values_sum[rim, :] = values_sum[rim, :] + rim_values[...].astype(F32)
    both = own_part[...] + arrived[...].astype(F32)
    low_out[0] = (query_attn[...] + query_conv[...]).astype(BF16)
    low_out[1] = both[:, :WIDE].astype(BF16)
    low_out[2] = both[:, WIDE:].astype(BF16)
    low_out[3] = values_sum[...].astype(BF16)
    mine = pl.ds(pl.multiple_of(core * HALF, HALF), HALF)
    unit = HIDDEN // 2
    for h in range(2):
        part = tokens[mine, h * WIDE : (h + 1) * WIDE]
        results = [tn(part, low_out[n]) for n in range(4)]
        point = point_grad[h * WIDE : (h + 1) * WIDE, :]
        target = (kept, sent)[h]
        for i in range(BLOCKS // 2):
            at = slice(i * unit, (i + 1) * unit)
            target[i, 0:48, :] = jnp.concatenate([results[0][at], results[1][at]], 0).astype(BF16)
            target[i, 48:96, :] = jnp.concatenate([results[2][at], point[at]], 0).astype(BF16)
            target[i, 96:128, :] = jnp.concatenate(
                [results[3][at], small[h * (BLOCKS // 2) + i]], 0
            ).astype(BF16)


def inputs_kernel(
    info,
    own,
    other,
    matrix,
    depth_weight,
    low,
    rim_inputs,
    back,
    first_grad,
    x_a,
    x_b,
    inputs,
):
    core = info[2]
    rim = pl.ds(pl.multiple_of((1 - core) * (HALF - EDGE), EDGE), EDGE)
    for c in range(WIDTH // CHUNK):
        cols = slice(c * CHUNK, (c + 1) * CHUNK)
        for b in range(HALF // 32):
            inputs[b * 32 : (b + 1) * 32, cols] = shifted_sum(
                lambda j: back.at[c], EDGE + b * 32, lambda j: depth_weight[j : j + 1, cols]
            )
    inputs[rim, :] = inputs[rim, :] + rim_inputs[...].astype(F32)
    for h in range(2):
        rows = (own, other)[h]
        total = inputs[:, h * WIDE : (h + 1) * WIDE]
        for n, index in enumerate((0, 1, 2, 4)):
            total = total + nt(low[n], rows[index * WIDE : (index + 1) * WIDE, :])
        inputs[:, h * WIDE : (h + 1) * WIDE] = total
    for step in range(4):
        at = slice(step * CHUNK, (step + 1) * CHUNK)
        value = nt(inputs[at, :].astype(BF16), matrix[...]) + first_grad[at, :]
        store_piece(info, x_a, x_b, step, CHUNK, value.astype(BF16))


def dp_groups(count):
    masks = []
    bit = 2
    while bit < count:
        if bit * 2 < count:
            masks.append((bit, 2 * bit, 3 * bit))
            bit *= 4
        else:
            masks.append((bit,))
            bit *= 2
    return masks


def swap(x, axis, mask):
    count = lax.axis_size(axis)
    return lax.ppermute(x, axis, [(i, i ^ mask) for i in range(count)])


def relative_codes():
    seq, dp = lax.axis_size("seq"), lax.axis_size("dp")
    codes = [j * dp for j in range(seq)]
    for masks in dp_groups(dp):
        codes = [c ^ m for m in (0,) + masks for c in codes]
    return codes + [c ^ 1 for c in codes]


def add_up(parts):
    total = parts[0].astype(jnp.float32)
    for part in parts[1:]:
        total = total + part.astype(jnp.float32)
    return total


def token_perms():
    seq, dp = lax.axis_size("seq"), lax.axis_size("dp")
    first, second = [], []
    for z in range(seq):
        for d in range(dp):
            core, rest = d & 1, d & ~1
            odd = z & 1
            first.append((z * dp + d, (2 * odd + core) * dp + rest + (z >> 1)))
            second.append((z * dp + d, (2 * (1 - odd) + core) * dp + rest + (z >> 1)))
    return first, second


def pad_rows(x, multiple):
    return jnp.pad(x, ((0, -x.shape[0] % multiple), (0, 0)))


def merge(packs, rows):
    cut = packs[0].shape[0] // (5 * rows + 8) * (5 * rows)
    weights = jnp.concatenate([p[:cut].reshape(5, -1, WIDE) for p in packs], 1)
    return jnp.concatenate([weights.reshape(-1, WIDE)] + [p[cut:] for p in packs])


def gather_weights(pack, rows, *tokens):
    held = merge([pack] + [swap(pack, "seq", j) for j in range(1, lax.axis_size("seq"))], rows)
    held, tokens = lax.optimization_barrier((held, tokens))
    tokens = send_pieces(*tokens)
    groups = dp_groups(lax.axis_size("dp"))
    for masks in groups[:-1]:
        held = merge([held] + [swap(held, "dp", m) for m in masks], rows)
    return [held] + [swap(held, "dp", m) for m in groups[-1]], *tokens


def send_pieces(a, b, back=False):
    first, second = token_perms()
    if back:
        first, second = ([(t, s) for s, t in perm] for perm in (first, second))
    return lax.ppermute(a, ("seq", "dp"), first), lax.ppermute(b, ("seq", "dp"), second)


def to_pieces(x):
    odd = lax.axis_index("seq") & 1
    a, b = (lax.dynamic_index_in_dim(x, index, 0, False) for index in (odd, 1 - odd))
    return send_pieces(a, b)


def wait_for(arrays, value):
    return lax.optimization_barrier((arrays, value))


class Scatter:
    def __init__(self, kept, sent, cut):
        self.bits = lax.axis_size("dp").bit_length() - 2
        self.stage = 0
        self.cut = cut
        self.held = kept, sent

    def pieces(self, whole, rows):
        dims = (2,) * self.bits + (-1,) + whole[0].shape[1:]
        return [part.reshape(dims)[..., rows, :] for part in whole]

    def step(self, value):
        if self.stage == 0:
            kept, sent = self.held
            arrived, value = wait_for(swap(sent, "dp", 1), value)
            first = self.pieces((kept, arrived), slice(0, self.cut))
            second = self.pieces((kept, arrived), slice(self.cut, None))
        elif self.stage <= self.bits:
            first, second = self.held
            arrived, value = wait_for(
                (
                    swap(first[1], "dp", 1 << (self.bits + 1 - self.stage)),
                    swap(second[1], "dp", 1 << self.stage),
                ),
                value,
            )
            first, second = [first[0], arrived[0]], [second[0], arrived[1]]
        else:
            arrived, value = wait_for(
                [swap(part, "seq", j + 1) for j, part in enumerate(self.held[1:])], value
            )
            self.held = add_up([self.held[0]] + arrived)
            return value
        self.stage += 1
        if self.stage <= self.bits:
            last = self.bits - self.stage
            self.held = [
                [add_up([p[i] for p in first]).astype(BF16) for i in range(2)],
                [
                    add_up([lax.index_in_dim(p, i, last, False) for p in second]).astype(BF16)
                    for i in range(2)
                ],
            ]
        else:
            self.held = [
                jnp.concatenate(
                    [add_up([p[j] for p in half]).astype(BF16) for half in (first, second)]
                )
                for j in range(lax.axis_size("seq"))
            ]
        self.held, value = wait_for(self.held, value)
        return value


def to_lines(x):
    return jnp.pad(x, (0, -x.shape[0] % WIDE)).reshape(-1, WIDE)


def to_block(x):
    return jnp.pad(x, ((0, 0), (0, -x.shape[1] % WIDE)))


def regroup(late_all, order, rows, hidden):
    count = late_all.shape[0]
    relative = jnp.take(late_all, order, axis=0)

    def out_rows(first):
        return late_all[:, first : first + rows].reshape(BLOCKS, HIDDEN // 2, WIDE)

    def units(first):
        return relative[:, first : first + hidden].reshape(BLOCKS, HIDDEN, WIDE)

    parts = [out_rows(0), out_rows(rows)]
    parts += [units(2 * rows + i * hidden) for i in range(2 * GROUPS)]
    return jnp.concatenate(parts, 1), jnp.arange(BLOCKS, dtype=jnp.int32)


def split_late(packs, rows, hidden):
    cuts = [0, HIDDEN // 2] + [HIDDEN * i for i in range(1, 2 * GROUPS + 2)]
    sizes = [rows, rows] + [hidden] * (2 * GROUPS)
    parts = [
        packs[:, cuts[i] : cuts[i + 1]].reshape(-1, sizes[i], WIDE) for i in range(len(sizes))
    ]
    whole = jnp.concatenate(parts, 1)
    return jnp.pad(whole, ((0, 0), (0, -whole.shape[1] % 16), (0, 0)))


def split_early(packs, small, rows):
    parts = [packs[:, 24 * i : 24 * (i + 1)].reshape(-1, rows, WIDE) for i in range(5)]
    return jnp.concatenate(parts + [small.astype(BF16)], 1)


def local(
    layer_in,
    cotangent,
    valid_len,
    sep_pos,
    w_query,
    w_key,
    w_value,
    w_depth,
    w_point,
    w_kernel,
    w_convout,
    w_output,
    gain_attn,
    shift_attn,
    w_up,
    w_down,
    gain_out,
    shift_out,
):
    seq, dp = lax.axis_size("seq"), lax.axis_size("dp")
    count = seq * dp
    z, d = lax.axis_index("seq"), lax.axis_index("dp")
    core = d & 1
    me = z * dp + d
    codes = np.array(relative_codes(), np.int32)
    order = jnp.asarray(codes) ^ me
    to_absolute = (jnp.arange(count)[:, None] == order[None, :]).astype(BF16)
    rows = w_query.shape[0]
    hidden = w_up.shape[2]
    half = count // 2
    parity = jnp.stack([z & 1])
    lines = [
        to_lines(w_kernel),
        to_lines(w_depth.reshape(-1)),
        to_lines(jnp.concatenate([gain_attn, shift_attn, gain_out, shift_out])),
    ]
    starts = np.cumsum([0] + [line.shape[0] for line in lines])
    small = pad_rows(jnp.concatenate(lines), 8)
    early, tokens_a, tokens_b = call(
        prepare_kernel,
        (
            shape((5 * rows + 8, WIDE), BF16),
            shape((HALF // 2, WIDTH), BF16),
            shape((HALF // 2, WIDTH), BF16),
        ),
        (parity, layer_in, w_query, w_key, w_value, w_point, w_convout, small),
    )
    late = pad_rows(
        jnp.concatenate(
            [
                w_output[:, :WIDE],
                w_output[:, WIDE:],
                jnp.swapaxes(w_up, 1, 2).reshape(GROUPS * hidden, WIDE),
                w_down.reshape(GROUPS * hidden, WIDE),
            ]
        ),
        16,
    )
    late_all = lax.all_gather(late, ("seq", "dp"), axis=0, tiled=False)
    parts, tokens_a, tokens_b = gather_weights(early, rows, tokens_a, tokens_b)
    token_pieces = (tokens_a, tokens_b, swap(tokens_a, "dp", 1), swap(tokens_b, "dp", 1))
    pair_info = jnp.stack([valid_len[:, 0], sep_pos[:, 0]]).astype(F32)
    place = jnp.stack([z, core, me, jnp.int32(rows)])
    offsets = np.arange(WIDTH, dtype=np.int32)
    code_rows = np.zeros((8, WIDTH), np.int32)
    code_rows[0], code_rows[1] = codes[offsets // rows], offsets % rows
    info, turned, tokens_own, matrix = call(
        permute_kernel,
        (
            shape((4,), jnp.int32),
            shape((LEN, WIDTH), BF16),
            shape((HALF, WIDTH), BF16),
            shape((WIDTH, WIDTH), BF16),
        ),
        (place, pair_info, swap(pair_info, "dp", 1)) + token_pieces + (jnp.asarray(code_rows),),
        scalars=3,
    )
    parts = parts + [swap(part, "dp", 1) for part in parts]
    own, other, small_rel, q, k, v, att, stats = call(
        attend_kernel,
        (
            shape((5 * WIDE, WIDE), BF16),
            shape((5 * WIDE, WIDE), BF16),
            shape((count * 8, WIDE), BF16),
            shape((HALF, WIDE), BF16),
            shape((LEN, WIDE), BF16),
            shape((LEN, WIDE), BF16),
            shape((HALF, WIDE), BF16),
            shape((HALF, CHUNK), F32),
        ),
        (info, turned, *parts),
    )
    att, cotangent = lax.optimization_barrier((att, cotangent[:, 0]))
    cot_a, cot_b = to_pieces(cotangent)
    small_rel = small_rel.reshape(count, -1, WIDE)
    kernel_rel = small_rel[:, starts[0] : starts[1]].reshape(count, -1)[:, : w_kernel.shape[0]]
    depth_rel = small_rel[:, starts[1] : starts[2]].reshape(count, -1)[:, : w_depth.size]
    gains_rel = small_rel[:, starts[2] : starts[3]].reshape(count, -1)[:, : 4 * rows]
    kernel_abs = jnp.dot(to_absolute, kernel_rel, preferred_element_type=F32).astype(BF16)
    taps_weight = jnp.pad(
        kernel_abs.reshape(WIDE, HEADS * KERNEL), ((0, 0), (0, CHUNK - HEADS * KERNEL))
    )
    depth_weight = jnp.pad(
        depth_rel.astype(F32).reshape(count, KERNEL, rows).transpose(1, 0, 2).reshape(KERNEL, WIDTH),
        ((0, 16 - KERNEL), (0, 0)),
    )
    gains = jnp.pad(
        jnp.dot(to_absolute, gains_rel, preferred_element_type=F32)
        .reshape(count, 4, rows)
        .transpose(1, 0, 2)
        .reshape(4, WIDTH),
        ((0, 4), (0, 0)),
    )
    context, key_conv, conv_attn, depth_low, values, spreads = call(
        conv_kernel,
        (
            shape((HALF, WIDTH), BF16),
            shape((HALF, WIDE), F32),
            shape((HALF, WIDE), BF16),
            shape((HALF, WIDTH), BF16),
            shape((WIDE // CHUNK, WINDOW, CHUNK), F32),
            shape((KERNEL, WIDE, WIDE), BF16),
        ),
        (info, turned, own, other, q, att, taps_weight, depth_weight),
        scratch=(
            pltpu.VMEM((WIDTH // CHUNK, WINDOW, CHUNK), F32),
            pltpu.VMEM((KERNEL, HALF, WIDE), F32),
            pltpu.VMEM((KERNEL, HALF, CHUNK), F32),
        ),
    )
    if count == BLOCKS:
        late_blocks, late_order = late_all, order
    else:
        late_blocks, late_order = regroup(late_all, order, rows, hidden)
    halves = (GROUPS, 2, BLOCKS // 2 * HIDDEN, WIDE)
    layer_a, layer_b, first_grad, context_grad, kept, sent, gain_grads = call(
        feed_kernel,
        (
            shape((HALF // 2, WIDTH), BF16),
            shape((HALF // 2, WIDTH), BF16),
            shape((HALF, WIDTH), F32),
            shape((HALF, WIDTH), BF16),
            shape((BLOCKS // 2, PACK, WIDE), BF16),
            shape((BLOCKS // 2, PACK, WIDE), BF16),
            shape((8, WIDTH), F32),
        ),
        (info, late_order, context, tokens_own, late_blocks, cot_a, cot_b, gains, matrix),
        scalars=2,
        scratch=(
            pltpu.VMEM((WIDTH, WIDTH), BF16),
            pltpu.VMEM(halves, BF16),
            pltpu.VMEM(halves, BF16),
            pltpu.VMEM((GROUPS, 2, HALF, WIDTH), BF16),
            pltpu.VMEM((GROUPS, 2, HALF, WIDTH), F32),
            pltpu.VMEM((HALF, WIDTH), F32),
            pltpu.VMEM((HALF, WIDTH), F32),
            pltpu.VMEM((HALF, WIDTH), BF16),
            pltpu.VMEM((HALF, WIDTH), BF16),
            pltpu.VMEM((HALF, WIDTH), BF16),
            pltpu.VMEM((HALF, WIDTH), F32),
            pltpu.VMEM((HALF, 1), F32),
        ),
    )
    if count != BLOCKS:
        kept, sent = split_late(kept, rows, hidden), split_late(sent, rows, hidden)
    first = Scatter(kept, sent, kept.shape[1] // 32 * 16)
    query_conv, key_low, kernel_grad, values_grad, rim_values = call(
        taps_back_kernel,
        (
            shape((HALF, WIDE), F32),
            shape((HALF, WIDE), BF16),
            shape((WIDE, CHUNK), F32),
            shape((WIDE // CHUNK, WINDOW, CHUNK), F32),
            shape((EDGE, WIDE), BF16),
        ),
        (info, q, context_grad, key_conv, conv_attn, values, spreads, taps_weight),
        scratch=(
            pltpu.VMEM((KERNEL, HALF, WIDE), F32),
            pltpu.VMEM((KERNEL, HALF, CHUNK), F32),
            pltpu.VMEM((KERNEL, HALF, CHUNK), F32),
            pltpu.VMEM((KERNEL, WINDOW, CHUNK), F32),
            pltpu.VMEM((KERNEL, HALF, CHUNK), BF16),
        ),
        micros=12,
    )
    key_low = first.step(key_low)
    layer_a, layer_b, key_low = lax.optimization_barrier((layer_a, layer_b, key_low))
    layer_a, layer_b = send_pieces(layer_a, layer_b, True)
    context_grad, key_low = lax.optimization_barrier((context_grad, key_low))
    rim_values = swap(rim_values, "dp", 1)
    query_attn, own_part, message = call(
        attend_back_kernel,
        (shape((HALF, WIDE), F32), shape((HALF, WIDTH), F32), shape((HALF, WIDTH), BF16)),
        (info, q, k, v, context, context_grad, stats),
        scratch=(pltpu.VMEM((LEN, WIDE), F32), pltpu.VMEM((LEN, WIDE), F32)),
        micros=13,
    )
    own_part = first.step(own_part)
    layer_a, own_part = wait_for(layer_a, own_part)
    own_part, key_low = wait_for(own_part, key_low)
    arrived = swap(message, "dp", 1)
    point_grad, depth_grad, back, rim_inputs = call(
        depth_back_kernel,
        (
            shape((WIDTH, WIDE), F32),
            shape((16, WIDTH), F32),
            shape((WIDTH // CHUNK, WINDOW, CHUNK), F32),
            shape((EDGE, WIDTH), BF16),
        ),
        (info, turned, own, other, key_low, depth_low, depth_weight),
        scratch=(
            pltpu.VMEM((WIDTH // CHUNK, WINDOW, CHUNK), F32),
        ),
        micros=5,
    )
    point_grad = first.step(point_grad)
    (layer_b, rim_values), point_grad = wait_for((layer_b, rim_values), point_grad)
    rim_inputs = swap(rim_inputs, "dp", 1)

    kernel_lines = kernel_grad[:, : HEADS * KERNEL].reshape(count, -1)
    gain_lines = gain_grads[:4].reshape(4, count, rows).transpose(1, 0, 2).reshape(count, -1)
    turned_lines = lax.dot_general(
        to_absolute,
        jnp.concatenate([to_block(kernel_lines), to_block(gain_lines)], 1).astype(BF16),
        (((0,), (0,)), ((), ())),
        preferred_element_type=F32,
    )
    cut = starts[1] * WIDE
    depth_lines = to_block(
        depth_grad[:KERNEL].reshape(KERNEL, count, rows).transpose(1, 0, 2).reshape(count, -1)
    )
    small = jnp.concatenate([turned_lines[:, :cut], depth_lines, turned_lines[:, cut:]], 1)
    small = jnp.pad(small, ((0, 0), (0, 8 * WIDE - small.shape[1]))).reshape(count, 8, WIDE)
    kept, sent, low = call(
        grads_kernel,
        (
            shape((BLOCKS // 2, 128, WIDE), BF16),
            shape((BLOCKS // 2, 128, WIDE), BF16),
            shape((4, HALF, WIDE), BF16),
        ),
        (
            info,
            turned,
            query_attn,
            query_conv,
            own_part,
            arrived,
            rim_values,
            values_grad,
            point_grad,
            small[:BLOCKS],
        ),
        scratch=(pltpu.VMEM((HALF, WIDE), F32),),
        micros=8,
    )
    if count != BLOCKS:
        kept, sent = split_early(kept, small[:half], rows), split_early(sent, small[half:], rows)
    second = Scatter(kept, sent, kept.shape[1] // 32 * 16)
    rim_inputs, low = wait_for(rim_inputs, low)
    while first.stage <= first.bits:
        low = first.step(low)
    low = second.step(low)
    x_low = call(
        inputs_kernel,
        (shape((HALF // 2, WIDTH), BF16), shape((HALF // 2, WIDTH), BF16)),
        (info, own, other, matrix, depth_weight, low, rim_inputs, back, first_grad),
        scratch=(pltpu.VMEM((HALF, WIDTH), F32),),
        micros=8,
    )
    x_low = first.step(x_low)
    x_low = second.step(x_low)
    x_a, x_b = send_pieces(*x_low, True)
    x_a = second.step(x_a)
    while second.stage <= second.bits:
        second.step(())
    second.step(())
    first, second = first.held, second.held
    piece = layer_in.shape[:1] + (1,) + layer_in.shape[2:]
    layer_out = call(place_kernel, shape(piece, BF16), (parity, layer_a, layer_b))
    x_grad = call(place_kernel, shape(piece, F32), (parity, x_a, x_b))

    def part(index):
        return second[index * rows : (index + 1) * rows]

    lines = second[5 * rows : 5 * rows + 8].reshape(-1)
    kernel_at, depth_at, gain_at = (start * WIDE for start in starts[:3])
    depth_line = lines[depth_at : depth_at + w_depth.size].reshape(KERNEL, rows)
    gain_line = lines[gain_at : gain_at + 4 * rows].reshape(4, rows)
    return (
        layer_out,
        x_grad,
        part(0),
        part(1),
        part(2),
        depth_line,
        part(3),
        lines[kernel_at : kernel_at + w_kernel.shape[0]],
        part(4),
        jnp.concatenate([first[:rows], first[rows : 2 * rows]], 1),
        gain_line[0],
        gain_line[1],
        jnp.swapaxes(
            first[2 * rows : 2 * rows + GROUPS * hidden].reshape(GROUPS, hidden, WIDE), 1, 2
        ),
        first[2 * rows + GROUPS * hidden : 2 * rows + 2 * GROUPS * hidden].reshape(
            GROUPS, hidden, WIDE
        ),
        gain_line[2],
        gain_line[3],
    )


def solution(mesh):
    in_specs = (
        P(None, "dp", "seq", None),
        P(None, "dp", "seq", None),
        P(None, "dp"),
        P(None, "dp"),
        P(("seq", "dp"), None),
        P(("seq", "dp"), None),
        P(("seq", "dp"), None),
        P(None, ("seq", "dp")),
        P(("seq", "dp"), None),
        P(("seq", "dp")),
        P(("seq", "dp"), None),
        P(("seq", "dp"), None),
        P(("seq", "dp")),
        P(("seq", "dp")),
        P(None, None, ("seq", "dp")),
        P(None, ("seq", "dp"), None),
        P(("seq", "dp")),
        P(("seq", "dp")),
    )
    out_specs = (
        P(None, "dp", "seq", None),
        P(None, "dp", "seq", None),
        P(("seq", "dp"), None),
        P(("seq", "dp"), None),
        P(("seq", "dp"), None),
        P(None, ("seq", "dp")),
        P(("seq", "dp"), None),
        P(("seq", "dp")),
        P(("seq", "dp"), None),
        P(("seq", "dp"), None),
        P(("seq", "dp")),
        P(("seq", "dp")),
        P(None, None, ("seq", "dp")),
        P(None, ("seq", "dp"), None),
        P(("seq", "dp")),
        P(("seq", "dp")),
    )
    return jax.shard_map(local, mesh=mesh, in_specs=in_specs, out_specs=out_specs, check_vma=False)
```

```python
import functools

import jax
import jax.numpy as jnp
import numpy as np
from jax import lax
from jax.experimental import pallas as pl
from jax.experimental.pallas import tpu as pltpu
from jax.sharding import PartitionSpec as P

HEADS = 6
HEAD_DIM = 64
KERNEL = 9
GROUPS = 2
LEN = 1024
HALF = LEN // 2
WIDTH = 768
WIDE = HEADS * HEAD_DIM
CHUNK = 128
EDGE = 16
WINDOW = HALF + 2 * EDGE
BLOCKS = 32
HIDDEN = 48
PACK = 240
COST = 10**8

F32 = jnp.float32
BF16 = jnp.bfloat16

inv_root_two = 0.7071067811865476
inv_root_tau = 0.3989422804014327


def nn(a, b):
    return jnp.dot(a, b, preferred_element_type=F32)


def nt(a, b):
    return lax.dot_general(a, b, (((1,), (1,)), ((), ())), preferred_element_type=F32)


def tn(a, b):
    return lax.dot_general(a, b, (((0,), (0,)), ((), ())), preferred_element_type=F32)


def call(kernel, out_shape, args, scalars=1, scratch=(), micros=0):
    vmem = pl.BlockSpec(memory_space=pltpu.VMEM)
    smem = pl.BlockSpec(memory_space=pltpu.SMEM)
    return pl.pallas_call(
        kernel,
        out_shape=out_shape,
        in_specs=[smem] * scalars
        + [vmem] * (len(args) - scalars),
        out_specs=jax.tree.map(
            lambda s: smem if s.dtype == jnp.int32 else vmem, out_shape
        ),
        scratch_shapes=list(scratch),
        compiler_params=pltpu.CompilerParams(vmem_limit_bytes=56 * 1024 * 1024),
        cost_estimate=pl.CostEstimate(flops=micros * COST, bytes_accessed=0, transcendentals=0),
    )(*args)


def shape(dims, dtype):
    return jax.ShapeDtypeStruct(dims, dtype)


def lane(rows):
    return lax.broadcasted_iota(jnp.int32, (rows, CHUNK), 1)


def load_window(core, source, target, chunks):
    value = source(pl.ds(pl.multiple_of(core * (HALF - EDGE), EDGE), HALF + EDGE))
    start = pl.multiple_of(EDGE - core * EDGE, EDGE)
    edge = pl.multiple_of(core * (HALF + EDGE), EDGE)
    for c in range(chunks):
        target[c, pl.ds(edge, EDGE), :] = jnp.zeros((EDGE, CHUNK), F32)
        target[c, pl.ds(start, HALF + EDGE), :] = value[:, c * CHUNK : (c + 1) * CHUNK].astype(F32)


def weight(own, other, index):
    rows = slice(index * WIDE, (index + 1) * WIDE)
    return own[rows, :], other[rows, :]


def project(tokens, own, other, index):
    first, second = weight(own, other, index)
    return nn(tokens[:, :WIDE], first) + nn(tokens[:, WIDE:], second)


def fill_masks(info, masks):
    sep, valid, core = info[1], info[0], info[2]

    def segment(position):
        return jnp.where(position < sep, 0, jnp.where(position < valid, 1, 2))

    row = core * HALF + lax.broadcasted_iota(jnp.int32, (HALF, CHUNK), 0)
    own = segment(row)
    for j in range(KERNEL):
        masks[j] = (segment(row + (j - 4)) == own).astype(F32)


def prepare_kernel(info, tokens, *refs):
    weights, small, early, token_a, token_b = refs[:5], refs[5], refs[6], refs[7], refs[8]
    rows = weights[0].shape[0]
    odd = info[0]
    token_a[...] = tokens[pl.ds(odd, 1), 0][0]
    token_b[...] = tokens[pl.ds(1 - odd, 1), 0][0]
    pieces = [ref[...].astype(F32) for ref in weights] + [small[...].astype(F32)]
    for i in range(3):
        pair = jnp.concatenate(pieces[2 * i : 2 * i + 2], 0)
        early[2 * i * rows : 2 * i * rows + pair.shape[0], :] = pair.astype(BF16)


def permute_kernel(
    place, mine, theirs, own_a, own_b, other_a, other_b, codes, info, out, own_out, matrix
):
    z, core, me, rows = place[0], place[1], place[2], place[3]
    high = z >> 1
    for i in range(2):
        own_value = jnp.where(high == 0, mine[i, 0], mine[i, 1])
        other_value = jnp.where(high == 0, theirs[i, 0], theirs[i, 1])
        info[i] = jnp.where((z & 1) == core, own_value, other_value).astype(jnp.int32)
    info[2] = core
    info[3] = high
    features = (codes[0:1, :] ^ me) * rows + codes[1:2, :]
    matrix[...] = (
        (lax.broadcasted_iota(jnp.int32, (WIDTH, WIDTH), 0) == features)
        .astype(F32)
        .astype(BF16)
    )
    quarter = HALF // 2
    for side, pieces in ((core, (own_a, own_b)), (1 - core, (other_a, other_b))):
        for place, piece in zip((high, 1 - high), pieces):
            at = pl.multiple_of(side * HALF + place * quarter, quarter)
            out[pl.ds(at, quarter), :] = nn(piece[...], matrix[...]).astype(BF16)
    own_out[pl.ds(pl.multiple_of(high * quarter, quarter), quarter), :] = own_a[...]
    own_out[pl.ds(pl.multiple_of((1 - high) * quarter, quarter), quarter), :] = own_b[...]


def attend_kernel(info, tokens, *refs):
    parts, refs = refs[:-8], refs[-8:]
    own, other, small_out, q_out, k_out, v_out, att_out, stat_out = refs
    core, valid = info[2], info[0]
    count = len(parts) // 2
    unit = WIDE // count
    rest = parts[0].shape[0] - 5 * unit
    for h, target in enumerate((own, other)):
        for i in range(count):
            part = parts[h * count + i]
            for w in range(5):
                target[w * WIDE + i * unit : w * WIDE + (i + 1) * unit, :] = part[
                    w * unit : (w + 1) * unit, :
                ]
            first = (h * count + i) * rest
            small_out[first : first + rest, :] = part[5 * unit :, :]
    mine = tokens[pl.ds(pl.multiple_of(core * HALF, HALF), HALF), :]
    q_out[...] = project(mine, own, other, 0).astype(BF16)
    k_out[...] = project(tokens[...], own, other, 1).astype(BF16)
    v_out[...] = project(tokens[...], own, other, 2).astype(BF16)
    rows = 256
    bias = jnp.where(
        lax.broadcasted_iota(jnp.int32, (1, LEN), 1) < valid, 0.0, -1e30
    ).astype(F32)
    for block in range(HALF // rows):
        at = slice(block * rows, (block + 1) * rows)
        stats = jnp.zeros((rows, CHUNK), F32)
        for pair in range(HEADS // 2):
            cols = slice(pair * CHUNK, (pair + 1) * CHUNK)
            q = q_out[at, cols] * BF16(0.125)
            k, v = k_out[:, cols], v_out[:, cols]
            results = []
            for head in range(2):
                keep = (lane(rows) < HEAD_DIM) == (head == 0)
                scores = nt(jnp.where(keep, q, BF16(0)), k) + bias
                peak = jnp.max(scores, -1, keepdims=True)
                exponent = jnp.exp(scores - peak)
                total = jnp.sum(exponent, -1, keepdims=True)
                results.append(nn(exponent.astype(BF16), v) / total)
                stats = jnp.where(
                    lane(rows) == 2 * pair + head, peak + jnp.log(total), stats
                )
            att_out[at, cols] = jnp.where(lane(rows) < HEAD_DIM, *results).astype(BF16)
        stat_out[at, :] = stats


def spread(j):
    row = lax.broadcasted_iota(jnp.int32, (CHUNK, WIDE), 0)
    col = lax.broadcasted_iota(jnp.int32, (CHUNK, WIDE), 1)
    return (row == (col >> 6) * KERNEL + j).astype(F32).astype(BF16)


def conv_kernel(
    info,
    tokens,
    own,
    other,
    q,
    att,
    taps_weight,
    depth_weight,
    context,
    key_out,
    attn_out,
    depth_out,
    values_out,
    window,
    logits,
    masks,
):
    core = info[2]
    load_window(core, lambda rows: tokens[rows, :], window, WIDTH // CHUNK)
    fill_masks(info, masks)
    rows = 64
    for c in range(WIDTH // CHUNK):
        cols = slice(c * CHUNK, (c + 1) * CHUNK)
        for b in range(HALF // rows):
            total = jnp.zeros((rows, CHUNK), F32)
            for j in range(KERNEL):
                first = EDGE - 4 + b * rows + j
                total = total + depth_weight[j : j + 1, cols] * window[c, first : first + rows, :]
            depth_out[b * rows : (b + 1) * rows, cols] = total.astype(BF16)
    key_conv = project(depth_out[...], own, other, 3)
    key_out[...] = key_conv
    attn_out[...] = (key_conv * q[...].astype(F32)).astype(BF16)
    load_window(
        core, lambda rows: project(tokens[rows, :], own, other, 4), values_out, WIDE // CHUNK
    )
    for j in range(KERNEL):
        logits[j] = nn(attn_out[...], nn(taps_weight[...], spread(j)).astype(BF16))
    context[:, :WIDE] = att[...]
    for b in range(HALF // rows):
        at = slice(b * rows, (b + 1) * rows)
        for c in range(WIDE // CHUNK):
            cols = slice(c * CHUNK, (c + 1) * CHUNK)
            peak = logits[0, at, cols]
            for j in range(1, KERNEL):
                peak = jnp.maximum(peak, logits[j, at, cols])
            total = jnp.zeros((rows, CHUNK), F32)
            result = jnp.zeros((rows, CHUNK), F32)
            for j in range(KERNEL):
                first = EDGE - 4 + b * rows + j
                exponent = jnp.exp(logits[j, at, cols] - peak)
                total = total + exponent
                result = result + exponent * masks[j, at, :] * values_out[
                    c, first : first + rows, :
                ]
            context[at, WIDE + c * CHUNK : WIDE + (c + 1) * CHUNK] = (result / total).astype(BF16)


def normalize(value):
    centred = value - jnp.mean(value, -1, keepdims=True)
    inv = lax.rsqrt(jnp.mean(centred * centred, -1, keepdims=True) + 1e-06)
    return centred * inv, inv


def normalize_back(grad, normed, inv, gain):
    e = grad * gain
    return inv * (
        e - jnp.mean(e, -1, keepdims=True) - normed * jnp.mean(e * normed, -1, keepdims=True)
    )


def piece_rows(info, step, rows):
    half = info[3] if step < 2 else 1 - info[3]
    return pl.ds(pl.multiple_of(half * (HALF // 2) + step % 2 * rows, rows), rows)


def sum_kernel(cut, kept, arrived, first_0, first_1, second_0, second_1):
    count = kept.shape[0] // 4
    for i in range(kept.shape[0]):
        total = kept[i].astype(F32) + arrived[i].astype(F32)
        high, low = i // (2 * count), i // count % 2
        (first_0, first_1)[high][i % (2 * count)] = total[:cut].astype(BF16)
        (second_0, second_1)[low][high * count + i % count] = total[cut:].astype(BF16)


def place_kernel(info, first, second, out):
    odd = info[0]
    out[pl.ds(odd, 1), 0] = first[...].astype(out.dtype)[None]
    out[pl.ds(1 - odd, 1), 0] = second[...].astype(out.dtype)[None]


def feed_kernel(
    info,
    order,
    context,
    tokens,
    late,
    cot_a,
    cot_b,
    gains,
    matrix,
    layer_a,
    layer_b,
    first_out,
    context_grad,
    kept,
    sent,
    small_out,
    out_weight,
    up,
    down,
    act,
    slope,
    normed,
    attn,
    attn_low,
    grad_low,
    branch_low,
    second,
    scale,
):
    rows = 128
    steps = [slice(i * rows, (i + 1) * rows) for i in range(HALF // rows)]
    gain_attn, shift_attn = gains[0:1, :], gains[1:2, :]
    gain_out, shift_out = gains[2:3, :], gains[3:4, :]
    for i in range(BLOCKS // 2):
        sides = [late[2 * i + k, 0:HIDDEN, :].astype(F32) for k in range(2)]
        out_weight[i * HIDDEN : (i + 1) * HIDDEN, :] = jnp.concatenate(
            [jnp.concatenate([s[: HIDDEN // 2], s[HIDDEN // 2 :]], 1) for s in sides], 0
        ).astype(BF16)
    for h in range(2):
        for i in range(BLOCKS // 2):
            source = order[h * (BLOCKS // 2) + i]
            for g in range(GROUPS):
                at = slice(i * HIDDEN, (i + 1) * HIDDEN)
                up[g, h, at, :] = late[source, (1 + g) * HIDDEN : (2 + g) * HIDDEN, :]
                down[g, h, at, :] = late[source, (3 + g) * HIDDEN : (4 + g) * HIDDEN, :]
    for at in steps:
        branch = nn(context[at, :], out_weight[...]) + tokens[at, :].astype(F32)
        n, inv = normalize(branch)
        normed[at, :] = n
        scale[at, :] = inv
        value = n * gain_attn + shift_attn
        attn[at, :] = value
        attn_low[at, :] = value.astype(BF16)
    for g in range(GROUPS):
        part = slice(g * WIDE, (g + 1) * WIDE)
        for h in range(2):
            for at in steps:
                pre = nt(attn_low[at, part], up[g, h])
                cdf = 0.5 * (1.0 + lax.erf(pre * inv_root_two))
                act[g, h, at, :] = (pre * cdf).astype(BF16)
                slope[g, h, at, :] = cdf + pre * jnp.exp(-0.5 * pre * pre) * inv_root_tau
    gain_grad = jnp.zeros((1, WIDTH), F32)
    shift_grad = jnp.zeros((1, WIDTH), F32)
    for step in range(HALF // rows):
        piece, inner = step // 2, slice(step % 2 * rows, (step % 2 + 1) * rows)
        at = piece_rows(info, step, rows)
        value = attn[at, :] + jnp.concatenate(
            [
                nn(act[g, 0, at, :], down[g, 0]) + nn(act[g, 1, at, :], down[g, 1])
                for g in range(GROUPS)
            ],
            1,
        )
        n, inv = normalize(value)
        (layer_a, layer_b)[piece][inner, :] = (n * gain_out + shift_out).astype(BF16)
        grad = (cot_a, cot_b)[piece][inner, :].astype(F32)
        gain_grad = gain_grad + jnp.sum(grad * n, 0, keepdims=True)
        shift_grad = shift_grad + jnp.sum(grad, 0, keepdims=True)
        value = normalize_back(grad, n, inv, gain_out)
        second[at, :] = value
        grad_low[at, :] = value.astype(BF16)
    small_out[2:3, :] = gain_grad
    small_out[3:4, :] = shift_grad
    for g in range(GROUPS):
        part = slice(g * WIDE, (g + 1) * WIDE)
        for h in range(2):
            target = (kept, sent)[h]
            result = tn(act[g, h], grad_low[:, part]).astype(BF16)
            for i in range(BLOCKS // 2):
                target[i, (3 + g) * HIDDEN : (4 + g) * HIDDEN, :] = result[
                    i * HIDDEN : (i + 1) * HIDDEN
                ]
            for at in steps:
                act[g, h, at, :] = (
                    nt(grad_low[at, part], down[g, h]) * slope[g, h, at, :]
                ).astype(BF16)
            result = tn(act[g, h], attn_low[:, part]).astype(BF16)
            for i in range(BLOCKS // 2):
                target[i, (1 + g) * HIDDEN : (2 + g) * HIDDEN, :] = result[
                    i * HIDDEN : (i + 1) * HIDDEN
                ]
    gain_grad = jnp.zeros((1, WIDTH), F32)
    shift_grad = jnp.zeros((1, WIDTH), F32)
    for at in steps:
        grad = second[at, :] + jnp.concatenate(
            [nn(act[g, 0, at, :], up[g, 0]) + nn(act[g, 1, at, :], up[g, 1]) for g in range(GROUPS)],
            1,
        )
        n = normed[at, :]
        gain_grad = gain_grad + jnp.sum(grad * n, 0, keepdims=True)
        shift_grad = shift_grad + jnp.sum(grad, 0, keepdims=True)
        value = normalize_back(grad, n, scale[at, :], gain_attn)
        first_out[at, :] = value
        branch_low[at, :] = value.astype(BF16)
        context_grad[at, :] = nt(branch_low[at, :], out_weight[...]).astype(BF16)
        grad_low[at, :] = nn(context[at, :], matrix[...]).astype(BF16)
    small_out[0:1, :] = gain_grad
    small_out[1:2, :] = shift_grad
    small_out[4:8, :] = jnp.zeros((4, WIDTH), F32)
    for h in range(2):
        result = tn(grad_low[:, h * WIDE : (h + 1) * WIDE], branch_low[...])
        for i in range(BLOCKS // 2):
            piece = result[i * (HIDDEN // 2) : (i + 1) * (HIDDEN // 2)]
            (kept, sent)[h][i, 0:HIDDEN, :] = jnp.concatenate(
                [piece[:, :WIDE], piece[:, WIDE:]], 0
            ).astype(BF16)


def shifted_sum(source, step, scale=None):
    total = jnp.zeros((32, CHUNK), F32)
    for j in range(KERNEL):
        first = step + 4 - j
        low, high = max(first, 0), min(first + 32, WINDOW)
        piece = source(j)[low:high, :]
        if high - low < 32:
            zero = jnp.zeros((32 - (high - low), CHUNK), F32)
            piece = jnp.concatenate([zero, piece] if low > first else [piece, zero], 0)
        total = total + (piece if scale is None else scale(j) * piece)
    return total


def taps_back_kernel(
    info,
    q,
    context_grad,
    key_conv,
    conv_attn,
    values,
    taps_weight,
    query_out,
    key_low,
    kernel_out,
    values_grad,
    rim_out,
    logits,
    masks,
    sums,
    pads,
    compact,
):
    core = info[2]
    fill_masks(info, masks)
    rows = 64
    steps = [slice(i * rows, (i + 1) * rows) for i in range(HALF // rows)]
    block = (lax.broadcasted_iota(jnp.int32, (CHUNK, CHUNK), 0) >> 6) == (
        lax.broadcasted_iota(jnp.int32, (CHUNK, CHUNK), 1) >> 6
    )
    ones = block.astype(F32).astype(BF16)
    pick_row = lax.broadcasted_iota(jnp.int32, (CHUNK, CHUNK), 0)
    pick_col = lax.broadcasted_iota(jnp.int32, (CHUNK, CHUNK), 1)
    for j in range(KERNEL):
        logits[j] = nn(conv_attn[...], nn(taps_weight[...], spread(j)).astype(BF16))
        pads[j, 0:EDGE, :] = jnp.zeros((EDGE, CHUNK), F32)
        pads[j, HALF + EDGE : WINDOW, :] = jnp.zeros((EDGE, CHUNK), F32)
    total_compact = jnp.zeros((HALF, CHUNK), F32)
    for c in range(WIDE // CHUNK):
        cols = slice(c * CHUNK, (c + 1) * CHUNK)
        grad_cols = slice(WIDE + c * CHUNK, WIDE + (c + 1) * CHUNK)
        for j in range(KERNEL):
            product = (
                context_grad[:, grad_cols].astype(F32)
                * values[c, EDGE - 4 + j : EDGE - 4 + j + HALF, :]
            )
            sums[j] = nn(product.astype(BF16), ones)
        for b, at in enumerate(steps):
            grad = context_grad[at, grad_cols].astype(F32)
            peak = logits[0, at, cols]
            for j in range(1, KERNEL):
                peak = jnp.maximum(peak, logits[j, at, cols])
            total = jnp.zeros((rows, CHUNK), F32)
            dot = jnp.zeros((rows, CHUNK), F32)
            for j in range(KERNEL):
                exponent = jnp.exp(logits[j, at, cols] - peak)
                mask = masks[j, at, :]
                logits[j, at, cols] = exponent
                change = sums[j, at, :] * mask
                sums[j, at, :] = change
                total = total + exponent
                dot = dot + exponent * change
            inv = 1.0 / total
            dot = dot * inv
            inside = slice(EDGE + b * rows, EDGE + (b + 1) * rows)
            for j in range(KERNEL):
                tap = logits[j, at, cols] * inv
                pads[j, inside, :] = tap * masks[j, at, :] * grad
                compact[j, at, :] = (tap * (sums[j, at, :] - dot)).astype(BF16)
        for j in range(KERNEL):
            pick = (pick_row & 63 == 0) & (pick_col == (2 * c + (pick_row >> 6)) * KERNEL + j)
            total_compact = total_compact + nn(compact[j], pick.astype(F32).astype(BF16))
        for b in range(WINDOW // 32):
            values_grad[c, b * 32 : (b + 1) * 32, :] = shifted_sum(lambda j: pads.at[j], b * 32)
    compact_low = total_compact.astype(BF16)
    kernel_out[...] = tn(conv_attn[...], compact_low)
    attn_grad = nt(compact_low, taps_weight[...])
    query_out[...] = attn_grad * key_conv[...]
    key_low[...] = (attn_grad * q[...].astype(F32)).astype(BF16)
    rim = pl.multiple_of((1 - core) * (HALF + EDGE), EDGE)
    for c in range(WIDE // CHUNK):
        rim_out[:, c * CHUNK : (c + 1) * CHUNK] = values_grad[c, pl.ds(rim, EDGE), :].astype(BF16)


def depth_back_kernel(
    info,
    tokens,
    own,
    other,
    key_low,
    depth_low,
    depth_weight,
    point_out,
    depth_grad,
    back_out,
    rim_out,
    window,
):
    core = info[2]
    load_window(core, lambda rows: tokens[rows, :], window, WIDTH // CHUNK)
    point_out[...] = tn(depth_low[...], key_low[...]).astype(BF16)
    depth_grad[...] = jnp.zeros((16, WIDTH), F32)
    for side, rows_weight in enumerate(weight(own, other, 3)):
        back = nt(key_low[...], rows_weight)
        for k in range(WIDE // CHUNK):
            c = side * (WIDE // CHUNK) + k
            back_out[c, 0:EDGE, :] = jnp.zeros((EDGE, CHUNK), F32)
            back_out[c, HALF + EDGE : WINDOW, :] = jnp.zeros((EDGE, CHUNK), F32)
            back_out[c, EDGE : HALF + EDGE, :] = back[:, k * CHUNK : (k + 1) * CHUNK]
    for c in range(WIDTH // CHUNK):
        cols = slice(c * CHUNK, (c + 1) * CHUNK)
        totals = [jnp.zeros((8, CHUNK), F32) for _ in range(KERNEL)]
        for b in range(HALF // 32):
            grad = back_out[c, EDGE + b * 32 : EDGE + (b + 1) * 32, :]
            for j in range(KERNEL):
                first = EDGE - 4 + b * 32 + j
                product = grad * window[c, first : first + 32, :]
                totals[j] = totals[j] + (
                    (product[0:8] + product[8:16]) + (product[16:24] + product[24:32])
                )
        for j in range(KERNEL):
            depth_grad[j : j + 1, cols] = jnp.sum(totals[j], 0, keepdims=True)
        low, high = (
            shifted_sum(lambda j: back_out.at[c], step, lambda j: depth_weight[j : j + 1, cols])
            for step in (0, WINDOW - 32)
        )
        turned = (c + WIDE // CHUNK) % (WIDTH // CHUNK)
        rim_out[:, turned * CHUNK : (turned + 1) * CHUNK] = jnp.where(
            core == 0, high[32 - EDGE :], low[:EDGE]
        ).astype(BF16)


def attend_back_kernel(
    info, q, k, v, context, context_grad, stats, query_out, own_out, message, key_sum, value_sum
):
    core, valid = info[2], info[0]
    rows = 256
    live = lax.broadcasted_iota(jnp.int32, (LEN, CHUNK), 0) < valid
    for pair in range(HEADS // 2):
        cols = slice(pair * CHUNK, (pair + 1) * CHUNK)
        keys, vals = k[:, cols], v[:, cols]
        for head in range(2):
            even = head == 0
            base = HEAD_DIM if even else 0
            key_lane = lane(LEN)
            keep_key = (key_lane < HEAD_DIM) == even
            keys_more = jnp.where(
                keep_key,
                keys.astype(F32),
                jnp.where(
                    key_lane == base,
                    jnp.where(live, 0.0, -1e30),
                    jnp.where(key_lane < base + 4, 1.0, 0.0),
                ),
            ).astype(BF16)
            vals_more = jnp.where(
                keep_key, vals.astype(F32), jnp.where(key_lane < base + 3, 1.0, 0.0)
            ).astype(BF16)
            keys_turned = keys_more.T
            for block in range(HALF // rows):
                at = slice(block * rows, (block + 1) * rows)
                here = lane(rows)
                keep = (here < HEAD_DIM) == even

                def three(value):
                    high = value.astype(BF16).astype(F32)
                    middle = (value - high).astype(BF16).astype(F32)
                    return high, middle, value - high - middle

                grad = context_grad[at, cols].astype(F32)
                product = jnp.where(keep, grad * context[at, cols].astype(F32), 0.0)
                dots = three(-jnp.sum(product, -1, keepdims=True))
                stat = three(-stats[at, 2 * pair + head : 2 * pair + head + 1])
                grad_more = jnp.where(
                    keep,
                    grad,
                    jnp.where(
                        here == base,
                        dots[0],
                        jnp.where(
                            here == base + 1, dots[1], jnp.where(here == base + 2, dots[2], 0.0)
                        ),
                    ),
                ).astype(BF16)
                query_more = jnp.where(
                    keep,
                    q[at, cols].astype(F32) * 0.125,
                    jnp.where(
                        here == base,
                        1.0,
                        jnp.where(
                            here == base + 1,
                            stat[0],
                            jnp.where(
                                here == base + 2, stat[1], jnp.where(here == base + 3, stat[2], 0.0)
                            ),
                        ),
                    ),
                ).astype(BF16)
                probs = jnp.exp(nt(keys_more, query_more))
                change = (probs * nt(vals_more, grad_more)).astype(BF16)
                value_part = nn(probs.astype(BF16), grad_more)
                key_part = nn(change, query_more)
                query_part = nn(keys_turned, change).T * 0.125
                if block == 0:
                    value_total, key_total = value_part, key_part
                else:
                    value_total, key_total = value_total + value_part, key_total + key_part
                if even:
                    query_out[at, cols] = query_part
                else:
                    query_out[at, cols] = jnp.where(keep, query_part, query_out[at, cols])
            if even:
                key_sum[:, cols] = key_total
                value_sum[:, cols] = value_total
            else:
                key_sum[:, cols] = jnp.where(keep_key, key_total, key_sum[:, cols])
                value_sum[:, cols] = jnp.where(keep_key, value_total, value_sum[:, cols])
    mine = pl.ds(pl.multiple_of(core * HALF, HALF), HALF)
    theirs = pl.ds(pl.multiple_of((1 - core) * HALF, HALF), HALF)
    own_out[:, :WIDE] = key_sum[mine, :]
    own_out[:, WIDE:] = value_sum[mine, :]
    message[:, :WIDE] = key_sum[theirs, :].astype(BF16)
    message[:, WIDE:] = value_sum[theirs, :].astype(BF16)


def grads_kernel(
    info,
    tokens,
    query_attn,
    query_conv,
    own_part,
    arrived,
    rim_values,
    values_grad,
    point_grad,
    small,
    kept,
    sent,
    low_out,
    values_sum,
):
    core = info[2]
    rim = pl.ds(pl.multiple_of((1 - core) * (HALF - EDGE), EDGE), EDGE)
    for c in range(WIDE // CHUNK):
        cols = slice(c * CHUNK, (c + 1) * CHUNK)
        values_sum[:, cols] = values_grad[c, EDGE : EDGE + HALF, :]
    values_sum[rim, :] = values_sum[rim, :] + rim_values[...].astype(F32)
    both = own_part[...] + arrived[...].astype(F32)
    low_out[0] = (query_attn[...] + query_conv[...]).astype(BF16)
    low_out[1] = both[:, :WIDE].astype(BF16)
    low_out[2] = both[:, WIDE:].astype(BF16)
    low_out[3] = values_sum[...].astype(BF16)
    mine = pl.ds(pl.multiple_of(core * HALF, HALF), HALF)
    unit = HIDDEN // 2
    for h in range(2):
        part = tokens[mine, h * WIDE : (h + 1) * WIDE]
        results = [tn(part, low_out[n]) for n in range(4)]
        point = point_grad[h * WIDE : (h + 1) * WIDE, :].astype(F32)
        target = (kept, sent)[h]
        for i in range(BLOCKS // 2):
            at = slice(i * unit, (i + 1) * unit)
            target[i, 0:48, :] = jnp.concatenate([results[0][at], results[1][at]], 0).astype(BF16)
            target[i, 48:96, :] = jnp.concatenate([results[2][at], point[at]], 0).astype(BF16)
            target[i, 96:128, :] = jnp.concatenate(
                [results[3][at], small[h * (BLOCKS // 2) + i]], 0
            ).astype(BF16)


def inputs_kernel(
    info,
    own,
    other,
    matrix,
    depth_weight,
    low,
    rim_inputs,
    back,
    first_grad,
    x_a,
    x_b,
    inputs,
):
    core = info[2]
    rim = pl.ds(pl.multiple_of((1 - core) * (HALF - EDGE), EDGE), EDGE)
    for c in range(WIDTH // CHUNK):
        cols = slice(c * CHUNK, (c + 1) * CHUNK)
        for b in range(HALF // 32):
            inputs[b * 32 : (b + 1) * 32, cols] = shifted_sum(
                lambda j: back.at[c], EDGE + b * 32, lambda j: depth_weight[j : j + 1, cols]
            )
    inputs[rim, :] = inputs[rim, :] + rim_inputs[...].astype(F32)
    for h in range(2):
        rows = (own, other)[h]
        total = inputs[:, h * WIDE : (h + 1) * WIDE]
        for n, index in enumerate((0, 1, 2, 4)):
            total = total + nt(low[n], rows[index * WIDE : (index + 1) * WIDE, :])
        inputs[:, h * WIDE : (h + 1) * WIDE] = total
    for step in range(4):
        at = piece_rows(info, step, CHUNK)
        value = nt(inputs[at, :].astype(BF16), matrix[...]) + first_grad[at, :]
        inner = slice(step % 2 * CHUNK, (step % 2 + 1) * CHUNK)
        (x_a, x_b)[step // 2][inner, :] = value.astype(BF16)


def dp_groups(count):
    masks = []
    bit = 2
    while bit < count:
        if bit * 2 < count:
            masks.append((bit, 2 * bit, 3 * bit))
            bit *= 4
        else:
            masks.append((bit,))
            bit *= 2
    return masks


def swap(x, axis, mask):
    count = lax.axis_size(axis)
    return lax.ppermute(x, axis, [(i, i ^ mask) for i in range(count)])


def relative_codes():
    seq, dp = lax.axis_size("seq"), lax.axis_size("dp")
    codes = [j * dp for j in range(seq)]
    for masks in dp_groups(dp):
        codes = [c ^ m for m in (0,) + masks for c in codes]
    return codes + [c ^ 1 for c in codes]


def add_up(parts):
    total = parts[0].astype(jnp.float32)
    for part in parts[1:]:
        total = total + part.astype(jnp.float32)
    return total


def token_perms():
    seq, dp = lax.axis_size("seq"), lax.axis_size("dp")
    first, second = [], []
    for z in range(seq):
        for d in range(dp):
            core, rest = d & 1, d & ~1
            odd = z & 1
            first.append((z * dp + d, (2 * odd + core) * dp + rest + (z >> 1)))
            second.append((z * dp + d, (2 * (1 - odd) + core) * dp + rest + (z >> 1)))
    return first, second


def pad_rows(x, multiple):
    return jnp.pad(x, ((0, -x.shape[0] % multiple), (0, 0)))


def merge(packs, rows):
    cut = packs[0].shape[0] // (5 * rows + 8) * (5 * rows)
    weights = jnp.concatenate([p[:cut].reshape(5, -1, WIDE) for p in packs], 1)
    return jnp.concatenate([weights.reshape(-1, WIDE)] + [p[cut:] for p in packs])


def gather_weights(pack, rows, *tokens):
    held = merge([pack] + [swap(pack, "seq", j) for j in range(1, lax.axis_size("seq"))], rows)
    tokens = send_pieces(*tokens)
    groups = dp_groups(lax.axis_size("dp"))
    for masks in groups[:-1]:
        held = merge([held] + [swap(held, "dp", m) for m in masks], rows)
    return [held] + [swap(held, "dp", m) for m in groups[-1]], *tokens


def send_pieces(a, b, back=False):
    first, second = token_perms()
    if back:
        first, second = ([(t, s) for s, t in perm] for perm in (first, second))
    return lax.ppermute(a, ("seq", "dp"), first), lax.ppermute(b, ("seq", "dp"), second)


def to_pieces(x):
    odd = lax.axis_index("seq") & 1
    a, b = (lax.dynamic_index_in_dim(x, index, 0, False) for index in (odd, 1 - odd))
    return send_pieces(a, b)


def wait_for(arrays, value):
    return lax.optimization_barrier((arrays, value))


class Scatter:
    def __init__(self, kept, sent, cut):
        self.bits = lax.axis_size("dp").bit_length() - 2
        self.stage = 0
        self.cut = cut
        self.held = kept, sent

    def pieces(self, whole, rows):
        dims = (2,) * self.bits + (-1,) + whole[0].shape[1:]
        return [part.reshape(dims)[..., rows, :] for part in whole]

    def step(self, value):
        if self.stage == 0:
            kept, sent = self.held
            arrived, value = wait_for(swap(sent, "dp", 1), value)
            if self.bits == 2:
                self.stage = 1
                size, rows, wide = kept.shape
                halves = [
                    shape((size // 2, n, wide), BF16) for n in (self.cut, rows - self.cut)
                ]
                sums = call(
                    functools.partial(sum_kernel, self.cut),
                    (halves[0], halves[0], halves[1], halves[1]),
                    (kept, arrived),
                    scalars=0,
                )
                split = (2, -1)
                self.held = [
                    [s.reshape(split + s.shape[1:]) for s in sums[:2]],
                    [s.reshape(split + s.shape[1:]) for s in sums[2:]],
                ]
                self.held, value = wait_for(self.held, value)
                return value
            first = self.pieces((kept, arrived), slice(0, self.cut))
            second = self.pieces((kept, arrived), slice(self.cut, None))
        elif self.stage <= self.bits:
            first, second = self.held
            arrived, value = wait_for(
                (
                    swap(first[1], "dp", 1 << (self.bits + 1 - self.stage)),
                    swap(second[1], "dp", 1 << self.stage),
                ),
                value,
            )
            first, second = [first[0], arrived[0]], [second[0], arrived[1]]
        else:
            arrived, value = wait_for(
                [swap(part, "seq", j + 1) for j, part in enumerate(self.held[1:])], value
            )
            self.held = add_up([self.held[0]] + arrived)
            return value
        self.stage += 1
        if self.stage <= self.bits:
            last = self.bits - self.stage
            self.held = [
                [add_up([p[i] for p in first]).astype(BF16) for i in range(2)],
                [
                    add_up([lax.index_in_dim(p, i, last, False) for p in second]).astype(BF16)
                    for i in range(2)
                ],
            ]
        else:
            self.held = [
                jnp.concatenate(
                    [add_up([p[j] for p in half]).astype(BF16) for half in (first, second)]
                )
                for j in range(lax.axis_size("seq"))
            ]
        self.held, value = wait_for(self.held, value)
        return value


def to_lines(x):
    return jnp.pad(x, (0, -x.shape[0] % WIDE)).reshape(-1, WIDE)


def to_block(x):
    return jnp.pad(x, ((0, 0), (0, -x.shape[1] % WIDE)))


def regroup(late_all, order, rows, hidden):
    count = late_all.shape[0]
    relative = jnp.take(late_all, order, axis=0)

    def out_rows(first):
        return late_all[:, first : first + rows].reshape(BLOCKS, HIDDEN // 2, WIDE)

    def units(first):
        return relative[:, first : first + hidden].reshape(BLOCKS, HIDDEN, WIDE)

    parts = [out_rows(0), out_rows(rows)]
    parts += [units(2 * rows + i * hidden) for i in range(2 * GROUPS)]
    return jnp.concatenate(parts, 1), jnp.arange(BLOCKS, dtype=jnp.int32)


def split_late(packs, rows, hidden):
    cuts = [0, HIDDEN // 2] + [HIDDEN * i for i in range(1, 2 * GROUPS + 2)]
    sizes = [rows, rows] + [hidden] * (2 * GROUPS)
    parts = [
        packs[:, cuts[i] : cuts[i + 1]].reshape(-1, sizes[i], WIDE) for i in range(len(sizes))
    ]
    whole = jnp.concatenate(parts, 1)
    return jnp.pad(whole, ((0, 0), (0, -whole.shape[1] % 16), (0, 0)))


def split_early(packs, small, rows):
    parts = [packs[:, 24 * i : 24 * (i + 1)].reshape(-1, rows, WIDE) for i in range(5)]
    return jnp.concatenate(parts + [small.astype(BF16)], 1)


def local(
    layer_in,
    cotangent,
    valid_len,
    sep_pos,
    w_query,
    w_key,
    w_value,
    w_depth,
    w_point,
    w_kernel,
    w_convout,
    w_output,
    gain_attn,
    shift_attn,
    w_up,
    w_down,
    gain_out,
    shift_out,
):
    seq, dp = lax.axis_size("seq"), lax.axis_size("dp")
    count = seq * dp
    z, d = lax.axis_index("seq"), lax.axis_index("dp")
    core = d & 1
    me = z * dp + d
    codes = np.array(relative_codes(), np.int32)
    order = jnp.asarray(codes) ^ me
    to_absolute = (jnp.arange(count)[:, None] == order[None, :]).astype(BF16)
    rows = w_query.shape[0]
    hidden = w_up.shape[2]
    half = count // 2
    parity = jnp.stack([z & 1])
    lines = [
        to_lines(w_kernel),
        to_lines(w_depth.reshape(-1)),
        to_lines(jnp.concatenate([gain_attn, shift_attn, gain_out, shift_out])),
    ]
    starts = np.cumsum([0] + [line.shape[0] for line in lines])
    small = pad_rows(jnp.concatenate(lines), 8)
    early, tokens_a, tokens_b = call(
        prepare_kernel,
        (
            shape((5 * rows + 8, WIDE), BF16),
            shape((HALF // 2, WIDTH), BF16),
            shape((HALF // 2, WIDTH), BF16),
        ),
        (parity, layer_in, w_query, w_key, w_value, w_point, w_convout, small),
    )
    early, w_output, w_up, w_down = lax.optimization_barrier((early, w_output, w_up, w_down))
    late = pad_rows(
        jnp.concatenate(
            [
                w_output[:, :WIDE],
                w_output[:, WIDE:],
                jnp.swapaxes(w_up, 1, 2).reshape(GROUPS * hidden, WIDE),
                w_down.reshape(GROUPS * hidden, WIDE),
            ]
        ),
        16,
    )
    late_all = lax.all_gather(late, ("seq", "dp"), axis=0, tiled=False)
    parts, tokens_a, tokens_b = gather_weights(early, rows, tokens_a, tokens_b)
    token_pieces = (tokens_a, tokens_b, swap(tokens_a, "dp", 1), swap(tokens_b, "dp", 1))
    pair_info = jnp.stack([valid_len[:, 0], sep_pos[:, 0]]).astype(F32)
    place = jnp.stack([z, core, me, jnp.int32(rows)])
    offsets = np.arange(WIDTH, dtype=np.int32)
    code_rows = np.zeros((8, WIDTH), np.int32)
    code_rows[0], code_rows[1] = codes[offsets // rows], offsets % rows
    info, turned, tokens_own, matrix = call(
        permute_kernel,
        (
            shape((4,), jnp.int32),
            shape((LEN, WIDTH), BF16),
            shape((HALF, WIDTH), BF16),
            shape((WIDTH, WIDTH), BF16),
        ),
        (place, pair_info, swap(pair_info, "dp", 1)) + token_pieces + (jnp.asarray(code_rows),),
        scalars=3,
    )
    parts, cotangent = wait_for(parts, cotangent[:, 0])
    cot_a, cot_b = to_pieces(cotangent)
    parts = parts + [swap(part, "dp", 1) for part in parts]
    own, other, small_rel, q, k, v, att, stats = call(
        attend_kernel,
        (
            shape((5 * WIDE, WIDE), BF16),
            shape((5 * WIDE, WIDE), BF16),
            shape((count * 8, WIDE), BF16),
            shape((HALF, WIDE), BF16),
            shape((LEN, WIDE), BF16),
            shape((LEN, WIDE), BF16),
            shape((HALF, WIDE), BF16),
            shape((HALF, CHUNK), F32),
        ),
        (info, turned, *parts),
    )
    small_rel = small_rel.reshape(count, -1, WIDE)
    kernel_rel = small_rel[:, starts[0] : starts[1]].reshape(count, -1)[:, : w_kernel.shape[0]]
    depth_rel = small_rel[:, starts[1] : starts[2]].reshape(count, -1)[:, : w_depth.size]
    gains_rel = small_rel[:, starts[2] : starts[3]].reshape(count, -1)[:, : 4 * rows]
    kernel_abs = jnp.dot(to_absolute, kernel_rel, preferred_element_type=F32).astype(BF16)
    taps_weight = jnp.pad(
        kernel_abs.reshape(WIDE, HEADS * KERNEL), ((0, 0), (0, CHUNK - HEADS * KERNEL))
    )
    depth_weight = jnp.pad(
        depth_rel.astype(F32).reshape(count, KERNEL, rows).transpose(1, 0, 2).reshape(KERNEL, WIDTH),
        ((0, 16 - KERNEL), (0, 0)),
    )
    gains = jnp.pad(
        jnp.dot(to_absolute, gains_rel, preferred_element_type=F32)
        .reshape(count, 4, rows)
        .transpose(1, 0, 2)
        .reshape(4, WIDTH),
        ((0, 4), (0, 0)),
    )
    context, key_conv, conv_attn, depth_low, values = call(
        conv_kernel,
        (
            shape((HALF, WIDTH), BF16),
            shape((HALF, WIDE), F32),
            shape((HALF, WIDE), BF16),
            shape((HALF, WIDTH), BF16),
            shape((WIDE // CHUNK, WINDOW, CHUNK), F32),
        ),
        (info, turned, own, other, q, att, taps_weight, depth_weight),
        scratch=(
            pltpu.VMEM((WIDTH // CHUNK, WINDOW, CHUNK), F32),
            pltpu.VMEM((KERNEL, HALF, WIDE), F32),
            pltpu.VMEM((KERNEL, HALF, CHUNK), F32),
        ),
    )
    if count == BLOCKS:
        late_blocks, late_order = late_all, order
    else:
        late_blocks, late_order = regroup(late_all, order, rows, hidden)
    halves = (GROUPS, 2, BLOCKS // 2 * HIDDEN, WIDE)
    layer_a, layer_b, first_grad, context_grad, kept, sent, gain_grads = call(
        feed_kernel,
        (
            shape((HALF // 2, WIDTH), BF16),
            shape((HALF // 2, WIDTH), BF16),
            shape((HALF, WIDTH), F32),
            shape((HALF, WIDTH), BF16),
            shape((BLOCKS // 2, PACK, WIDE), BF16),
            shape((BLOCKS // 2, PACK, WIDE), BF16),
            shape((8, WIDTH), F32),
        ),
        (info, late_order, context, tokens_own, late_blocks, cot_a, cot_b, gains, matrix),
        scalars=2,
        scratch=(
            pltpu.VMEM((WIDTH, WIDTH), BF16),
            pltpu.VMEM(halves, BF16),
            pltpu.VMEM(halves, BF16),
            pltpu.VMEM((GROUPS, 2, HALF, WIDTH), BF16),
            pltpu.VMEM((GROUPS, 2, HALF, WIDTH), F32),
            pltpu.VMEM((HALF, WIDTH), F32),
            pltpu.VMEM((HALF, WIDTH), F32),
            pltpu.VMEM((HALF, WIDTH), BF16),
            pltpu.VMEM((HALF, WIDTH), BF16),
            pltpu.VMEM((HALF, WIDTH), BF16),
            pltpu.VMEM((HALF, WIDTH), F32),
            pltpu.VMEM((HALF, 1), F32),
        ),
    )
    if count != BLOCKS:
        kept, sent = split_late(kept, rows, hidden), split_late(sent, rows, hidden)
    first = Scatter(kept, sent, kept.shape[1] // 32 * 16)
    query_conv, key_low, kernel_grad, values_grad, rim_values = call(
        taps_back_kernel,
        (
            shape((HALF, WIDE), F32),
            shape((HALF, WIDE), BF16),
            shape((WIDE, CHUNK), F32),
            shape((WIDE // CHUNK, WINDOW, CHUNK), F32),
            shape((EDGE, WIDE), BF16),
        ),
        (info, q, context_grad, key_conv, conv_attn, values, taps_weight),
        scratch=(
            pltpu.VMEM((KERNEL, HALF, WIDE), F32),
            pltpu.VMEM((KERNEL, HALF, CHUNK), F32),
            pltpu.VMEM((KERNEL, HALF, CHUNK), F32),
            pltpu.VMEM((KERNEL, WINDOW, CHUNK), F32),
            pltpu.VMEM((KERNEL, HALF, CHUNK), BF16),
        ),
        micros=12,
    )
    key_low = first.step(key_low)
    layer_a, layer_b, key_low = lax.optimization_barrier((layer_a, layer_b, key_low))
    layer_a, layer_b = send_pieces(layer_a, layer_b, True)
    context_grad, key_low = lax.optimization_barrier((context_grad, key_low))
    rim_values = swap(rim_values, "dp", 1)
    query_attn, own_part, message = call(
        attend_back_kernel,
        (shape((HALF, WIDE), F32), shape((HALF, WIDTH), F32), shape((HALF, WIDTH), BF16)),
        (info, q, k, v, context, context_grad, stats),
        scratch=(pltpu.VMEM((LEN, WIDE), F32), pltpu.VMEM((LEN, WIDE), F32)),
        micros=13,
    )
    own_part = first.step(own_part)
    layer_a, own_part = wait_for(layer_a, own_part)
    own_part, key_low = wait_for(own_part, key_low)
    arrived = swap(message, "dp", 1)
    point_grad, depth_grad, back, rim_inputs = call(
        depth_back_kernel,
        (
            shape((WIDTH, WIDE), BF16),
            shape((16, WIDTH), F32),
            shape((WIDTH // CHUNK, WINDOW, CHUNK), F32),
            shape((EDGE, WIDTH), BF16),
        ),
        (info, turned, own, other, key_low, depth_low, depth_weight),
        scratch=(
            pltpu.VMEM((WIDTH // CHUNK, WINDOW, CHUNK), F32),
        ),
        micros=5,
    )
    point_grad = first.step(point_grad)
    (layer_b, rim_values), point_grad = wait_for((layer_b, rim_values), point_grad)
    rim_inputs = swap(rim_inputs, "dp", 1)

    kernel_lines = kernel_grad[:, : HEADS * KERNEL].reshape(count, -1)
    gain_lines = gain_grads[:4].reshape(4, count, rows).transpose(1, 0, 2).reshape(count, -1)
    turned_lines = lax.dot_general(
        to_absolute,
        jnp.concatenate([to_block(kernel_lines), to_block(gain_lines)], 1).astype(BF16),
        (((0,), (0,)), ((), ())),
        preferred_element_type=F32,
    )
    cut = starts[1] * WIDE
    depth_lines = to_block(
        depth_grad[:KERNEL].reshape(KERNEL, count, rows).transpose(1, 0, 2).reshape(count, -1)
    )
    small = jnp.concatenate([turned_lines[:, :cut], depth_lines, turned_lines[:, cut:]], 1)
    small = jnp.pad(small, ((0, 0), (0, 8 * WIDE - small.shape[1]))).reshape(count, 8, WIDE)
    kept, sent, low = call(
        grads_kernel,
        (
            shape((BLOCKS // 2, 128, WIDE), BF16),
            shape((BLOCKS // 2, 128, WIDE), BF16),
            shape((4, HALF, WIDE), BF16),
        ),
        (
            info,
            turned,
            query_attn,
            query_conv,
            own_part,
            arrived,
            rim_values,
            values_grad,
            point_grad,
            small[:BLOCKS],
        ),
        scratch=(pltpu.VMEM((HALF, WIDE), F32),),
        micros=8,
    )
    if count != BLOCKS:
        kept, sent = split_early(kept, small[:half], rows), split_early(sent, small[half:], rows)
    second = Scatter(kept, sent, kept.shape[1] // 32 * 16)
    rim_inputs, low = wait_for(rim_inputs, low)
    while first.stage <= first.bits:
        low = first.step(low)
    low = second.step(low)
    x_low = call(
        inputs_kernel,
        (shape((HALF // 2, WIDTH), BF16), shape((HALF // 2, WIDTH), BF16)),
        (info, own, other, matrix, depth_weight, low, rim_inputs, back, first_grad),
        scratch=(pltpu.VMEM((HALF, WIDTH), F32),),
        micros=8,
    )
    x_low = first.step(x_low)
    x_low = second.step(x_low)
    x_a, x_b = send_pieces(*x_low, True)
    x_a = second.step(x_a)
    (layer_a, layer_b), x_a = wait_for((layer_a, layer_b), x_a)
    while second.stage <= second.bits:
        second.step(())
    second.step(())
    first, second = first.held, second.held
    piece = layer_in.shape[:1] + (1,) + layer_in.shape[2:]
    layer_out = call(place_kernel, shape(piece, BF16), (parity, layer_a, layer_b))
    x_grad = call(place_kernel, shape(piece, F32), (parity, x_a, x_b))

    def part(index):
        return second[index * rows : (index + 1) * rows]

    lines = second[5 * rows : 5 * rows + 8].reshape(-1)
    kernel_at, depth_at, gain_at = (start * WIDE for start in starts[:3])
    depth_line = lines[depth_at : depth_at + w_depth.size].reshape(KERNEL, rows)
    gain_line = lines[gain_at : gain_at + 4 * rows].reshape(4, rows)
    return (
        layer_out,
        x_grad,
        part(0),
        part(1),
        part(2),
        depth_line,
        part(3),
        lines[kernel_at : kernel_at + w_kernel.shape[0]],
        part(4),
        jnp.concatenate([first[:rows], first[rows : 2 * rows]], 1),
        gain_line[0],
        gain_line[1],
        jnp.swapaxes(
            first[2 * rows : 2 * rows + GROUPS * hidden].reshape(GROUPS, hidden, WIDE), 1, 2
        ),
        first[2 * rows + GROUPS * hidden : 2 * rows + 2 * GROUPS * hidden].reshape(
            GROUPS, hidden, WIDE
        ),
        gain_line[2],
        gain_line[3],
    )


def solution(mesh):
    in_specs = (
        P(None, "dp", "seq", None),
        P(None, "dp", "seq", None),
        P(None, "dp"),
        P(None, "dp"),
        P(("seq", "dp"), None),
        P(("seq", "dp"), None),
        P(("seq", "dp"), None),
        P(None, ("seq", "dp")),
        P(("seq", "dp"), None),
        P(("seq", "dp")),
        P(("seq", "dp"), None),
        P(("seq", "dp"), None),
        P(("seq", "dp")),
        P(("seq", "dp")),
        P(None, None, ("seq", "dp")),
        P(None, ("seq", "dp"), None),
        P(("seq", "dp")),
        P(("seq", "dp")),
    )
    out_specs = (
        P(None, "dp", "seq", None),
        P(None, "dp", "seq", None),
        P(("seq", "dp"), None),
        P(("seq", "dp"), None),
        P(("seq", "dp"), None),
        P(None, ("seq", "dp")),
        P(("seq", "dp"), None),
        P(("seq", "dp")),
        P(("seq", "dp"), None),
        P(("seq", "dp"), None),
        P(("seq", "dp")),
        P(("seq", "dp")),
        P(None, None, ("seq", "dp")),
        P(None, ("seq", "dp"), None),
        P(("seq", "dp")),
        P(("seq", "dp")),
    )
    return jax.shard_map(local, mesh=mesh, in_specs=in_specs, out_specs=out_specs, check_vma=False)
```

```python
import functools

import jax
import jax.numpy as jnp
import numpy as np
from jax import lax
from jax.experimental import pallas as pl
from jax.experimental.pallas import tpu as pltpu
from jax.sharding import PartitionSpec as P

HEADS = 6
HEAD_DIM = 64
KERNEL = 9
GROUPS = 2
LEN = 1024
HALF = LEN // 2
WIDTH = 768
WIDE = HEADS * HEAD_DIM
CHUNK = 128
EDGE = 16
WINDOW = HALF + 2 * EDGE
BLOCKS = 32
HIDDEN = 48
PACK = 240
COST = 10**8

F32 = jnp.float32
BF16 = jnp.bfloat16

inv_root_two = 0.7071067811865476
inv_root_tau = 0.3989422804014327


def nn(a, b):
    return jnp.dot(a, b, preferred_element_type=F32)


def nt(a, b):
    return lax.dot_general(a, b, (((1,), (1,)), ((), ())), preferred_element_type=F32)


def tn(a, b):
    return lax.dot_general(a, b, (((0,), (0,)), ((), ())), preferred_element_type=F32)


def call(kernel, out_shape, args, scalars=1, scratch=(), micros=0):
    vmem = pl.BlockSpec(memory_space=pltpu.VMEM)
    smem = pl.BlockSpec(memory_space=pltpu.SMEM)
    return pl.pallas_call(
        kernel,
        out_shape=out_shape,
        in_specs=[smem] * scalars
        + [vmem] * (len(args) - scalars),
        out_specs=jax.tree.map(
            lambda s: smem if s.dtype == jnp.int32 else vmem, out_shape
        ),
        scratch_shapes=list(scratch),
        compiler_params=pltpu.CompilerParams(vmem_limit_bytes=56 * 1024 * 1024),
        cost_estimate=pl.CostEstimate(flops=micros * COST, bytes_accessed=0, transcendentals=0),
    )(*args)


def shape(dims, dtype):
    return jax.ShapeDtypeStruct(dims, dtype)


def lane(rows):
    return lax.broadcasted_iota(jnp.int32, (rows, CHUNK), 1)


def load_window(core, source, target, chunks):
    value = source(pl.ds(pl.multiple_of(core * (HALF - EDGE), EDGE), HALF + EDGE))
    start = pl.multiple_of(EDGE - core * EDGE, EDGE)
    edge = pl.multiple_of(core * (HALF + EDGE), EDGE)
    for c in range(chunks):
        target[c, pl.ds(edge, EDGE), :] = jnp.zeros((EDGE, CHUNK), F32)
        target[c, pl.ds(start, HALF + EDGE), :] = value[:, c * CHUNK : (c + 1) * CHUNK].astype(F32)


def weight(own, other, index):
    rows = slice(index * WIDE, (index + 1) * WIDE)
    return own[rows, :], other[rows, :]


def project(tokens, own, other, index):
    first, second = weight(own, other, index)
    return nn(tokens[:, :WIDE], first) + nn(tokens[:, WIDE:], second)


def fill_masks(info, masks):
    sep, valid, core = info[1], info[0], info[2]

    def segment(position):
        return jnp.where(position < sep, 0, jnp.where(position < valid, 1, 2))

    row = core * HALF + lax.broadcasted_iota(jnp.int32, (HALF, CHUNK), 0)
    own = segment(row)
    for j in range(KERNEL):
        masks[j] = (segment(row + (j - 4)) == own).astype(F32)


def prepare_kernel(info, tokens, *refs):
    weights, small, early, token_a, token_b = refs[:5], refs[5], refs[6], refs[7], refs[8]
    rows = weights[0].shape[0]
    odd = info[0]
    token_a[...] = tokens[pl.ds(odd, 1), 0][0]
    token_b[...] = tokens[pl.ds(1 - odd, 1), 0][0]
    pieces = [ref[...].astype(F32) for ref in weights] + [small[...].astype(F32)]
    for i in range(3):
        pair = jnp.concatenate(pieces[2 * i : 2 * i + 2], 0)
        early[2 * i * rows : 2 * i * rows + pair.shape[0], :] = pair.astype(BF16)


def pack_kernel(out, up, down, late):
    half = HIDDEN // 2
    sides = out[...].astype(F32)
    late[0:HIDDEN, :] = jnp.concatenate([sides[:half, :WIDE], sides[:half, WIDE:]], 0).astype(BF16)
    for g in range(GROUPS):
        late[(1 + g) * HIDDEN : (2 + g) * HIDDEN, :] = up[g]
        late[(3 + g) * HIDDEN : (4 + g) * HIDDEN, :] = down[g]


def permute_kernel(
    place, mine, theirs, own_a, own_b, other_a, other_b, codes, info, out, own_out, matrix
):
    z, core, me, rows = place[0], place[1], place[2], place[3]
    high = z >> 1
    for i in range(2):
        own_value = jnp.where(high == 0, mine[i, 0], mine[i, 1])
        other_value = jnp.where(high == 0, theirs[i, 0], theirs[i, 1])
        info[i] = jnp.where((z & 1) == core, own_value, other_value).astype(jnp.int32)
    info[2] = core
    info[3] = high
    features = (codes[0:1, :] ^ me) * rows + codes[1:2, :]
    matrix[...] = (
        (lax.broadcasted_iota(jnp.int32, (WIDTH, WIDTH), 0) == features)
        .astype(F32)
        .astype(BF16)
    )
    quarter = HALF // 2
    for side, pieces in ((core, (own_a, own_b)), (1 - core, (other_a, other_b))):
        for place, piece in zip((high, 1 - high), pieces):
            at = pl.multiple_of(side * HALF + place * quarter, quarter)
            out[pl.ds(at, quarter), :] = nn(piece[...], matrix[...]).astype(BF16)
    own_out[pl.ds(pl.multiple_of(high * quarter, quarter), quarter), :] = own_a[...]
    own_out[pl.ds(pl.multiple_of((1 - high) * quarter, quarter), quarter), :] = own_b[...]


def attend_kernel(info, tokens, *refs):
    parts, refs = refs[:-8], refs[-8:]
    own, other, small_out, q_out, k_out, v_out, att_out, stat_out = refs
    core, valid = info[2], info[0]
    count = len(parts) // 2
    unit = WIDE // count
    rest = parts[0].shape[0] - 5 * unit
    for h, target in enumerate((own, other)):
        for i in range(count):
            part = parts[h * count + i]
            for w in range(5):
                target[w * WIDE + i * unit : w * WIDE + (i + 1) * unit, :] = part[
                    w * unit : (w + 1) * unit, :
                ]
            first = (h * count + i) * rest
            small_out[first : first + rest, :] = part[5 * unit :, :]
    mine = tokens[pl.ds(pl.multiple_of(core * HALF, HALF), HALF), :]
    q_out[...] = project(mine, own, other, 0).astype(BF16)
    k_out[...] = project(tokens[...], own, other, 1).astype(BF16)
    v_out[...] = project(tokens[...], own, other, 2).astype(BF16)
    rows = 256
    bias = jnp.where(
        lax.broadcasted_iota(jnp.int32, (1, LEN), 1) < valid, 0.0, -1e30
    ).astype(F32)
    for block in range(HALF // rows):
        at = slice(block * rows, (block + 1) * rows)
        stats = jnp.zeros((rows, CHUNK), F32)
        for pair in range(HEADS // 2):
            cols = slice(pair * CHUNK, (pair + 1) * CHUNK)
            q = q_out[at, cols] * BF16(0.125)
            k, v = k_out[:, cols], v_out[:, cols]
            results = []
            for head in range(2):
                keep = (lane(rows) < HEAD_DIM) == (head == 0)
                scores = nt(jnp.where(keep, q, BF16(0)), k) + bias
                peak = jnp.max(scores, -1, keepdims=True)
                exponent = jnp.exp(scores - peak)
                total = jnp.sum(exponent, -1, keepdims=True)
                results.append(nn(exponent.astype(BF16), v) / total)
                stats = jnp.where(
                    lane(rows) == 2 * pair + head, peak + jnp.log(total), stats
                )
            att_out[at, cols] = jnp.where(lane(rows) < HEAD_DIM, *results).astype(BF16)
        stat_out[at, :] = stats


def spread(j):
    row = lax.broadcasted_iota(jnp.int32, (CHUNK, WIDE), 0)
    col = lax.broadcasted_iota(jnp.int32, (CHUNK, WIDE), 1)
    return (row == (col >> 6) * KERNEL + j).astype(F32).astype(BF16)


def conv_kernel(
    info,
    tokens,
    own,
    other,
    q,
    att,
    taps_weight,
    depth_weight,
    context,
    key_out,
    attn_out,
    depth_out,
    values_out,
    window,
    logits,
    masks,
):
    core = info[2]
    load_window(core, lambda rows: tokens[rows, :], window, WIDTH // CHUNK)
    fill_masks(info, masks)
    rows = 64
    for c in range(WIDTH // CHUNK):
        cols = slice(c * CHUNK, (c + 1) * CHUNK)
        for b in range(HALF // rows):
            total = jnp.zeros((rows, CHUNK), F32)
            for j in range(KERNEL):
                first = EDGE - 4 + b * rows + j
                total = total + depth_weight[j : j + 1, cols] * window[c, first : first + rows, :]
            depth_out[b * rows : (b + 1) * rows, cols] = total.astype(BF16)
    key_conv = project(depth_out[...], own, other, 3)
    key_out[...] = key_conv
    attn_out[...] = (key_conv * q[...].astype(F32)).astype(BF16)
    load_window(
        core, lambda rows: project(tokens[rows, :], own, other, 4), values_out, WIDE // CHUNK
    )
    for j in range(KERNEL):
        logits[j] = nn(attn_out[...], nn(taps_weight[...], spread(j)).astype(BF16))
    context[:, :WIDE] = att[...]
    for b in range(HALF // rows):
        at = slice(b * rows, (b + 1) * rows)
        for c in range(WIDE // CHUNK):
            cols = slice(c * CHUNK, (c + 1) * CHUNK)
            peak = logits[0, at, cols]
            for j in range(1, KERNEL):
                peak = jnp.maximum(peak, logits[j, at, cols])
            total = jnp.zeros((rows, CHUNK), F32)
            result = jnp.zeros((rows, CHUNK), F32)
            for j in range(KERNEL):
                first = EDGE - 4 + b * rows + j
                exponent = jnp.exp(logits[j, at, cols] - peak)
                total = total + exponent
                result = result + exponent * masks[j, at, :] * values_out[
                    c, first : first + rows, :
                ]
            context[at, WIDE + c * CHUNK : WIDE + (c + 1) * CHUNK] = (result / total).astype(BF16)


def normalize(value):
    centred = value - jnp.mean(value, -1, keepdims=True)
    inv = lax.rsqrt(jnp.mean(centred * centred, -1, keepdims=True) + 1e-06)
    return centred * inv, inv


def normalize_back(grad, normed, inv, gain):
    e = grad * gain
    return inv * (
        e - jnp.mean(e, -1, keepdims=True) - normed * jnp.mean(e * normed, -1, keepdims=True)
    )


def piece_rows(info, step, rows):
    half = info[3] if step < 2 else 1 - info[3]
    return pl.ds(pl.multiple_of(half * (HALF // 2) + step % 2 * rows, rows), rows)


def sum_kernel(cut, kept, arrived, first_0, first_1, second_0, second_1):
    count = kept.shape[0] // 4
    for i in range(kept.shape[0]):
        total = kept[i].astype(F32) + arrived[i].astype(F32)
        high, low = i // (2 * count), i // count % 2
        (first_0, first_1)[high][i % (2 * count)] = total[:cut].astype(BF16)
        (second_0, second_1)[low][high * count + i % count] = total[cut:].astype(BF16)


def place_kernel(info, first, second, out):
    odd = info[0]
    out[pl.ds(odd, 1), 0] = first[...].astype(out.dtype)[None]
    out[pl.ds(1 - odd, 1), 0] = second[...].astype(out.dtype)[None]


def feed_kernel(
    info,
    order,
    context,
    tokens,
    late,
    cot_a,
    cot_b,
    gains,
    matrix,
    layer_a,
    layer_b,
    first_out,
    context_grad,
    kept,
    sent,
    small_out,
    out_weight,
    up,
    down,
    act,
    slope,
    normed,
    attn,
    attn_low,
    grad_low,
    branch_low,
    second,
    scale,
):
    rows = 128
    steps = [slice(i * rows, (i + 1) * rows) for i in range(HALF // rows)]
    gain_attn, shift_attn = gains[0:1, :], gains[1:2, :]
    gain_out, shift_out = gains[2:3, :], gains[3:4, :]
    for i in range(BLOCKS // 2):
        sides = [late[2 * i + k, 0:HIDDEN, :].astype(F32) for k in range(2)]
        out_weight[i * HIDDEN : (i + 1) * HIDDEN, :] = jnp.concatenate(
            [jnp.concatenate([s[: HIDDEN // 2], s[HIDDEN // 2 :]], 1) for s in sides], 0
        ).astype(BF16)
    for h in range(2):
        for i in range(BLOCKS // 2):
            source = order[h * (BLOCKS // 2) + i]
            for g in range(GROUPS):
                at = slice(i * HIDDEN, (i + 1) * HIDDEN)
                up[g, h, at, :] = late[source, (1 + g) * HIDDEN : (2 + g) * HIDDEN, :]
                down[g, h, at, :] = late[source, (3 + g) * HIDDEN : (4 + g) * HIDDEN, :]
    for at in steps:
        branch = nn(context[at, :], out_weight[...]) + tokens[at, :].astype(F32)
        n, inv = normalize(branch)
        normed[at, :] = n
        scale[at, :] = inv
        value = n * gain_attn + shift_attn
        attn[at, :] = value
        attn_low[at, :] = value.astype(BF16)
    for g in range(GROUPS):
        part = slice(g * WIDE, (g + 1) * WIDE)
        for h in range(2):
            for at in steps:
                pre = nt(attn_low[at, part], up[g, h])
                cdf = 0.5 * (1.0 + lax.erf(pre * inv_root_two))
                act[g, h, at, :] = (pre * cdf).astype(BF16)
                slope[g, h, at, :] = cdf + pre * jnp.exp(-0.5 * pre * pre) * inv_root_tau
    gain_grad = jnp.zeros((1, WIDTH), F32)
    shift_grad = jnp.zeros((1, WIDTH), F32)
    for step in range(HALF // rows):
        piece, inner = step // 2, slice(step % 2 * rows, (step % 2 + 1) * rows)
        at = piece_rows(info, step, rows)
        value = attn[at, :] + jnp.concatenate(
            [
                nn(act[g, 0, at, :], down[g, 0]) + nn(act[g, 1, at, :], down[g, 1])
                for g in range(GROUPS)
            ],
            1,
        )
        n, inv = normalize(value)
        (layer_a, layer_b)[piece][inner, :] = (n * gain_out + shift_out).astype(BF16)
        grad = (cot_a, cot_b)[piece][inner, :].astype(F32)
        gain_grad = gain_grad + jnp.sum(grad * n, 0, keepdims=True)
        shift_grad = shift_grad + jnp.sum(grad, 0, keepdims=True)
        value = normalize_back(grad, n, inv, gain_out)
        second[at, :] = value
        grad_low[at, :] = value.astype(BF16)
    small_out[2:3, :] = gain_grad
    small_out[3:4, :] = shift_grad
    for g in range(GROUPS):
        part = slice(g * WIDE, (g + 1) * WIDE)
        for h in range(2):
            target = (kept, sent)[h]
            result = tn(act[g, h], grad_low[:, part]).astype(BF16)
            for i in range(BLOCKS // 2):
                target[i, (3 + g) * HIDDEN : (4 + g) * HIDDEN, :] = result[
                    i * HIDDEN : (i + 1) * HIDDEN
                ]
            for at in steps:
                act[g, h, at, :] = (
                    nt(grad_low[at, part], down[g, h]) * slope[g, h, at, :]
                ).astype(BF16)
            result = tn(act[g, h], attn_low[:, part]).astype(BF16)
            for i in range(BLOCKS // 2):
                target[i, (1 + g) * HIDDEN : (2 + g) * HIDDEN, :] = result[
                    i * HIDDEN : (i + 1) * HIDDEN
                ]
    gain_grad = jnp.zeros((1, WIDTH), F32)
    shift_grad = jnp.zeros((1, WIDTH), F32)
    for at in steps:
        grad = second[at, :] + jnp.concatenate(
            [nn(act[g, 0, at, :], up[g, 0]) + nn(act[g, 1, at, :], up[g, 1]) for g in range(GROUPS)],
            1,
        )
        n = normed[at, :]
        gain_grad = gain_grad + jnp.sum(grad * n, 0, keepdims=True)
        shift_grad = shift_grad + jnp.sum(grad, 0, keepdims=True)
        value = normalize_back(grad, n, scale[at, :], gain_attn)
        first_out[at, :] = value
        branch_low[at, :] = value.astype(BF16)
        context_grad[at, :] = nt(branch_low[at, :], out_weight[...]).astype(BF16)
        grad_low[at, :] = nn(context[at, :], matrix[...]).astype(BF16)
    small_out[0:1, :] = gain_grad
    small_out[1:2, :] = shift_grad
    small_out[4:8, :] = jnp.zeros((4, WIDTH), F32)
    for h in range(2):
        result = tn(grad_low[:, h * WIDE : (h + 1) * WIDE], branch_low[...])
        for i in range(BLOCKS // 2):
            piece = result[i * (HIDDEN // 2) : (i + 1) * (HIDDEN // 2)]
            (kept, sent)[h][i, 0:HIDDEN, :] = jnp.concatenate(
                [piece[:, :WIDE], piece[:, WIDE:]], 0
            ).astype(BF16)


def shifted_sum(source, step, scale=None):
    total = jnp.zeros((32, CHUNK), F32)
    for j in range(KERNEL):
        first = step + 4 - j
        low, high = max(first, 0), min(first + 32, WINDOW)
        piece = source(j)[low:high, :]
        if high - low < 32:
            zero = jnp.zeros((32 - (high - low), CHUNK), F32)
            piece = jnp.concatenate([zero, piece] if low > first else [piece, zero], 0)
        total = total + (piece if scale is None else scale(j) * piece)
    return total


def taps_back_kernel(
    info,
    q,
    context_grad,
    key_conv,
    conv_attn,
    values,
    taps_weight,
    query_out,
    key_low,
    kernel_out,
    values_grad,
    rim_out,
    logits,
    masks,
    sums,
    pads,
    compact,
):
    core = info[2]
    fill_masks(info, masks)
    rows = 64
    steps = [slice(i * rows, (i + 1) * rows) for i in range(HALF // rows)]
    block = (lax.broadcasted_iota(jnp.int32, (CHUNK, CHUNK), 0) >> 6) == (
        lax.broadcasted_iota(jnp.int32, (CHUNK, CHUNK), 1) >> 6
    )
    ones = block.astype(F32).astype(BF16)
    pick_row = lax.broadcasted_iota(jnp.int32, (CHUNK, CHUNK), 0)
    pick_col = lax.broadcasted_iota(jnp.int32, (CHUNK, CHUNK), 1)
    for j in range(KERNEL):
        logits[j] = nn(conv_attn[...], nn(taps_weight[...], spread(j)).astype(BF16))
        pads[j, 0:EDGE, :] = jnp.zeros((EDGE, CHUNK), F32)
        pads[j, HALF + EDGE : WINDOW, :] = jnp.zeros((EDGE, CHUNK), F32)
    total_compact = jnp.zeros((HALF, CHUNK), F32)
    for c in range(WIDE // CHUNK):
        cols = slice(c * CHUNK, (c + 1) * CHUNK)
        grad_cols = slice(WIDE + c * CHUNK, WIDE + (c + 1) * CHUNK)
        for j in range(KERNEL):
            product = (
                context_grad[:, grad_cols].astype(F32)
                * values[c, EDGE - 4 + j : EDGE - 4 + j + HALF, :]
            )
            sums[j] = nn(product.astype(BF16), ones)
        for b, at in enumerate(steps):
            grad = context_grad[at, grad_cols].astype(F32)
            peak = logits[0, at, cols]
            for j in range(1, KERNEL):
                peak = jnp.maximum(peak, logits[j, at, cols])
            total = jnp.zeros((rows, CHUNK), F32)
            dot = jnp.zeros((rows, CHUNK), F32)
            for j in range(KERNEL):
                exponent = jnp.exp(logits[j, at, cols] - peak)
                mask = masks[j, at, :]
                logits[j, at, cols] = exponent
                change = sums[j, at, :] * mask
                sums[j, at, :] = change
                total = total + exponent
                dot = dot + exponent * change
            inv = 1.0 / total
            dot = dot * inv
            inside = slice(EDGE + b * rows, EDGE + (b + 1) * rows)
            for j in range(KERNEL):
                tap = logits[j, at, cols] * inv
                pads[j, inside, :] = tap * masks[j, at, :] * grad
                compact[j, at, :] = (tap * (sums[j, at, :] - dot)).astype(BF16)
        for j in range(KERNEL):
            pick = (pick_row & 63 == 0) & (pick_col == (2 * c + (pick_row >> 6)) * KERNEL + j)
            total_compact = total_compact + nn(compact[j], pick.astype(F32).astype(BF16))
        for b in range(WINDOW // 32):
            values_grad[c, b * 32 : (b + 1) * 32, :] = shifted_sum(lambda j: pads.at[j], b * 32)
    compact_low = total_compact.astype(BF16)
    kernel_out[...] = tn(conv_attn[...], compact_low)
    attn_grad = nt(compact_low, taps_weight[...])
    query_out[...] = attn_grad * key_conv[...]
    key_low[...] = (attn_grad * q[...].astype(F32)).astype(BF16)
    rim = pl.multiple_of((1 - core) * (HALF + EDGE), EDGE)
    for c in range(WIDE // CHUNK):
        rim_out[:, c * CHUNK : (c + 1) * CHUNK] = values_grad[c, pl.ds(rim, EDGE), :].astype(BF16)


def depth_back_kernel(
    info,
    tokens,
    own,
    other,
    key_low,
    depth_low,
    depth_weight,
    point_out,
    depth_grad,
    back_out,
    rim_out,
    window,
):
    core = info[2]
    load_window(core, lambda rows: tokens[rows, :], window, WIDTH // CHUNK)
    point_out[...] = tn(depth_low[...], key_low[...]).astype(BF16)
    depth_grad[...] = jnp.zeros((16, WIDTH), F32)
    for side, rows_weight in enumerate(weight(own, other, 3)):
        back = nt(key_low[...], rows_weight)
        for k in range(WIDE // CHUNK):
            c = side * (WIDE // CHUNK) + k
            back_out[c, 0:EDGE, :] = jnp.zeros((EDGE, CHUNK), F32)
            back_out[c, HALF + EDGE : WINDOW, :] = jnp.zeros((EDGE, CHUNK), F32)
            back_out[c, EDGE : HALF + EDGE, :] = back[:, k * CHUNK : (k + 1) * CHUNK]
    for c in range(WIDTH // CHUNK):
        cols = slice(c * CHUNK, (c + 1) * CHUNK)
        totals = [jnp.zeros((8, CHUNK), F32) for _ in range(KERNEL)]
        for b in range(HALF // 32):
            grad = back_out[c, EDGE + b * 32 : EDGE + (b + 1) * 32, :]
            for j in range(KERNEL):
                first = EDGE - 4 + b * 32 + j
                product = grad * window[c, first : first + 32, :]
                totals[j] = totals[j] + (
                    (product[0:8] + product[8:16]) + (product[16:24] + product[24:32])
                )
        for j in range(KERNEL):
            depth_grad[j : j + 1, cols] = jnp.sum(totals[j], 0, keepdims=True)
        low, high = (
            shifted_sum(lambda j: back_out.at[c], step, lambda j: depth_weight[j : j + 1, cols])
            for step in (0, WINDOW - 32)
        )
        turned = (c + WIDE // CHUNK) % (WIDTH // CHUNK)
        rim_out[:, turned * CHUNK : (turned + 1) * CHUNK] = jnp.where(
            core == 0, high[32 - EDGE :], low[:EDGE]
        ).astype(BF16)


def attend_back_kernel(
    info, q, k, v, context, context_grad, stats, query_out, own_out, message, key_sum, value_sum
):
    core, valid = info[2], info[0]
    rows = 256
    live = lax.broadcasted_iota(jnp.int32, (LEN, CHUNK), 0) < valid
    for pair in range(HEADS // 2):
        cols = slice(pair * CHUNK, (pair + 1) * CHUNK)
        keys, vals = k[:, cols], v[:, cols]
        for head in range(2):
            even = head == 0
            base = HEAD_DIM if even else 0
            key_lane = lane(LEN)
            keep_key = (key_lane < HEAD_DIM) == even
            keys_more = jnp.where(
                keep_key,
                keys.astype(F32),
                jnp.where(
                    key_lane == base,
                    jnp.where(live, 0.0, -1e30),
                    jnp.where(key_lane < base + 4, 1.0, 0.0),
                ),
            ).astype(BF16)
            vals_more = jnp.where(
                keep_key, vals.astype(F32), jnp.where(key_lane < base + 3, 1.0, 0.0)
            ).astype(BF16)
            keys_turned = keys_more.T
            for block in range(HALF // rows):
                at = slice(block * rows, (block + 1) * rows)
                here = lane(rows)
                keep = (here < HEAD_DIM) == even

                def three(value):
                    high = value.astype(BF16).astype(F32)
                    middle = (value - high).astype(BF16).astype(F32)
                    return high, middle, value - high - middle

                grad = context_grad[at, cols].astype(F32)
                product = jnp.where(keep, grad * context[at, cols].astype(F32), 0.0)
                dots = three(-jnp.sum(product, -1, keepdims=True))
                stat = three(-stats[at, 2 * pair + head : 2 * pair + head + 1])
                grad_more = jnp.where(
                    keep,
                    grad,
                    jnp.where(
                        here == base,
                        dots[0],
                        jnp.where(
                            here == base + 1, dots[1], jnp.where(here == base + 2, dots[2], 0.0)
                        ),
                    ),
                ).astype(BF16)
                query_more = jnp.where(
                    keep,
                    q[at, cols].astype(F32) * 0.125,
                    jnp.where(
                        here == base,
                        1.0,
                        jnp.where(
                            here == base + 1,
                            stat[0],
                            jnp.where(
                                here == base + 2, stat[1], jnp.where(here == base + 3, stat[2], 0.0)
                            ),
                        ),
                    ),
                ).astype(BF16)
                probs = jnp.exp(nt(keys_more, query_more))
                change = (probs * nt(vals_more, grad_more)).astype(BF16)
                value_part = nn(probs.astype(BF16), grad_more)
                key_part = nn(change, query_more)
                query_part = nn(keys_turned, change).T * 0.125
                if block == 0:
                    value_total, key_total = value_part, key_part
                else:
                    value_total, key_total = value_total + value_part, key_total + key_part
                if even:
                    query_out[at, cols] = query_part
                else:
                    query_out[at, cols] = jnp.where(keep, query_part, query_out[at, cols])
            if even:
                key_sum[:, cols] = key_total
                value_sum[:, cols] = value_total
            else:
                key_sum[:, cols] = jnp.where(keep_key, key_total, key_sum[:, cols])
                value_sum[:, cols] = jnp.where(keep_key, value_total, value_sum[:, cols])
    mine = pl.ds(pl.multiple_of(core * HALF, HALF), HALF)
    theirs = pl.ds(pl.multiple_of((1 - core) * HALF, HALF), HALF)
    own_out[:, :WIDE] = key_sum[mine, :]
    own_out[:, WIDE:] = value_sum[mine, :]
    message[:, :WIDE] = key_sum[theirs, :].astype(BF16)
    message[:, WIDE:] = value_sum[theirs, :].astype(BF16)


def grads_kernel(
    info,
    tokens,
    query_attn,
    query_conv,
    own_part,
    arrived,
    rim_values,
    values_grad,
    point_grad,
    small,
    kept,
    sent,
    low_out,
    values_sum,
):
    core = info[2]
    rim = pl.ds(pl.multiple_of((1 - core) * (HALF - EDGE), EDGE), EDGE)
    for c in range(WIDE // CHUNK):
        cols = slice(c * CHUNK, (c + 1) * CHUNK)
        values_sum[:, cols] = values_grad[c, EDGE : EDGE + HALF, :]
    values_sum[rim, :] = values_sum[rim, :] + rim_values[...].astype(F32)
    both = own_part[...] + arrived[...].astype(F32)
    low_out[0] = (query_attn[...] + query_conv[...]).astype(BF16)
    low_out[1] = both[:, :WIDE].astype(BF16)
    low_out[2] = both[:, WIDE:].astype(BF16)
    low_out[3] = values_sum[...].astype(BF16)
    mine = pl.ds(pl.multiple_of(core * HALF, HALF), HALF)
    unit = HIDDEN // 2
    for h in range(2):
        part = tokens[mine, h * WIDE : (h + 1) * WIDE]
        results = [tn(part, low_out[n]) for n in range(4)]
        point = point_grad[h * WIDE : (h + 1) * WIDE, :].astype(F32)
        target = (kept, sent)[h]
        for i in range(BLOCKS // 2):
            at = slice(i * unit, (i + 1) * unit)
            target[i, 0:48, :] = jnp.concatenate([results[0][at], results[1][at]], 0).astype(BF16)
            target[i, 48:96, :] = jnp.concatenate([results[2][at], point[at]], 0).astype(BF16)
            target[i, 96:128, :] = jnp.concatenate(
                [results[3][at], small[h * (BLOCKS // 2) + i]], 0
            ).astype(BF16)


def inputs_kernel(
    info,
    own,
    other,
    matrix,
    depth_weight,
    low,
    rim_inputs,
    back,
    first_grad,
    x_a,
    x_b,
    inputs,
):
    core = info[2]
    rim = pl.ds(pl.multiple_of((1 - core) * (HALF - EDGE), EDGE), EDGE)
    for c in range(WIDTH // CHUNK):
        cols = slice(c * CHUNK, (c + 1) * CHUNK)
        for b in range(HALF // 32):
            inputs[b * 32 : (b + 1) * 32, cols] = shifted_sum(
                lambda j: back.at[c], EDGE + b * 32, lambda j: depth_weight[j : j + 1, cols]
            )
    inputs[rim, :] = inputs[rim, :] + rim_inputs[...].astype(F32)
    for h in range(2):
        rows = (own, other)[h]
        total = inputs[:, h * WIDE : (h + 1) * WIDE]
        for n, index in enumerate((0, 1, 2, 4)):
            total = total + nt(low[n], rows[index * WIDE : (index + 1) * WIDE, :])
        inputs[:, h * WIDE : (h + 1) * WIDE] = total
    for step in range(4):
        at = piece_rows(info, step, CHUNK)
        value = nt(inputs[at, :].astype(BF16), matrix[...]) + first_grad[at, :]
        inner = slice(step % 2 * CHUNK, (step % 2 + 1) * CHUNK)
        (x_a, x_b)[step // 2][inner, :] = value.astype(BF16)


def dp_groups(count):
    masks = []
    bit = 2
    while bit < count:
        if bit * 2 < count:
            masks.append((bit, 2 * bit, 3 * bit))
            bit *= 4
        else:
            masks.append((bit,))
            bit *= 2
    return masks


def swap(x, axis, mask):
    count = lax.axis_size(axis)
    return lax.ppermute(x, axis, [(i, i ^ mask) for i in range(count)])


def relative_codes():
    seq, dp = lax.axis_size("seq"), lax.axis_size("dp")
    codes = [j * dp for j in range(seq)]
    for masks in dp_groups(dp):
        codes = [c ^ m for m in (0,) + masks for c in codes]
    return codes + [c ^ 1 for c in codes]


def add_up(parts):
    total = parts[0].astype(jnp.float32)
    for part in parts[1:]:
        total = total + part.astype(jnp.float32)
    return total


def token_perms():
    seq, dp = lax.axis_size("seq"), lax.axis_size("dp")
    first, second = [], []
    for z in range(seq):
        for d in range(dp):
            core, rest = d & 1, d & ~1
            odd = z & 1
            first.append((z * dp + d, (2 * odd + core) * dp + rest + (z >> 1)))
            second.append((z * dp + d, (2 * (1 - odd) + core) * dp + rest + (z >> 1)))
    return first, second


def pad_rows(x, multiple):
    return jnp.pad(x, ((0, -x.shape[0] % multiple), (0, 0)))


def merge(packs, rows):
    cut = packs[0].shape[0] // (5 * rows + 8) * (5 * rows)
    weights = jnp.concatenate([p[:cut].reshape(5, -1, WIDE) for p in packs], 1)
    return jnp.concatenate([weights.reshape(-1, WIDE)] + [p[cut:] for p in packs])


def gather_weights(pack, rows, *tokens):
    held = merge([pack] + [swap(pack, "seq", j) for j in range(1, lax.axis_size("seq"))], rows)
    tokens = send_pieces(*tokens)
    groups = dp_groups(lax.axis_size("dp"))
    for masks in groups[:-1]:
        held = merge([held] + [swap(held, "dp", m) for m in masks], rows)
    return [held] + [swap(held, "dp", m) for m in groups[-1]], *tokens


def send_pieces(a, b, back=False):
    first, second = token_perms()
    if back:
        first, second = ([(t, s) for s, t in perm] for perm in (first, second))
    return lax.ppermute(a, ("seq", "dp"), first), lax.ppermute(b, ("seq", "dp"), second)


def to_pieces(x):
    odd = lax.axis_index("seq") & 1
    a, b = (lax.dynamic_index_in_dim(x, index, 0, False) for index in (odd, 1 - odd))
    return send_pieces(a, b)


def wait_for(arrays, value):
    return lax.optimization_barrier((arrays, value))


class Scatter:
    def __init__(self, kept, sent, cut):
        self.bits = lax.axis_size("dp").bit_length() - 2
        self.stage = 0
        self.cut = cut
        self.held = kept, sent

    def pieces(self, whole, rows):
        dims = (2,) * self.bits + (-1,) + whole[0].shape[1:]
        return [part.reshape(dims)[..., rows, :] for part in whole]

    def step(self, value):
        if self.stage == 0:
            kept, sent = self.held
            arrived, value = wait_for(swap(sent, "dp", 1), value)
            if self.bits == 2:
                self.stage = 1
                size, rows, wide = kept.shape
                halves = [
                    shape((size // 2, n, wide), BF16) for n in (self.cut, rows - self.cut)
                ]
                sums = call(
                    functools.partial(sum_kernel, self.cut),
                    (halves[0], halves[0], halves[1], halves[1]),
                    (kept, arrived),
                    scalars=0,
                )
                split = (2, -1)
                self.held = [
                    [s.reshape(split + s.shape[1:]) for s in sums[:2]],
                    [s.reshape(split + s.shape[1:]) for s in sums[2:]],
                ]
                self.held, value = wait_for(self.held, value)
                return value
            first = self.pieces((kept, arrived), slice(0, self.cut))
            second = self.pieces((kept, arrived), slice(self.cut, None))
        elif self.stage <= self.bits:
            first, second = self.held
            arrived, value = wait_for(
                (
                    swap(first[1], "dp", 1 << (self.bits + 1 - self.stage)),
                    swap(second[1], "dp", 1 << self.stage),
                ),
                value,
            )
            first, second = [first[0], arrived[0]], [second[0], arrived[1]]
        else:
            arrived, value = wait_for(
                [swap(part, "seq", j + 1) for j, part in enumerate(self.held[1:])], value
            )
            self.held = add_up([self.held[0]] + arrived)
            return value
        self.stage += 1
        if self.stage <= self.bits:
            last = self.bits - self.stage
            self.held = [
                [add_up([p[i] for p in first]).astype(BF16) for i in range(2)],
                [
                    add_up([lax.index_in_dim(p, i, last, False) for p in second]).astype(BF16)
                    for i in range(2)
                ],
            ]
        else:
            self.held = [
                jnp.concatenate(
                    [add_up([p[j] for p in half]).astype(BF16) for half in (first, second)]
                )
                for j in range(lax.axis_size("seq"))
            ]
        self.held, value = wait_for(self.held, value)
        return value


def to_lines(x):
    return jnp.pad(x, (0, -x.shape[0] % WIDE)).reshape(-1, WIDE)


def to_block(x):
    return jnp.pad(x, ((0, 0), (0, -x.shape[1] % WIDE)))


def regroup(late_all, order, rows, hidden):
    count = late_all.shape[0]
    relative = jnp.take(late_all, order, axis=0)

    def out_rows(first):
        return late_all[:, first : first + rows].reshape(BLOCKS, HIDDEN // 2, WIDE)

    def units(first):
        return relative[:, first : first + hidden].reshape(BLOCKS, HIDDEN, WIDE)

    parts = [out_rows(0), out_rows(rows)]
    parts += [units(2 * rows + i * hidden) for i in range(2 * GROUPS)]
    return jnp.concatenate(parts, 1), jnp.arange(BLOCKS, dtype=jnp.int32)


def split_late(packs, rows, hidden):
    cuts = [0, HIDDEN // 2] + [HIDDEN * i for i in range(1, 2 * GROUPS + 2)]
    sizes = [rows, rows] + [hidden] * (2 * GROUPS)
    parts = [
        packs[:, cuts[i] : cuts[i + 1]].reshape(-1, sizes[i], WIDE) for i in range(len(sizes))
    ]
    whole = jnp.concatenate(parts, 1)
    return jnp.pad(whole, ((0, 0), (0, -whole.shape[1] % 16), (0, 0)))


def split_early(packs, small, rows):
    parts = [packs[:, 24 * i : 24 * (i + 1)].reshape(-1, rows, WIDE) for i in range(5)]
    return jnp.concatenate(parts + [small.astype(BF16)], 1)


def local(
    layer_in,
    cotangent,
    valid_len,
    sep_pos,
    w_query,
    w_key,
    w_value,
    w_depth,
    w_point,
    w_kernel,
    w_convout,
    w_output,
    gain_attn,
    shift_attn,
    w_up,
    w_down,
    gain_out,
    shift_out,
):
    seq, dp = lax.axis_size("seq"), lax.axis_size("dp")
    count = seq * dp
    z, d = lax.axis_index("seq"), lax.axis_index("dp")
    core = d & 1
    me = z * dp + d
    codes = np.array(relative_codes(), np.int32)
    order = jnp.asarray(codes) ^ me
    to_absolute = (jnp.arange(count)[:, None] == order[None, :]).astype(BF16)
    rows = w_query.shape[0]
    hidden = w_up.shape[2]
    half = count // 2
    parity = jnp.stack([z & 1])
    if count == BLOCKS:
        late = call(
            pack_kernel,
            shape((PACK, WIDE), BF16),
            (w_output, jnp.swapaxes(w_up, 1, 2), w_down),
            scalars=0,
        )
    else:
        late = pad_rows(
            jnp.concatenate(
                [
                    w_output[:, :WIDE],
                    w_output[:, WIDE:],
                    jnp.swapaxes(w_up, 1, 2).reshape(GROUPS * hidden, WIDE),
                    w_down.reshape(GROUPS * hidden, WIDE),
                ]
            ),
            16,
        )
    lines = [
        to_lines(w_kernel),
        to_lines(w_depth.reshape(-1)),
        to_lines(jnp.concatenate([gain_attn, shift_attn, gain_out, shift_out])),
    ]
    starts = np.cumsum([0] + [line.shape[0] for line in lines])
    small = pad_rows(jnp.concatenate(lines), 8)
    early, tokens_a, tokens_b = call(
        prepare_kernel,
        (
            shape((5 * rows + 8, WIDE), BF16),
            shape((HALF // 2, WIDTH), BF16),
            shape((HALF // 2, WIDTH), BF16),
        ),
        (parity, layer_in, w_query, w_key, w_value, w_point, w_convout, small),
    )
    late_all = lax.all_gather(late, ("seq", "dp"), axis=0, tiled=False)
    parts, tokens_a, tokens_b = gather_weights(early, rows, tokens_a, tokens_b)
    token_pieces = (tokens_a, tokens_b, swap(tokens_a, "dp", 1), swap(tokens_b, "dp", 1))
    pair_info = jnp.stack([valid_len[:, 0], sep_pos[:, 0]]).astype(F32)
    place = jnp.stack([z, core, me, jnp.int32(rows)])
    offsets = np.arange(WIDTH, dtype=np.int32)
    code_rows = np.zeros((8, WIDTH), np.int32)
    code_rows[0], code_rows[1] = codes[offsets // rows], offsets % rows
    info, turned, tokens_own, matrix = call(
        permute_kernel,
        (
            shape((4,), jnp.int32),
            shape((LEN, WIDTH), BF16),
            shape((HALF, WIDTH), BF16),
            shape((WIDTH, WIDTH), BF16),
        ),
        (place, pair_info, swap(pair_info, "dp", 1)) + token_pieces + (jnp.asarray(code_rows),),
        scalars=3,
    )
    parts, cotangent = wait_for(parts, cotangent[:, 0])
    cot_a, cot_b = to_pieces(cotangent)
    parts = parts + [swap(part, "dp", 1) for part in parts]
    own, other, small_rel, q, k, v, att, stats = call(
        attend_kernel,
        (
            shape((5 * WIDE, WIDE), BF16),
            shape((5 * WIDE, WIDE), BF16),
            shape((count * 8, WIDE), BF16),
            shape((HALF, WIDE), BF16),
            shape((LEN, WIDE), BF16),
            shape((LEN, WIDE), BF16),
            shape((HALF, WIDE), BF16),
            shape((HALF, CHUNK), F32),
        ),
        (info, turned, *parts),
    )
    small_rel = small_rel.reshape(count, -1, WIDE)
    kernel_rel = small_rel[:, starts[0] : starts[1]].reshape(count, -1)[:, : w_kernel.shape[0]]
    depth_rel = small_rel[:, starts[1] : starts[2]].reshape(count, -1)[:, : w_depth.size]
    gains_rel = small_rel[:, starts[2] : starts[3]].reshape(count, -1)[:, : 4 * rows]
    kernel_abs = jnp.dot(to_absolute, kernel_rel, preferred_element_type=F32).astype(BF16)
    taps_weight = jnp.pad(
        kernel_abs.reshape(WIDE, HEADS * KERNEL), ((0, 0), (0, CHUNK - HEADS * KERNEL))
    )
    depth_weight = jnp.pad(
        depth_rel.astype(F32).reshape(count, KERNEL, rows).transpose(1, 0, 2).reshape(KERNEL, WIDTH),
        ((0, 16 - KERNEL), (0, 0)),
    )
    gains = jnp.pad(
        jnp.dot(to_absolute, gains_rel, preferred_element_type=F32)
        .reshape(count, 4, rows)
        .transpose(1, 0, 2)
        .reshape(4, WIDTH),
        ((0, 4), (0, 0)),
    )
    context, key_conv, conv_attn, depth_low, values = call(
        conv_kernel,
        (
            shape((HALF, WIDTH), BF16),
            shape((HALF, WIDE), F32),
            shape((HALF, WIDE), BF16),
            shape((HALF, WIDTH), BF16),
            shape((WIDE // CHUNK, WINDOW, CHUNK), F32),
        ),
        (info, turned, own, other, q, att, taps_weight, depth_weight),
        scratch=(
            pltpu.VMEM((WIDTH // CHUNK, WINDOW, CHUNK), F32),
            pltpu.VMEM((KERNEL, HALF, WIDE), F32),
            pltpu.VMEM((KERNEL, HALF, CHUNK), F32),
        ),
    )
    if count == BLOCKS:
        late_blocks, late_order = late_all, order
    else:
        late_blocks, late_order = regroup(late_all, order, rows, hidden)
    halves = (GROUPS, 2, BLOCKS // 2 * HIDDEN, WIDE)
    layer_a, layer_b, first_grad, context_grad, kept, sent, gain_grads = call(
        feed_kernel,
        (
            shape((HALF // 2, WIDTH), BF16),
            shape((HALF // 2, WIDTH), BF16),
            shape((HALF, WIDTH), F32),
            shape((HALF, WIDTH), BF16),
            shape((BLOCKS // 2, PACK, WIDE), BF16),
            shape((BLOCKS // 2, PACK, WIDE), BF16),
            shape((8, WIDTH), F32),
        ),
        (info, late_order, context, tokens_own, late_blocks, cot_a, cot_b, gains, matrix),
        scalars=2,
        scratch=(
            pltpu.VMEM((WIDTH, WIDTH), BF16),
            pltpu.VMEM(halves, BF16),
            pltpu.VMEM(halves, BF16),
            pltpu.VMEM((GROUPS, 2, HALF, WIDTH), BF16),
            pltpu.VMEM((GROUPS, 2, HALF, WIDTH), F32),
            pltpu.VMEM((HALF, WIDTH), F32),
            pltpu.VMEM((HALF, WIDTH), F32),
            pltpu.VMEM((HALF, WIDTH), BF16),
            pltpu.VMEM((HALF, WIDTH), BF16),
            pltpu.VMEM((HALF, WIDTH), BF16),
            pltpu.VMEM((HALF, WIDTH), F32),
            pltpu.VMEM((HALF, 1), F32),
        ),
    )
    if count != BLOCKS:
        kept, sent = split_late(kept, rows, hidden), split_late(sent, rows, hidden)
    first = Scatter(kept, sent, kept.shape[1] // 32 * 16)
    query_conv, key_low, kernel_grad, values_grad, rim_values = call(
        taps_back_kernel,
        (
            shape((HALF, WIDE), F32),
            shape((HALF, WIDE), BF16),
            shape((WIDE, CHUNK), F32),
            shape((WIDE // CHUNK, WINDOW, CHUNK), F32),
            shape((EDGE, WIDE), BF16),
        ),
        (info, q, context_grad, key_conv, conv_attn, values, taps_weight),
        scratch=(
            pltpu.VMEM((KERNEL, HALF, WIDE), F32),
            pltpu.VMEM((KERNEL, HALF, CHUNK), F32),
            pltpu.VMEM((KERNEL, HALF, CHUNK), F32),
            pltpu.VMEM((KERNEL, WINDOW, CHUNK), F32),
            pltpu.VMEM((KERNEL, HALF, CHUNK), BF16),
        ),
        micros=12,
    )
    key_low = first.step(key_low)
    layer_a, layer_b, key_low = lax.optimization_barrier((layer_a, layer_b, key_low))
    layer_a, layer_b = send_pieces(layer_a, layer_b, True)
    context_grad, key_low = lax.optimization_barrier((context_grad, key_low))
    rim_values = swap(rim_values, "dp", 1)
    query_attn, own_part, message = call(
        attend_back_kernel,
        (shape((HALF, WIDE), F32), shape((HALF, WIDTH), F32), shape((HALF, WIDTH), BF16)),
        (info, q, k, v, context, context_grad, stats),
        scratch=(pltpu.VMEM((LEN, WIDE), F32), pltpu.VMEM((LEN, WIDE), F32)),
        micros=13,
    )
    own_part = first.step(own_part)
    layer_a, own_part = wait_for(layer_a, own_part)
    own_part, key_low = wait_for(own_part, key_low)
    arrived = swap(message, "dp", 1)
    point_grad, depth_grad, back, rim_inputs = call(
        depth_back_kernel,
        (
            shape((WIDTH, WIDE), BF16),
            shape((16, WIDTH), F32),
            shape((WIDTH // CHUNK, WINDOW, CHUNK), F32),
            shape((EDGE, WIDTH), BF16),
        ),
        (info, turned, own, other, key_low, depth_low, depth_weight),
        scratch=(
            pltpu.VMEM((WIDTH // CHUNK, WINDOW, CHUNK), F32),
        ),
        micros=5,
    )
    point_grad = first.step(point_grad)
    (layer_b, rim_values), point_grad = wait_for((layer_b, rim_values), point_grad)
    rim_inputs = swap(rim_inputs, "dp", 1)

    kernel_lines = kernel_grad[:, : HEADS * KERNEL].reshape(count, -1)
    gain_lines = gain_grads[:4].reshape(4, count, rows).transpose(1, 0, 2).reshape(count, -1)
    turned_lines = lax.dot_general(
        to_absolute,
        jnp.concatenate([to_block(kernel_lines), to_block(gain_lines)], 1).astype(BF16),
        (((0,), (0,)), ((), ())),
        preferred_element_type=F32,
    )
    cut = starts[1] * WIDE
    depth_lines = to_block(
        depth_grad[:KERNEL].reshape(KERNEL, count, rows).transpose(1, 0, 2).reshape(count, -1)
    )
    small = jnp.concatenate([turned_lines[:, :cut], depth_lines, turned_lines[:, cut:]], 1)
    small = jnp.pad(small, ((0, 0), (0, 8 * WIDE - small.shape[1]))).reshape(count, 8, WIDE)
    kept, sent, low = call(
        grads_kernel,
        (
            shape((BLOCKS // 2, 128, WIDE), BF16),
            shape((BLOCKS // 2, 128, WIDE), BF16),
            shape((4, HALF, WIDE), BF16),
        ),
        (
            info,
            turned,
            query_attn,
            query_conv,
            own_part,
            arrived,
            rim_values,
            values_grad,
            point_grad,
            small[:BLOCKS],
        ),
        scratch=(pltpu.VMEM((HALF, WIDE), F32),),
        micros=8,
    )
    if count != BLOCKS:
        kept, sent = split_early(kept, small[:half], rows), split_early(sent, small[half:], rows)
    second = Scatter(kept, sent, kept.shape[1] // 32 * 16)
    rim_inputs, low = wait_for(rim_inputs, low)
    while first.stage <= first.bits:
        low = first.step(low)
    low = second.step(low)
    x_low = call(
        inputs_kernel,
        (shape((HALF // 2, WIDTH), BF16), shape((HALF // 2, WIDTH), BF16)),
        (info, own, other, matrix, depth_weight, low, rim_inputs, back, first_grad),
        scratch=(pltpu.VMEM((HALF, WIDTH), F32),),
        micros=8,
    )
    x_low = first.step(x_low)
    x_low = second.step(x_low)
    x_a, x_b = send_pieces(*x_low, True)
    x_a = second.step(x_a)
    (layer_a, layer_b), x_a = wait_for((layer_a, layer_b), x_a)
    while second.stage <= second.bits:
        second.step(())
    second.step(())
    first, second = first.held, second.held
    piece = layer_in.shape[:1] + (1,) + layer_in.shape[2:]
    layer_out = call(place_kernel, shape(piece, BF16), (parity, layer_a, layer_b))
    x_grad = call(place_kernel, shape(piece, F32), (parity, x_a, x_b))

    def part(index):
        return second[index * rows : (index + 1) * rows]

    lines = second[5 * rows : 5 * rows + 8].reshape(-1)
    kernel_at, depth_at, gain_at = (start * WIDE for start in starts[:3])
    depth_line = lines[depth_at : depth_at + w_depth.size].reshape(KERNEL, rows)
    gain_line = lines[gain_at : gain_at + 4 * rows].reshape(4, rows)
    return (
        layer_out,
        x_grad,
        part(0),
        part(1),
        part(2),
        depth_line,
        part(3),
        lines[kernel_at : kernel_at + w_kernel.shape[0]],
        part(4),
        jnp.concatenate([first[:rows], first[rows : 2 * rows]], 1),
        gain_line[0],
        gain_line[1],
        jnp.swapaxes(
            first[2 * rows : 2 * rows + GROUPS * hidden].reshape(GROUPS, hidden, WIDE), 1, 2
        ),
        first[2 * rows + GROUPS * hidden : 2 * rows + 2 * GROUPS * hidden].reshape(
            GROUPS, hidden, WIDE
        ),
        gain_line[2],
        gain_line[3],
    )


def solution(mesh):
    in_specs = (
        P(None, "dp", "seq", None),
        P(None, "dp", "seq", None),
        P(None, "dp"),
        P(None, "dp"),
        P(("seq", "dp"), None),
        P(("seq", "dp"), None),
        P(("seq", "dp"), None),
        P(None, ("seq", "dp")),
        P(("seq", "dp"), None),
        P(("seq", "dp")),
        P(("seq", "dp"), None),
        P(("seq", "dp"), None),
        P(("seq", "dp")),
        P(("seq", "dp")),
        P(None, None, ("seq", "dp")),
        P(None, ("seq", "dp"), None),
        P(("seq", "dp")),
        P(("seq", "dp")),
    )
    out_specs = (
        P(None, "dp", "seq", None),
        P(None, "dp", "seq", None),
        P(("seq", "dp"), None),
        P(("seq", "dp"), None),
        P(("seq", "dp"), None),
        P(None, ("seq", "dp")),
        P(("seq", "dp"), None),
        P(("seq", "dp")),
        P(("seq", "dp"), None),
        P(("seq", "dp"), None),
        P(("seq", "dp")),
        P(("seq", "dp")),
        P(None, None, ("seq", "dp")),
        P(None, ("seq", "dp"), None),
        P(("seq", "dp")),
        P(("seq", "dp")),
    )
    return jax.shard_map(local, mesh=mesh, in_specs=in_specs, out_specs=out_specs, check_vma=False)
```
